32 devices in a mesh: ctx: 8 (over z, x), section: 4 (over y, core).
Axes of the slice: x: 2, y: 2, z: 4, core: 2. Of those that a mesh axis runs over, the one named last changes fastest.
Arguments:
- query_heads: bfloat16 [4, 1024, 4096], P('section', 'ctx'), may hold values from -12 to 12
- key_heads: bfloat16 [4, 1024, 512], P('section', 'ctx'), may hold values from -12 to 12
- value_heads: bfloat16 [4, 1024, 512], P('section', 'ctx'), may hold values from -6 to 6
- attn_output: bfloat16 [4, 1024, 4096], P('section', 'ctx'), may hold values from -6 to 6
- output_grad: bfloat16 [4, 1024, 4096], P('section', 'ctx'), may hold values from -6 to 6
- doc_start: int32 [1024], P('ctx'), may hold values from 0 to 1023, as said below
- fetch_list: int32 [8, 2], P('ctx'), may hold values from 0 to 1, as said below
Outputs:
- handed_grad: bfloat16 [4, 1024, 4096], P('section', 'ctx')
- key_grad: bfloat16 [4, 1024, 512], P('section', 'ctx')
- value_grad: bfloat16 [4, 1024, 512], P('section', 'ctx')
The draws below stay inside these ranges and needn't reach their ends.
Inputs may be any that keep to these rules, and one draw needn't show every extreme that they name: doc_start never falls, doc_start[t] <= t, and positions with equal doc_start form one document; a document holds at most 257 positions, and some hold exactly that many; the last position forms a document of its own. fetch_list[i, d - 1] is 1 exactly when some position of shard i and some position of shard i - d lie in one document.
All inputs are finite; a program needn't handle non-finite values.
Results may differ from the reference program's by a relative error of at most 0.0095.
Values may be sent and summed in bfloat16 or wider, within the bound.
No kernel may reach another device: no remote copies, remote signals or barrier semaphores. Data moves between devices by JAX's collectives and lax.ppermute only.
A program may use at most 64 MiB of HBM per device.

```python
import math
import jax
import jax.numpy as jnp
from jax import lax

HQ = 32
HK = 4
HD = 128
TOK_DEV = 128
FETCH = 2
SEQ = 1024
LAYERS = 4
N_CTX = 8


def document_layout(key):
    total_len = SEQ
    longest = FETCH * TOK_DEV + 1
    pick_key, long_key, short_key = jax.random.split(jax.random.fold_in(key, 101), 3)
    is_long = jax.random.randint(pick_key, (total_len,), 0, 2)
    long_len = jax.random.randint(long_key, (total_len,), TOK_DEV, longest + 1)
    short_len = jax.random.randint(short_key, (total_len,), 1, max(TOK_DEV // 2, 2) + 1)
    order_idx = jnp.arange(total_len, dtype=jnp.int32)
    lengths = jnp.where(is_long == 1, long_len, short_len)
    lengths = jnp.where(order_idx % 4 == 0, longest, lengths)
    starts = jnp.cumsum(lengths) - lengths
    inside = starts < total_len
    marks = jnp.zeros((total_len,), jnp.int32).at[jnp.where(inside, starts, 0)].max(inside.astype(jnp.int32))
    marks = jnp.where(order_idx == total_len - 1, 1, marks)
    doc_begin = lax.cummax(marks * order_idx, axis=0)
    first_begin = doc_begin[::TOK_DEV]
    shard_ids = jnp.arange(N_CTX, dtype=jnp.int32)
    distance = jnp.arange(1, FETCH + 1, dtype=jnp.int32)
    source = shard_ids[:, None] - distance[None, :]
    fetched = ((source >= 0) & (first_begin[:, None] < (source + 1) * TOK_DEV)).astype(jnp.int32)
    return (doc_begin.astype(jnp.int32), fetched)


def draw_doc_start(key, part):
    return document_layout(key)[0]


def draw_fetch_list(key, part):
    return document_layout(key)[1]


def draw_key_heads(key, part):
    key = jax.random.fold_in(key, 2)
    base = jnp.clip(jax.random.normal(key, (LAYERS, SEQ, HK * HD), jnp.float32), -4.0, 4.0)
    return base.astype(jnp.bfloat16)


def draw_query_heads(key, part):
    key = jax.random.fold_in(key, 1)
    base = jnp.clip(jax.random.normal(key, (LAYERS, SEQ, HQ * HD), jnp.float32), -4.0, 4.0)
    return base.astype(jnp.bfloat16)


def shard_levels(rng, dims, shards, low, high):
    def one(position, parts):
        steps = jax.random.uniform(jax.random.fold_in(jax.random.fold_in(rng, 6), position), (parts,), jnp.float32, low / len(shards), high / len(shards))
        return jnp.repeat(jnp.exp(steps), dims[position] // parts).reshape((-1,) + (1,) * (len(dims) - position - 1))

    factor_of = one(*shards[0])
    for cut in shards[1:]:
        factor_of = factor_of * one(*cut)
    return factor_of


def scatter_about(rng, extent, deviation, bound, cuts=(), kind=jnp.bfloat16):
    loudness = shard_levels(rng, extent, cuts, -0.22, 0.18) if cuts else 1.0
    values = jax.random.normal(rng, extent, jnp.float32) * deviation * loudness
    return jnp.minimum(jnp.maximum(values, -bound), bound).astype(kind)


def setup_inputs(seed: int = 0) -> dict:
    streams_of = jax.random.split(jax.random.key(seed), 8)
    query_heads = draw_query_heads(jax.random.fold_in(streams_of[7], 71), 0)
    key_heads = draw_key_heads(jax.random.fold_in(streams_of[7], 71), 0)
    value_heads = scatter_about(streams_of[2], (LAYERS, SEQ, HK * HD), 1.0, 6.0, ((0, 4), (1, 8)))
    attn_output = scatter_about(streams_of[3], (LAYERS, SEQ, HQ * HD), 1.0, 6.0, ((0, 4), (1, 8)))
    output_grad = scatter_about(streams_of[4], (LAYERS, SEQ, HQ * HD), 1.0, 6.0, ((0, 4), (1, 8)))
    doc_start = draw_doc_start(jax.random.fold_in(streams_of[7], 71), 0)
    fetch_list = draw_fetch_list(jax.random.fold_in(streams_of[7], 71), 0)
    return {"query_heads": query_heads, "key_heads": key_heads, "value_heads": value_heads, "attn_output": attn_output, "output_grad": output_grad, "doc_start": doc_start, "fetch_list": fetch_list}


ROPE_BASE = 1000000.0
TRAINED_CONTEXT = 32768.0
YARN_FACTOR = 4.0
NEG_LARGE = -1.0e30


def yarn_frequencies(head_dim):
    half_dim = head_dim // 2

    def correction(rotations):
        return head_dim * math.log(TRAINED_CONTEXT / (rotations * 2.0 * math.pi)) / (2.0 * math.log(ROPE_BASE))

    lower_dim = max(math.floor(correction(32.0)), 0)
    upper_dim = min(math.ceil(correction(1.0)), head_dim - 1)
    spread_dims = max(upper_dim - lower_dim, 0.001)
    indices = jnp.arange(half_dim, dtype=jnp.float32)
    extrapolated = jnp.power(jnp.float32(ROPE_BASE), -2.0 * indices / head_dim)
    ramp_weight = jnp.clip((indices - lower_dim) / spread_dims, 0.0, 1.0)
    return extrapolated / YARN_FACTOR * ramp_weight + extrapolated * (1.0 - ramp_weight)


def rope_tables(positions, head_dim):
    freqs = yarn_frequencies(head_dim)
    angles = positions.astype(jnp.float32)[:, None] * freqs[None, :]
    angles = jnp.concatenate([angles, angles], axis=1)
    factor = 0.1 * math.log(YARN_FACTOR) + 1.0
    return (jnp.cos(angles) * factor)[:, None, :], (jnp.sin(angles) * factor)[:, None, :]


def apply_rope(inputs, cosine, sine_table):
    half_dim = inputs.shape[-1] // 2
    turned = jnp.concatenate([-inputs[..., half_dim:], inputs[..., :half_dim]], axis=-1)
    return inputs * cosine + turned * sine_table


def undo_rope(grads, cosine, sine_table):
    half_dim = grads.shape[-1] // 2
    scaled = grads * sine_table
    return grads * cosine + jnp.concatenate([scaled[..., half_dim:], -scaled[..., :half_dim]], axis=-1)


def layer_grads(query_heads, key_heads, value_heads, attn_output, output_grad, doc_start, fetch_list):
    seq_len = query_heads.shape[0]
    ratio = HQ // HK
    score_scale = HD ** -0.5
    span = (FETCH + 1) * TOK_DEV
    front = FETCH * TOK_DEV
    positions = jnp.arange(seq_len, dtype=jnp.int32) - doc_start
    cosine, sine_table = rope_tables(positions, HD)
    q_rot = apply_rope(query_heads.astype(jnp.float32).reshape(seq_len, HQ, HD), cosine, sine_table)
    q_rot = q_rot.astype(jnp.bfloat16).reshape(seq_len, HK, ratio, HD)
    k_rot = apply_rope(key_heads.astype(jnp.float32).reshape(seq_len, HK, HD), cosine, sine_table).astype(jnp.bfloat16)
    val_rows = value_heads.reshape(seq_len, HK, HD)
    grad_rows = output_grad.reshape(seq_len, HK, ratio, HD)
    delta = jnp.sum((output_grad.astype(jnp.float32) * attn_output.astype(jnp.float32)).reshape(seq_len, HK, ratio, HD), axis=-1)
    k_pad = jnp.concatenate([jnp.zeros((front, HK, HD), jnp.bfloat16), k_rot], axis=0)
    v_pad = jnp.concatenate([jnp.zeros((front, HK, HD), jnp.bfloat16), val_rows], axis=0)
    window_idx = jnp.arange(span, dtype=jnp.int32)
    block_idx = jnp.arange(TOK_DEV, dtype=jnp.int32)

    def shard_step(carry, shard_index):
        dk_acc, dv_acc = carry
        row_start = shard_index * TOK_DEV
        q_blk = lax.dynamic_slice_in_dim(q_rot, row_start, TOK_DEV, 0).astype(jnp.float32)
        g_blk = lax.dynamic_slice_in_dim(grad_rows, row_start, TOK_DEV, 0).astype(jnp.float32)
        d_blk = lax.dynamic_slice_in_dim(delta, row_start, TOK_DEV, 0)
        s_blk = lax.dynamic_slice_in_dim(doc_start, row_start, TOK_DEV, 0)
        k_win = lax.dynamic_slice_in_dim(k_pad, row_start, span, 0).astype(jnp.float32)
        v_win = lax.dynamic_slice_in_dim(v_pad, row_start, span, 0).astype(jnp.float32)
        t_pos = row_start + block_idx
        u_pos = row_start - front + window_idx
        offset = FETCH - window_idx // TOK_DEV
        table = jnp.concatenate([jnp.ones((1,), jnp.int32), fetch_list[shard_index]], axis=0)
        listed = table[offset]
        allowed = (u_pos[None, :] >= s_blk[:, None]) & (u_pos[None, :] <= t_pos[:, None]) & (listed[None, :] == 1)
        pair_mask = allowed[:, None, None, :]
        scores = jnp.einsum("tgre,uge->tgru", q_blk, k_win) * score_scale
        largest = jnp.max(jnp.where(pair_mask, scores, NEG_LARGE), axis=-1)
        exp_total = jnp.sum(jnp.where(pair_mask, jnp.exp(scores - largest[..., None]), 0.0), axis=-1)
        lse = largest + jnp.log(exp_total)
        prob = jnp.where(pair_mask, jnp.exp(scores - lse[..., None]), 0.0)
        prob_b = prob.astype(jnp.bfloat16)
        dprob = jnp.einsum("tgre,uge->tgru", g_blk, v_win)
        dscore = (prob * (dprob - d_blk[..., None])).astype(jnp.bfloat16).astype(jnp.float32)
        dq_blk = jnp.einsum("tgru,uge->tgre", dscore, k_win) * score_scale
        dk_win = jnp.einsum("tgru,tgre->uge", dscore, q_blk) * score_scale
        dv_win = jnp.einsum("tgru,tgre->uge", prob_b.astype(jnp.float32), g_blk)
        dk_acc = lax.dynamic_update_slice_in_dim(dk_acc, lax.dynamic_slice_in_dim(dk_acc, row_start, span, 0) + dk_win, row_start, 0)
        dv_acc = lax.dynamic_update_slice_in_dim(dv_acc, lax.dynamic_slice_in_dim(dv_acc, row_start, span, 0) + dv_win, row_start, 0)
        return (dk_acc, dv_acc), dq_blk

    start_acc = jnp.zeros((seq_len + front, HK, HD), jnp.float32)
    (dk_acc, dv_acc), dq_blocks = lax.scan(shard_step, (start_acc, start_acc), jnp.arange(seq_len // TOK_DEV, dtype=jnp.int32))
    dq_rot = dq_blocks.reshape(seq_len, HQ, HD)
    query_grad = undo_rope(dq_rot, cosine, sine_table).astype(jnp.bfloat16).reshape(seq_len, HQ * HD)
    key_grad = undo_rope(dk_acc[front:], cosine, sine_table).astype(jnp.bfloat16).reshape(seq_len, HK * HD)
    value_grad = dv_acc[front:].astype(jnp.bfloat16).reshape(seq_len, HK * HD)
    return query_grad, key_grad, value_grad


def reference(query_heads, key_heads, value_heads, attn_output, output_grad, doc_start, fetch_list):
    def per_layer(stacked):
        return layer_grads(stacked[0], stacked[1], stacked[2], stacked[3], stacked[4], doc_start, fetch_list)

    query_grad, key_grad, value_grad = lax.map(per_layer, (query_heads, key_heads, value_heads, attn_output, output_grad))
    handed_grad = jnp.concatenate([query_grad[1:], jnp.zeros_like(query_grad[:1])], axis=0)
    return handed_grad, key_grad, value_grad
```

```python
import math

import jax
import jax.numpy as jnp
from jax import lax
from jax.experimental import pallas as pl
from jax.experimental.pallas import tpu as pltpu
from jax.sharding import PartitionSpec as P

HQ = 32
HK = 4
HD = 128
RATIO = HQ // HK
HALF = HD // 2
FETCH = 2
PAIR = 2

ROPE_BASE = 1000000.0
TRAINED_CONTEXT = 32768.0
YARN_FACTOR = 4.0
NEG_LARGE = -1e30
SCORE_SCALE = HD ** (-0.5)
EXP2_SCALE = SCORE_SCALE / math.log(2.0)

F32 = jnp.float32
BF16 = jnp.bfloat16


def from_behind(value, axis, steps):
    count = lax.axis_size(axis)
    initial, last = (max(0, -steps), min(count, count - steps))
    return lax.ppermute(value, axis, [(source, source + steps) for source in range(initial, last)])


def dot_nn(left, right):
    return lax.dot_general(left, right, (((1,), (0,)), ((), ())), preferred_element_type=F32)


def dot_nt(left, right):
    return lax.dot_general(left, right, (((1,), (1,)), ((), ())), preferred_element_type=F32)


def frequencies(rows, columns):
    def correction(rotations):
        return HD * math.log(TRAINED_CONTEXT / (rotations * 2.0 * math.pi)) / (2.0 * math.log(ROPE_BASE))

    lower_dim = max(math.floor(correction(32.0)), 0)
    upper_dim = min(math.ceil(correction(1.0)), HD - 1)
    spread_dims = max(upper_dim - lower_dim, 0.001)
    indices = lax.broadcasted_iota(jnp.int32, (rows, columns), 0).astype(F32)
    extrapolated = jnp.exp(indices * F32(-2.0 / HD * math.log(ROPE_BASE)))
    ramp_weight = jnp.clip((indices - lower_dim) / spread_dims, 0.0, 1.0)
    return extrapolated / YARN_FACTOR * ramp_weight + extrapolated * (1.0 - ramp_weight)


def half_tables(positions):
    factor = 0.1 * math.log(YARN_FACTOR) + 1.0
    angles = frequencies(HALF, positions.shape[1]) * positions.astype(F32)
    return jnp.cos(angles) * factor, jnp.sin(angles) * factor


def upright(cos_t, sin_t):
    cosine = jnp.concatenate([cos_t, cos_t], axis=0).T
    signed_sine = jnp.concatenate([sin_t, -sin_t], axis=0).T
    return cosine, signed_sine


def rotate(values, cosine, signed_sine):
    return values * cosine - pltpu.roll(values, HALF, 1) * signed_sine


def unrotate(values, cosine, signed_sine):
    return values * cosine + pltpu.roll(values, HALF, 1) * signed_sine


def head_columns(head):
    return slice(head * HD, (head + 1) * HD)


def stack_heads(ref, group, first):
    return jnp.concatenate([ref[group, :, head_columns(first + i)] for i in range(PAIR)], axis=0)


def block_diagonal(upper, lower):
    zero = jnp.zeros_like(upper)
    return jnp.concatenate(
        [jnp.concatenate([upper, zero], axis=1), jnp.concatenate([zero, lower], axis=1)], axis=0
    )


def group_rows(ref, group, columns):
    pairs = range(RATIO // PAIR)
    return jnp.concatenate([ref[group * len(pairs) + i, :, columns] for i in pairs], axis=0)


def pack_kernel(k_hbm, v_hbm, kv_ref, arrived):
    copies = [
        pltpu.make_async_copy(source.at[:, head_columns(group)], kv_ref.at[which, group], arrived.at[which, group])
        for which, source in enumerate((k_hbm, v_hbm))
        for group in range(HK)
    ]
    for copy in copies:
        copy.start()
    for copy in copies:
        copy.wait()


def own_kernel(
    first_ref, doc_ref, q_hbm, k_hbm, v_hbm, o_hbm, g_hbm,
    qg_ref, prob_ref, ds_ref, kt_ref, stat_ref, half_ref, cos_ref, sin_ref, cos12_ref, sin12_ref,
    q_ref, k_ref, v_ref, o_ref, g_ref, arrived,
):
    rows = q_hbm.shape[0]
    arguments = ((k_hbm, k_ref), (q_hbm, q_ref), (v_hbm, v_ref), (g_hbm, g_ref), (o_hbm, o_ref))

    def fetch(which, group):
        source, buffer = arguments[which]
        width = buffer.shape[2]
        columns = pl.ds(pl.multiple_of(group * width, width), width)
        return pltpu.make_async_copy(source.at[:, columns], buffer.at[group], arrived.at[which, group])

    for group in range(HK):
        for which in range(len(arguments)):
            fetch(which, group).start()

    doc_row = doc_ref[...] - first_ref[0]
    columns = lax.broadcasted_iota(jnp.int32, (1, rows), 1)
    cos_t, sin_t = half_tables(columns - doc_row)
    half_ref[0] = cos_t * SCORE_SCALE
    half_ref[1] = sin_t * SCORE_SCALE
    cos_ref[...], sin_ref[...] = upright(cos_t, sin_t)
    reach = doc_row[:, 0:1]
    for distance in range(FETCH, 0, -1):
        at = slice((FETCH - distance) * rows, (FETCH - distance + 1) * rows)
        back_cos, back_sin = upright(*half_tables(columns - distance * rows - reach))
        cos12_ref[at, :] = back_cos
        sin12_ref[at, :] = back_sin
    key_idx = lax.broadcasted_iota(jnp.int32, (rows, rows), 0)
    query_idx = lax.broadcasted_iota(jnp.int32, (rows, rows), 1)
    mask = (key_idx <= query_idx) & (key_idx >= doc_row)
    bias = jnp.where(mask, 0.0, NEG_LARGE)
    bias = jnp.concatenate([bias] * PAIR, axis=1)
    ones = jnp.ones((8, HD), BF16)

    @pl.loop(0, HK)
    def _(group):
        for which in range(len(arguments)):
            fetch(which, group).wait()
        cosine = cos_ref[...]
        signed_sine = sin_ref[...]
        k_rot = rotate(k_ref[group].astype(F32), cosine, signed_sine)
        kt_ref[group] = k_rot.T.astype(BF16)
        left = block_diagonal(k_rot.astype(BF16), v_ref[group])

        def products(first):
            pair = group * (RATIO // PAIR) + first // PAIR
            for i in range(PAIR):
                rows_of = slice(i * rows, (i + 1) * rows)
                q_rot = rotate(q_ref[group, :, head_columns(first + i)].astype(F32), cosine, signed_sine)
                qg_ref[pair, rows_of, :HD] = q_rot.astype(BF16)
            grads = stack_heads(g_ref, group, first)
            qg_ref[pair, :, HD:] = grads
            product = grads.astype(F32) * stack_heads(o_ref, group, first).astype(F32)
            high = product.astype(BF16)
            low = (product - high.astype(F32)).astype(BF16)
            delta = (dot_nt(ones, high) + dot_nt(ones, low))[0:1]
            both = dot_nt(left, qg_ref[pair])
            return both[:rows], both[rows:], delta

        def finish(first, scores, dprob, delta):
            at = slice(first * HD, (first + PAIR) * HD)
            scores = scores + bias
            largest = jnp.max(scores, axis=0, keepdims=True)
            prob = jnp.exp2((scores - largest) * EXP2_SCALE)
            total = jnp.sum(prob, axis=0, keepdims=True)
            dscore = (prob * (dprob - delta)).astype(BF16)
            prob_ref[group, :, at] = prob.astype(BF16)
            ds_ref[group, :, at] = dscore
            stat_ref[group, 0:1, at] = largest
            stat_ref[group, 1:2, at] = total
            stat_ref[group, 2:3, at] = delta

        ahead = products(0)
        for first in range(0, RATIO, PAIR):
            now = ahead
            if first + PAIR < RATIO:
                ahead = products(first + PAIR)
            finish(first, *now)


def cross_kernel(
    first_ref, list_ref, doc_ref, qg_ref, kv2_ref, kv1_ref, ds0_ref, kt_ref, stat_ref, half_ref, cos12_ref, sin12_ref,
    dq_ref, ret2_ref, ret1_ref, scale_ref, own_ref, prob_buf, ds_buf,
):
    rows = doc_ref.shape[1]
    doc_row = doc_ref[...] - first_ref[0]
    reach = doc_row[:, 0:1]
    in_reach = jnp.where(doc_row == reach, 1.0, 0.0)
    in_reach = jnp.concatenate([in_reach] * PAIR, axis=1)
    key_idx = lax.broadcasted_iota(jnp.int32, (rows, PAIR * rows), 0)
    far = jnp.where(list_ref[0, 1] == 1, -2 * rows, -(1 << 30))
    near = jnp.where(list_ref[0, 0] == 1, -rows, -(1 << 30))
    bias = jnp.concatenate([key_idx + far, key_idx + near], axis=0)
    bias = jnp.where(bias >= reach, 0.0, NEG_LARGE)

    def attend(skipped):
        used = FETCH * rows - skipped
        behind_by_two = rows - skipped
        own_bias = bias[skipped:]

        def key_rows(which, group):
            near_rows = kv1_ref[which, group]
            if behind_by_two == 0:
                return near_rows
            return jnp.concatenate([kv2_ref[which, group, skipped:, :], near_rows], axis=0)

        @pl.loop(0, HK)
        def _(group):
            k_rot = rotate(key_rows(0, group).astype(F32), cos12_ref[skipped:, :], sin12_ref[skipped:, :])
            k_rot_t = jnp.concatenate([k_rot.T.astype(BF16), kt_ref[group]], axis=1)
            left = block_diagonal(k_rot.astype(BF16), key_rows(1, group))
            cos_t = jnp.concatenate([half_ref[0]] * PAIR, axis=1)
            sin_t = jnp.concatenate([half_ref[1]] * PAIR, axis=1)

            def products(first):
                both = dot_nt(left, qg_ref[group * (RATIO // PAIR) + first // PAIR])
                return both[:used], both[used:]

            def middle(first, scores, dprob):
                at = slice(first * HD, (first + PAIR) * HD)
                own_max = stat_ref[group, 0:1, at]
                own_sum = stat_ref[group, 1:2, at]
                delta = stat_ref[group, 2:3, at]
                scores = scores + own_bias
                largest = jnp.maximum(own_max, jnp.max(scores, axis=0, keepdims=True))
                prob = jnp.exp2((scores - largest) * EXP2_SCALE)
                total = jnp.sum(prob, axis=0, keepdims=True) * in_reach
                own_scale = jnp.exp2(jnp.where(in_reach > 0.0, own_max - largest, 0.0) * EXP2_SCALE)
                inverse = 1.0 / (own_sum * own_scale + total)
                own_scale = own_scale * inverse
                scale_ref[group, 0:1, at] = own_scale
                prob = (prob * (inverse * in_reach)).astype(BF16)
                dscore = prob * (dprob - delta).astype(BF16)
                prob_buf[:used, at] = prob
                ds_buf[:used, at] = dscore
                own_dscore = ds0_ref[group, :, at] * own_scale.astype(BF16)
                own_ref[group, :, at] = own_dscore
                return jnp.concatenate([dscore, own_dscore], axis=0)

            def finish(first, dscore):
                dq = dot_nn(k_rot_t, dscore)
                upper, lower = dq[:HALF], dq[HALF:]
                dq = jnp.concatenate([upper * cos_t + lower * sin_t, lower * cos_t - upper * sin_t], axis=0)
                dq = dq.astype(BF16)
                for i in range(PAIR):
                    lanes = pl.ds(pl.multiple_of((group * RATIO + first + i) * HD, HD), HD)
                    dq_ref[0, :, lanes] = dq[:, head_columns(i)].T

            ahead = products(0)
            behind = None
            for first in range(0, RATIO, PAIR):
                now = ahead
                if first + PAIR < RATIO:
                    ahead = products(first + PAIR)
                done = middle(first, *now)
                if behind is not None:
                    finish(first - PAIR, behind)
                behind = done
            finish(RATIO - PAIR, behind)
            dk = dot_nn(ds_buf[:used, :], group_rows(qg_ref, group, slice(HD))) * SCORE_SCALE
            dv = dot_nn(prob_buf[:used, :], group_rows(qg_ref, group, slice(HD, 2 * HD)))
            for which, grad in enumerate((dk.astype(BF16), dv.astype(BF16))):
                ret1_ref[which, group] = grad[behind_by_two:]
                if skipped:
                    ret2_ref[which, group, :skipped, :] = jnp.zeros((skipped, HD), BF16)
                if behind_by_two:
                    ret2_ref[which, group, skipped:, :] = grad[:behind_by_two]

    farthest = jnp.min(doc_row.astype(F32))
    pl.when(farthest >= -rows)(lambda: attend(rows))
    pl.when((farthest < -rows) & (farthest >= -rows - rows // 2))(lambda: attend(rows // 2))
    pl.when(farthest < -rows - rows // 2)(lambda: attend(0))


def own_kv_kernel(qg_ref, prob_ref, ds_ref, scale_ref, dk_ref, dv_ref):
    @pl.loop(0, HK)
    def _(group):
        prob = (prob_ref[group].astype(F32) * scale_ref[group, 0:1, :]).astype(BF16)
        dk_ref[group] = dot_nn(ds_ref[group], group_rows(qg_ref, group, slice(HD))) * SCORE_SCALE
        dv_ref[group] = dot_nn(prob, group_rows(qg_ref, group, slice(HD, 2 * HD)))


def sum_kernel(
    dk_ref, dv_ref, ret2_ref, ret1_ref, cos_ref, sin_ref, dq_ref, key_hbm, value_hbm, handed_hbm, key_buf, value_buf, copied
):
    rows = dq_ref.shape[1]
    half = rows // 2
    copies = [
        pltpu.make_async_copy(dq_ref.at[:, pl.ds(i * half, half)], handed_hbm.at[:, pl.ds(i * half, half)], copied.at[i])
        for i in range(2)
    ]
    for copy in copies:
        copy.start()
    for group in range(HK):
        at = head_columns(group)
        dv = dv_ref[group] + ret1_ref[1, group].astype(F32) + ret2_ref[1, group].astype(F32)
        value_buf[0, :, at] = dv.astype(BF16)
    copies.append(pltpu.make_async_copy(value_buf, value_hbm, copied.at[2]))
    copies[-1].start()
    for group in range(HK):
        at = head_columns(group)
        dk = dk_ref[group] + ret1_ref[0, group].astype(F32) + ret2_ref[0, group].astype(F32)
        key_buf[0, :, at] = unrotate(dk, cos_ref[...], sin_ref[...]).astype(BF16)
    copies.append(pltpu.make_async_copy(key_buf, key_hbm, copied.at[3]))
    copies[-1].start()
    for copy in copies:
        copy.wait()


def cost(flops, moved, exps=0):
    return pl.CostEstimate(flops=int(flops), bytes_accessed=int(moved), transcendentals=int(exps))


def shards(query_heads, key_heads, value_heads, attn_output, output_grad, doc_start, fetch_list):
    rows = query_heads.shape[1]
    wide = RATIO * HD
    kv_width = HK * HD
    first_row = (lax.axis_index("ctx") * rows).astype(jnp.int32).reshape(1)
    doc_row = doc_start.reshape(1, rows)
    smem = pl.BlockSpec(memory_space=pltpu.SMEM)
    vmem = pl.BlockSpec(memory_space=pltpu.VMEM)
    hbm = pl.BlockSpec(memory_space=pltpu.HBM)
    params = pltpu.CompilerParams(vmem_limit_bytes=40 * 1024 * 1024)
    shape = jax.ShapeDtypeStruct
    block_flops = 2 * HQ * rows * rows * HD
    arguments = [
        pltpu.with_memory_space_constraint(x[0], pltpu.HBM)
        for x in (query_heads, key_heads, value_heads, attn_output, output_grad)
    ]

    kv = pl.pallas_call(
        pack_kernel,
        in_specs=[hbm, hbm],
        out_specs=vmem,
        out_shape=shape((2, HK, rows, HD), BF16),
        scratch_shapes=[pltpu.SemaphoreType.DMA((2, HK))],
        compiler_params=params,
        cost_estimate=cost(0, 2**19),
        name="pack_keys",
    )(arguments[1], arguments[2])
    kv2 = from_behind(kv, "ctx", 2)
    kv1 = from_behind(kv, "ctx", 1)

    qg, prob0, ds0, k_own_t, stat, half, cos, sin, cos12, sin12 = pl.pallas_call(
        own_kernel,
        in_specs=[smem, vmem] + [hbm] * 5,
        out_specs=[vmem] * 10,
        out_shape=[
            shape((HQ // PAIR, PAIR * rows, 2 * HD), BF16),
            shape((HK, rows, RATIO * rows), BF16),
            shape((HK, rows, RATIO * rows), BF16),
            shape((HK, HD, rows), BF16),
            shape((HK, 8, RATIO * rows), F32),
            shape((2, HALF, rows), F32),
            shape((rows, HD), F32),
            shape((rows, HD), F32),
            shape((FETCH * rows, HD), F32),
            shape((FETCH * rows, HD), F32),
        ],
        scratch_shapes=[
            pltpu.VMEM((HK, rows, wide), BF16),
            pltpu.VMEM((HK, rows, HD), BF16),
            pltpu.VMEM((HK, rows, HD), BF16),
            pltpu.VMEM((HK, rows, wide), BF16),
            pltpu.VMEM((HK, rows, wide), BF16),
            pltpu.SemaphoreType.DMA((5, HK)),
        ],
        compiler_params=params,
        cost_estimate=cost(3 * block_flops, 9 * 2**20, HQ * rows * rows),
        name="own_block",
    )(first_row, pltpu.with_memory_space_constraint(doc_row, pltpu.HBM), *arguments)

    dq, ret2, ret1, scale, ds_own = pl.pallas_call(
        cross_kernel,
        in_specs=[smem, smem] + [vmem] * 10,
        out_specs=[vmem] * 5,
        out_shape=[
            shape((1, rows, HQ * HD), BF16),
            shape((2, HK, rows, HD), BF16),
            shape((2, HK, rows, HD), BF16),
            shape((HK, 8, RATIO * rows), F32),
            shape((HK, rows, RATIO * rows), BF16),
        ],
        scratch_shapes=[
            pltpu.VMEM((FETCH * rows, RATIO * rows), BF16),
            pltpu.VMEM((FETCH * rows, RATIO * rows), BF16),
        ],
        compiler_params=params,
        cost_estimate=cost(10 * block_flops, 6 * 2**20, 2 * HQ * rows * rows),
        name="cross_blocks",
    )(first_row, fetch_list, doc_row, qg, kv2, kv1, ds0, k_own_t, stat, half, cos12, sin12)

    arrived1 = from_behind(ret1, "ctx", -1)
    arrived2 = from_behind(ret2, "ctx", -2)
    dq_next = from_behind(dq, "section", -1)

    dk0, dv0 = pl.pallas_call(
        own_kv_kernel,
        in_specs=[vmem] * 4,
        out_specs=[vmem] * 2,
        out_shape=[shape((HK, rows, HD), F32), shape((HK, rows, HD), F32)],
        compiler_params=params,
        cost_estimate=cost(2 * block_flops, 5 * 2**20),
        name="own_keys",
    )(qg, prob0, ds_own, scale)

    key_grad, value_grad, handed_grad = pl.pallas_call(
        sum_kernel,
        in_specs=[vmem] * 6 + [pl.BlockSpec(memory_space=pl.ANY)],
        out_specs=[hbm] * 3,
        out_shape=[
            shape((1, rows, kv_width), BF16),
            shape((1, rows, kv_width), BF16),
            shape((1, rows, HQ * HD), BF16),
        ],
        scratch_shapes=[
            pltpu.VMEM((1, rows, kv_width), BF16),
            pltpu.VMEM((1, rows, kv_width), BF16),
            pltpu.SemaphoreType.DMA((4,)),
        ],
        compiler_params=params,
        cost_estimate=cost(0, 3 * 2**20),
        name="sum_keys",
    )(dk0, dv0, arrived2, arrived1, cos, sin, dq_next)
    return (handed_grad, key_grad, value_grad)


def solution(mesh):
    return jax.shard_map(
        shards,
        mesh=mesh,
        in_specs=(
            P("section", "ctx", None),
            P("section", "ctx", None),
            P("section", "ctx", None),
            P("section", "ctx", None),
            P("section", "ctx", None),
            P("ctx"),
            P("ctx", None),
        ),
        out_specs=(P("section", "ctx", None), P("section", "ctx", None), P("section", "ctx", None)),
        check_vma=False,
    )
```

```python
import math

import jax
import jax.numpy as jnp
from jax import lax
from jax.experimental import pallas as pl
from jax.experimental.pallas import tpu as pltpu
from jax.sharding import PartitionSpec as P

HQ = 32
HK = 4
HD = 128
RATIO = HQ // HK
HALF = HD // 2
FETCH = 2
PAIR = 2

ROPE_BASE = 1000000.0
TRAINED_CONTEXT = 32768.0
YARN_FACTOR = 4.0
NEG_LARGE = -1e30
SCORE_SCALE = HD ** (-0.5)
EXP2_SCALE = SCORE_SCALE / math.log(2.0)

F32 = jnp.float32
BF16 = jnp.bfloat16


def from_behind(value, axis, steps):
    count = lax.axis_size(axis)
    initial, last = (max(0, -steps), min(count, count - steps))
    return lax.ppermute(value, axis, [(source, source + steps) for source in range(initial, last)])


def dot_nn(left, right):
    return lax.dot_general(left, right, (((1,), (0,)), ((), ())), preferred_element_type=F32)


def dot_nt(left, right):
    return lax.dot_general(left, right, (((1,), (1,)), ((), ())), preferred_element_type=F32)


def frequencies(rows, columns):
    def correction(rotations):
        return HD * math.log(TRAINED_CONTEXT / (rotations * 2.0 * math.pi)) / (2.0 * math.log(ROPE_BASE))

    lower_dim = max(math.floor(correction(32.0)), 0)
    upper_dim = min(math.ceil(correction(1.0)), HD - 1)
    spread_dims = max(upper_dim - lower_dim, 0.001)
    indices = lax.broadcasted_iota(jnp.int32, (rows, columns), 0).astype(F32)
    extrapolated = jnp.exp(indices * F32(-2.0 / HD * math.log(ROPE_BASE)))
    ramp_weight = jnp.clip((indices - lower_dim) / spread_dims, 0.0, 1.0)
    return extrapolated / YARN_FACTOR * ramp_weight + extrapolated * (1.0 - ramp_weight)


def half_tables(positions):
    factor = 0.1 * math.log(YARN_FACTOR) + 1.0
    angles = frequencies(HALF, positions.shape[1]) * positions.astype(F32)
    return jnp.cos(angles) * factor, jnp.sin(angles) * factor


def upright(cos_t, sin_t):
    cosine = jnp.concatenate([cos_t, cos_t], axis=0).T
    signed_sine = jnp.concatenate([sin_t, -sin_t], axis=0).T
    return cosine, signed_sine


def rotate(values, cosine, signed_sine):
    return values * cosine - pltpu.roll(values, HALF, 1) * signed_sine


def unrotate(values, cosine, signed_sine):
    return values * cosine + pltpu.roll(values, HALF, 1) * signed_sine


def head_columns(head):
    return slice(head * HD, (head + 1) * HD)


def stack_heads(ref, group, first):
    return jnp.concatenate([ref[group, :, head_columns(first + i)] for i in range(PAIR)], axis=0)


def block_diagonal(upper, lower):
    zero = jnp.zeros_like(upper)
    return jnp.concatenate(
        [jnp.concatenate([upper, zero], axis=1), jnp.concatenate([zero, lower], axis=1)], axis=0
    )


def group_rows(ref, group, columns):
    pairs = range(RATIO // PAIR)
    return jnp.concatenate([ref[group * len(pairs) + i, :, columns] for i in pairs], axis=0)


def pack_kernel(k_hbm, v_hbm, kv_ref, arrived):
    copies = [
        pltpu.make_async_copy(source.at[:, head_columns(group)], kv_ref.at[which, group], arrived.at[which, group])
        for which, source in enumerate((k_hbm, v_hbm))
        for group in range(HK)
    ]
    for copy in copies:
        copy.start()
    for copy in copies:
        copy.wait()


def own_kernel(
    first_ref, doc_ref, q_hbm, k_hbm, v_hbm, o_hbm, g_hbm,
    qg_ref, prob_ref, ds_ref, kt_ref, stat_ref, half_ref, cos_ref, sin_ref, cos1_ref, sin1_ref, cos2_ref, sin2_ref,
    q_ref, k_ref, v_ref, o_ref, g_ref, arrived,
):
    rows = q_hbm.shape[0]
    arguments = ((k_hbm, k_ref), (q_hbm, q_ref), (v_hbm, v_ref), (g_hbm, g_ref), (o_hbm, o_ref))

    def fetch(which, group):
        source, buffer = arguments[which]
        width = buffer.shape[2]
        columns = pl.ds(pl.multiple_of(group * width, width), width)
        return pltpu.make_async_copy(source.at[:, columns], buffer.at[group], arrived.at[which, group])

    for group in range(HK):
        for which in range(len(arguments)):
            fetch(which, group).start()

    doc_row = doc_ref[...] - first_ref[0]
    columns = lax.broadcasted_iota(jnp.int32, (1, rows), 1)
    cos_t, sin_t = half_tables(columns - doc_row)
    half_ref[0] = cos_t * SCORE_SCALE
    half_ref[1] = sin_t * SCORE_SCALE
    cos_ref[...], sin_ref[...] = upright(cos_t, sin_t)
    reach = doc_row[:, 0:1]
    cos1_ref[...], sin1_ref[...] = upright(*half_tables(columns - rows - reach))
    cos2_ref[...], sin2_ref[...] = upright(*half_tables(columns - 2 * rows - reach))
    key_idx = lax.broadcasted_iota(jnp.int32, (rows, rows), 0)
    query_idx = lax.broadcasted_iota(jnp.int32, (rows, rows), 1)
    mask = (key_idx <= query_idx) & (key_idx >= doc_row)
    bias = jnp.where(mask, 0.0, NEG_LARGE)
    bias = jnp.concatenate([bias] * PAIR, axis=1)
    ones = jnp.ones((8, HD), BF16)

    @pl.loop(0, HK)
    def _(group):
        for which in range(len(arguments)):
            fetch(which, group).wait()
        cosine = cos_ref[...]
        signed_sine = sin_ref[...]
        k_rot = rotate(k_ref[group].astype(F32), cosine, signed_sine)
        kt_ref[group] = k_rot.T.astype(BF16)
        left = block_diagonal(k_rot.astype(BF16), v_ref[group])

        def products(first):
            pair = group * (RATIO // PAIR) + first // PAIR
            for i in range(PAIR):
                rows_of = slice(i * rows, (i + 1) * rows)
                q_rot = rotate(q_ref[group, :, head_columns(first + i)].astype(F32), cosine, signed_sine)
                qg_ref[pair, rows_of, :HD] = q_rot.astype(BF16)
            grads = stack_heads(g_ref, group, first)
            qg_ref[pair, :, HD:] = grads
            product = grads.astype(F32) * stack_heads(o_ref, group, first).astype(F32)
            high = product.astype(BF16)
            low = (product - high.astype(F32)).astype(BF16)
            delta = (dot_nt(ones, high) + dot_nt(ones, low))[0:1]
            both = dot_nt(left, qg_ref[pair])
            return both[:rows], both[rows:], delta

        def finish(first, scores, dprob, delta):
            at = slice(first * HD, (first + PAIR) * HD)
            scores = scores + bias
            largest = jnp.max(scores, axis=0, keepdims=True)
            prob = jnp.exp2((scores - largest) * EXP2_SCALE)
            total = jnp.sum(prob, axis=0, keepdims=True)
            dscore = (prob * (dprob - delta)).astype(BF16)
            prob_ref[group, :, at] = prob.astype(BF16)
            ds_ref[group, :, at] = dscore
            stat_ref[group, 0:1, at] = largest
            stat_ref[group, 1:2, at] = total
            stat_ref[group, 2:3, at] = delta

        ahead = products(0)
        for first in range(0, RATIO, PAIR):
            now = ahead
            if first + PAIR < RATIO:
                ahead = products(first + PAIR)
            finish(first, *now)


def reach_bias(listed, distance, doc_row, rows):
    key_idx = lax.broadcasted_iota(jnp.int32, (rows, PAIR * rows), 0)
    start = jnp.where(listed == 1, -distance * rows, -(1 << 30))
    return jnp.where(key_idx + start >= doc_row[:, 0:1], 0.0, NEG_LARGE)


def softmax_step(scores, stat_ref, group, at, in_reach):
    before = stat_ref[group, 0:1, at]
    largest = jnp.maximum(before, jnp.max(scores, axis=0, keepdims=True))
    prob = jnp.exp2((scores - jnp.where(in_reach, largest, -NEG_LARGE)) * EXP2_SCALE)
    largest = jnp.where(in_reach, largest, before)
    scale = jnp.exp2((before - largest) * EXP2_SCALE)
    total = stat_ref[group, 1:2, at] * scale + jnp.sum(prob, axis=0, keepdims=True)
    return prob, largest, total, scale


def staged(products, middle, finish):
    ahead = products(0)
    behind = None
    for first in range(0, RATIO, PAIR):
        now = ahead
        if first + PAIR < RATIO:
            ahead = products(first + PAIR)
        done = middle(first, *now)
        if behind is not None:
            finish(first - PAIR, behind)
        behind = done
    finish(RATIO - PAIR, behind)


def store_query_grad(dq_ref, group, first, dq, half_ref):
    cos_t = jnp.concatenate([half_ref[0]] * PAIR, axis=1)
    sin_t = jnp.concatenate([half_ref[1]] * PAIR, axis=1)
    upper, lower = dq[:HALF], dq[HALF:]
    dq = jnp.concatenate([upper * cos_t + lower * sin_t, lower * cos_t - upper * sin_t], axis=0).astype(BF16)
    for i in range(PAIR):
        lanes = pl.ds(pl.multiple_of((group * RATIO + first + i) * HD, HD), HD)
        dq_ref[0, :, lanes] = dq[:, head_columns(i)].T


def key_products(qg_ref, group, dscore, prob):
    dk = dot_nn(dscore, group_rows(qg_ref, group, slice(HD))) * SCORE_SCALE
    dv = dot_nn(prob, group_rows(qg_ref, group, slice(HD, 2 * HD)))
    return dk.astype(BF16), dv.astype(BF16)


def near_kernel(
    first_ref, list_ref, doc_ref, qg_ref, kv_ref, ds0_ref, kt0_ref, stat_ref, half_ref, cos_ref, sin_ref,
    dq_ref, ret2_ref, ret1_ref, scale_ref, own_ref, prob_ref, ds_ref, kt_ref, next_ref,
):
    rows = doc_ref.shape[1]
    doc_row = doc_ref[...] - first_ref[0]
    in_reach = jnp.concatenate([doc_row == doc_row[:, 0:1]] * PAIR, axis=1)
    bias = reach_bias(list_ref[0, 0], 1, doc_row, rows)

    def attend(last):
        @pl.loop(0, HK)
        def _(group):
            k_rot = rotate(kv_ref[0, group].astype(F32), cos_ref[...], sin_ref[...])
            k_rot_t = k_rot.T.astype(BF16)
            left = block_diagonal(k_rot.astype(BF16), kv_ref[1, group])
            both_t = jnp.concatenate([k_rot_t, kt0_ref[group]], axis=1)

            def products(first):
                both = dot_nt(left, qg_ref[group * (RATIO // PAIR) + first // PAIR])
                return both[:rows], both[rows:]

            def middle(first, scores, dprob):
                at = slice(first * HD, (first + PAIR) * HD)
                prob, largest, total, scale = softmax_step(scores + bias, stat_ref, group, at, in_reach)
                delta = stat_ref[group, 2:3, at]
                if last:
                    inverse = 1.0 / total
                    scale = scale * inverse
                    prob = prob * inverse
                    scale_ref[group, 0:1, at] = scale
                prob = prob.astype(BF16)
                dscore = prob * (dprob - delta).astype(BF16)
                prob_ref[group, :, at] = prob
                ds_ref[group, :, at] = dscore
                if last:
                    own_dscore = ds0_ref[group, :, at] * scale.astype(BF16)
                    own_ref[group, :, at] = own_dscore
                    return jnp.concatenate([dscore, own_dscore], axis=0)
                next_ref[group, 0:1, at] = largest
                next_ref[group, 1:2, at] = total
                next_ref[group, 2:3, at] = delta
                next_ref[group, 3:4, at] = scale
                return None

            def finish(first, dscore):
                if last:
                    store_query_grad(dq_ref, group, first, dot_nn(both_t, dscore), half_ref)

            staged(products, middle, finish)
            if last:
                ret1_ref[0, group], ret1_ref[1, group] = key_products(qg_ref, group, ds_ref[group], prob_ref[group])
                ret2_ref[0, group] = jnp.zeros((rows, HD), BF16)
                ret2_ref[1, group] = jnp.zeros((rows, HD), BF16)
            else:
                kt_ref[group] = k_rot_t

    pl.when(list_ref[0, 1] != 1)(lambda: attend(True))
    pl.when(list_ref[0, 1] == 1)(lambda: attend(False))


def far_kernel(
    first_ref, list_ref, doc_ref, qg_ref, kv_ref, ds0_ref, kt0_ref, half_ref, cos_ref, sin_ref,
    prob1_ref, ds1_ref, kt1_ref, stat_ref, *refs,
):
    dq_ref, ret2_ref, ret1_ref, scale_ref, own_ref, prob_buf, ds_buf = refs[5:]
    rows = doc_ref.shape[1]
    doc_row = doc_ref[...] - first_ref[0]
    in_reach = jnp.concatenate([doc_row == doc_row[:, 0:1]] * PAIR, axis=1)

    def attend(skipped):
        used = rows - skipped
        bias = reach_bias(list_ref[0, 1], 2, doc_row, rows)[skipped:]

        @pl.loop(0, HK)
        def _(group):
            k_rot = rotate(kv_ref[0, group, skipped:, :].astype(F32), cos_ref[skipped:, :], sin_ref[skipped:, :])
            left = block_diagonal(k_rot.astype(BF16), kv_ref[1, group, skipped:, :])
            k_rot_t = k_rot.T.astype(BF16)
            near_t = jnp.concatenate([kt1_ref[group], kt0_ref[group]], axis=1)

            def products(first):
                both = dot_nt(left, qg_ref[group * (RATIO // PAIR) + first // PAIR])
                return both[:used], both[used:]

            def middle(first, scores, dprob):
                at = slice(first * HD, (first + PAIR) * HD)
                prob, _, total, scale = softmax_step(scores + bias, stat_ref, group, at, in_reach)
                inverse = 1.0 / total
                near_scale = scale * inverse
                own_scale = near_scale * stat_ref[group, 3:4, at]
                scale_ref[group, 0:1, at] = own_scale
                prob = (prob * inverse).astype(BF16)
                dscore = prob * (dprob - stat_ref[group, 2:3, at]).astype(BF16)
                near_scale = near_scale.astype(BF16)
                near_dscore = ds1_ref[group, :, at] * near_scale
                own_dscore = ds0_ref[group, :, at] * own_scale.astype(BF16)
                own_ref[group, :, at] = own_dscore
                prob_buf[:used, at] = prob
                prob_buf[used : used + rows, at] = prob1_ref[group, :, at] * near_scale
                ds_buf[:used, at] = dscore
                ds_buf[used : used + rows, at] = near_dscore
                return dscore, jnp.concatenate([near_dscore, own_dscore], axis=0)

            def finish(first, dscores):
                dq = dot_nn(near_t, dscores[1]) + dot_nn(k_rot_t, dscores[0])
                store_query_grad(dq_ref, group, first, dq, half_ref)

            staged(products, middle, finish)
            grads = key_products(qg_ref, group, ds_buf[: used + rows, :], prob_buf[: used + rows, :])
            for which, grad in enumerate(grads):
                ret1_ref[which, group] = grad[used:]
                ret2_ref[which, group, skipped:, :] = grad[:used]
                if skipped:
                    ret2_ref[which, group, :skipped, :] = jnp.zeros((skipped, HD), BF16)

    @pl.when(list_ref[0, 1] == 1)
    def _():
        farthest = jnp.min(doc_row.astype(F32))
        pl.when(farthest >= -rows - rows // 2)(lambda: attend(rows // 2))
        pl.when(farthest < -rows - rows // 2)(lambda: attend(0))


def own_kv_kernel(qg_ref, prob_ref, ds_ref, scale_ref, dk_ref, dv_ref):
    @pl.loop(0, HK)
    def _(group):
        prob = (prob_ref[group].astype(F32) * scale_ref[group, 0:1, :]).astype(BF16)
        dk_ref[group] = dot_nn(ds_ref[group], group_rows(qg_ref, group, slice(HD))) * SCORE_SCALE
        dv_ref[group] = dot_nn(prob, group_rows(qg_ref, group, slice(HD, 2 * HD)))


def sum_kernel(
    dk_ref, dv_ref, ret2_ref, ret1_ref, cos_ref, sin_ref, dq_ref, key_hbm, value_hbm, handed_hbm, key_buf, value_buf, copied
):
    rows = dq_ref.shape[1]
    half = rows // 2
    copies = [
        pltpu.make_async_copy(dq_ref.at[:, pl.ds(i * half, half)], handed_hbm.at[:, pl.ds(i * half, half)], copied.at[i])
        for i in range(2)
    ]
    for copy in copies:
        copy.start()
    for group in range(HK):
        at = head_columns(group)
        dv = dv_ref[group] + ret1_ref[1, group].astype(F32) + ret2_ref[1, group].astype(F32)
        value_buf[0, :, at] = dv.astype(BF16)
    copies.append(pltpu.make_async_copy(value_buf, value_hbm, copied.at[2]))
    copies[-1].start()
    for group in range(HK):
        at = head_columns(group)
        dk = dk_ref[group] + ret1_ref[0, group].astype(F32) + ret2_ref[0, group].astype(F32)
        key_buf[0, :, at] = unrotate(dk, cos_ref[...], sin_ref[...]).astype(BF16)
    copies.append(pltpu.make_async_copy(key_buf, key_hbm, copied.at[3]))
    copies[-1].start()
    for copy in copies:
        copy.wait()


def cost(flops, moved, exps=0):
    return pl.CostEstimate(flops=int(flops), bytes_accessed=int(moved), transcendentals=int(exps))


def shards(query_heads, key_heads, value_heads, attn_output, output_grad, doc_start, fetch_list):
    rows = query_heads.shape[1]
    wide = RATIO * HD
    kv_width = HK * HD
    first_row = (lax.axis_index("ctx") * rows).astype(jnp.int32).reshape(1)
    doc_row = doc_start.reshape(1, rows)
    smem = pl.BlockSpec(memory_space=pltpu.SMEM)
    vmem = pl.BlockSpec(memory_space=pltpu.VMEM)
    hbm = pl.BlockSpec(memory_space=pltpu.HBM)
    params = pltpu.CompilerParams(vmem_limit_bytes=40 * 1024 * 1024)
    shape = jax.ShapeDtypeStruct
    block_flops = 2 * HQ * rows * rows * HD
    arguments = [
        pltpu.with_memory_space_constraint(x[0], pltpu.HBM)
        for x in (query_heads, key_heads, value_heads, attn_output, output_grad)
    ]

    kv = pl.pallas_call(
        pack_kernel,
        in_specs=[hbm, hbm],
        out_specs=vmem,
        out_shape=shape((2, HK, rows, HD), BF16),
        scratch_shapes=[pltpu.SemaphoreType.DMA((2, HK))],
        compiler_params=params,
        cost_estimate=cost(0, 2**19),
        name="pack_keys",
    )(arguments[1], arguments[2])
    kv2 = from_behind(kv, "ctx", 2)
    kv1 = from_behind(kv, "ctx", 1)

    qg, prob0, ds0, k_own_t, stat, half, cos, sin, cos1, sin1, cos2, sin2 = pl.pallas_call(
        own_kernel,
        in_specs=[smem, vmem] + [hbm] * 5,
        out_specs=[vmem] * 12,
        out_shape=[
            shape((HQ // PAIR, PAIR * rows, 2 * HD), BF16),
            shape((HK, rows, RATIO * rows), BF16),
            shape((HK, rows, RATIO * rows), BF16),
            shape((HK, HD, rows), BF16),
            shape((HK, 8, RATIO * rows), F32),
            shape((2, HALF, rows), F32),
            shape((rows, HD), F32),
            shape((rows, HD), F32),
            shape((rows, HD), F32),
            shape((rows, HD), F32),
            shape((rows, HD), F32),
            shape((rows, HD), F32),
        ],
        scratch_shapes=[
            pltpu.VMEM((HK, rows, wide), BF16),
            pltpu.VMEM((HK, rows, HD), BF16),
            pltpu.VMEM((HK, rows, HD), BF16),
            pltpu.VMEM((HK, rows, wide), BF16),
            pltpu.VMEM((HK, rows, wide), BF16),
            pltpu.SemaphoreType.DMA((5, HK)),
        ],
        compiler_params=params,
        cost_estimate=cost(3 * block_flops, 9 * 2**20, HQ * rows * rows),
        name="own_block",
    )(first_row, pltpu.with_memory_space_constraint(doc_row, pltpu.HBM), *arguments)

    results = [
        shape((1, rows, HQ * HD), BF16),
        shape((2, HK, rows, HD), BF16),
        shape((2, HK, rows, HD), BF16),
        shape((HK, 8, RATIO * rows), F32),
        shape((HK, rows, RATIO * rows), BF16),
    ]
    *settled, prob1, ds1, k_near_t, stat1 = pl.pallas_call(
        near_kernel,
        in_specs=[smem, smem] + [vmem] * 9,
        out_specs=[vmem] * 9,
        out_shape=results
        + [
            shape((HK, rows, RATIO * rows), BF16),
            shape((HK, rows, RATIO * rows), BF16),
            shape((HK, HD, rows), BF16),
            shape((HK, 8, RATIO * rows), F32),
        ],
        compiler_params=params,
        cost_estimate=cost(5 * block_flops, 9 * 2**20, HQ * rows * rows),
        name="near_block",
    )(first_row, fetch_list, doc_row, qg, kv1, ds0, k_own_t, stat, half, cos1, sin1)

    dq, ret2, ret1, scale, ds_own = pl.pallas_call(
        far_kernel,
        in_specs=[smem, smem] + [vmem] * 17,
        out_specs=[vmem] * 5,
        out_shape=results,
        scratch_shapes=[
            pltpu.VMEM((FETCH * rows, RATIO * rows), BF16),
            pltpu.VMEM((FETCH * rows, RATIO * rows), BF16),
        ],
        input_output_aliases={14 + i: i for i in range(5)},
        compiler_params=params,
        cost_estimate=cost(5 * block_flops, 9 * 2**20, HQ * rows * rows),
        name="far_block",
    )(
        first_row, fetch_list, doc_row, qg, kv2, ds0, k_own_t, half, cos2, sin2,
        prob1, ds1, k_near_t, stat1, *settled,
    )
    arrived1 = from_behind(ret1, "ctx", -1)
    arrived2 = from_behind(ret2, "ctx", -2)
    dq_next = from_behind(dq, "section", -1)

    dk0, dv0 = pl.pallas_call(
        own_kv_kernel,
        in_specs=[vmem] * 4,
        out_specs=[vmem] * 2,
        out_shape=[shape((HK, rows, HD), F32), shape((HK, rows, HD), F32)],
        compiler_params=params,
        cost_estimate=cost(2 * block_flops, 5 * 2**20),
        name="own_keys",
    )(qg, prob0, ds_own, scale)

    key_grad, value_grad, handed_grad = pl.pallas_call(
        sum_kernel,
        in_specs=[vmem] * 6 + [pl.BlockSpec(memory_space=pl.ANY)],
        out_specs=[hbm] * 3,
        out_shape=[
            shape((1, rows, kv_width), BF16),
            shape((1, rows, kv_width), BF16),
            shape((1, rows, HQ * HD), BF16),
        ],
        scratch_shapes=[
            pltpu.VMEM((1, rows, kv_width), BF16),
            pltpu.VMEM((1, rows, kv_width), BF16),
            pltpu.SemaphoreType.DMA((4,)),
        ],
        compiler_params=params,
        cost_estimate=cost(0, 3 * 2**20),
        name="sum_keys",
    )(dk0, dv0, arrived2, arrived1, cos, sin, dq_next)
    return (handed_grad, key_grad, value_grad)


def solution(mesh):
    return jax.shard_map(
        shards,
        mesh=mesh,
        in_specs=(
            P("section", "ctx", None),
            P("section", "ctx", None),
            P("section", "ctx", None),
            P("section", "ctx", None),
            P("section", "ctx", None),
            P("ctx"),
            P("ctx", None),
        ),
        out_specs=(P("section", "ctx", None), P("section", "ctx", None), P("section", "ctx", None)),
        check_vma=False,
    )
```

```python
import math

import jax
import jax.numpy as jnp
from jax import lax
from jax.experimental import pallas as pl
from jax.experimental.pallas import tpu as pltpu
from jax.sharding import PartitionSpec as P

HQ = 32
HK = 4
HD = 128
RATIO = HQ // HK
HALF = HD // 2
FETCH = 2
PAIR = 2

ROPE_BASE = 1000000.0
TRAINED_CONTEXT = 32768.0
YARN_FACTOR = 4.0
NEG_LARGE = -1e30
SCORE_SCALE = HD ** (-0.5)
EXP2_SCALE = SCORE_SCALE / math.log(2.0)

F32 = jnp.float32
BF16 = jnp.bfloat16


def from_behind(value, axis, steps):
    count = lax.axis_size(axis)
    initial, last = (max(0, -steps), min(count, count - steps))
    return lax.ppermute(value, axis, [(source, source + steps) for source in range(initial, last)])


def dot_nn(left, right):
    return lax.dot_general(left, right, (((1,), (0,)), ((), ())), preferred_element_type=F32)


def dot_nt(left, right):
    return lax.dot_general(left, right, (((1,), (1,)), ((), ())), preferred_element_type=F32)


def frequencies(rows, columns):
    def correction(rotations):
        return HD * math.log(TRAINED_CONTEXT / (rotations * 2.0 * math.pi)) / (2.0 * math.log(ROPE_BASE))

    lower_dim = max(math.floor(correction(32.0)), 0)
    upper_dim = min(math.ceil(correction(1.0)), HD - 1)
    spread_dims = max(upper_dim - lower_dim, 0.001)
    indices = lax.broadcasted_iota(jnp.int32, (rows, columns), 0).astype(F32)
    extrapolated = jnp.exp(indices * F32(-2.0 / HD * math.log(ROPE_BASE)))
    ramp_weight = jnp.clip((indices - lower_dim) / spread_dims, 0.0, 1.0)
    return extrapolated / YARN_FACTOR * ramp_weight + extrapolated * (1.0 - ramp_weight)


def half_tables(positions):
    factor = 0.1 * math.log(YARN_FACTOR) + 1.0
    angles = frequencies(HALF, positions.shape[1]) * positions.astype(F32)
    return jnp.cos(angles) * factor, jnp.sin(angles) * factor


def upright(cos_t, sin_t):
    cosine = jnp.concatenate([cos_t, cos_t], axis=0).T
    signed_sine = jnp.concatenate([sin_t, -sin_t], axis=0).T
    return cosine, signed_sine


def rotate(values, cosine, signed_sine):
    return values * cosine - pltpu.roll(values, HALF, 1) * signed_sine


def unrotate(values, cosine, signed_sine):
    return values * cosine + pltpu.roll(values, HALF, 1) * signed_sine


def head_columns(head):
    return slice(head * HD, (head + 1) * HD)


def stack_heads(ref, group, first):
    return jnp.concatenate([ref[group, :, head_columns(first + i)] for i in range(PAIR)], axis=0)


def block_diagonal(upper, lower):
    zero = jnp.zeros_like(upper)
    return jnp.concatenate(
        [jnp.concatenate([upper, zero], axis=1), jnp.concatenate([zero, lower], axis=1)], axis=0
    )


def group_rows(ref, group, columns):
    pairs = range(RATIO // PAIR)
    return jnp.concatenate([ref[group * len(pairs) + i, :, columns] for i in pairs], axis=0)


def pack_kernel(k_hbm, v_hbm, kv_ref, arrived):
    copies = [
        pltpu.make_async_copy(source.at[:, head_columns(group)], kv_ref.at[which, group], arrived.at[which, group])
        for which, source in enumerate((k_hbm, v_hbm))
        for group in range(HK)
    ]
    for copy in copies:
        copy.start()
    for copy in copies:
        copy.wait()


def own_kernel(
    first_ref, list_ref, doc_ref, q_hbm, k_hbm, v_hbm, o_hbm, g_hbm,
    notes_ref, qg_ref, prob_ref, ds_ref, kt_ref, stat_ref, half_ref, cos_ref, sin_ref, cos1_ref, sin1_ref, cos2_ref, sin2_ref,
    q_ref, k_ref, v_ref, o_ref, g_ref, arrived,
):
    rows = q_hbm.shape[0]
    arguments = ((k_hbm, k_ref), (q_hbm, q_ref), (v_hbm, v_ref), (g_hbm, g_ref), (o_hbm, o_ref))

    def fetch(which, group):
        source, buffer = arguments[which]
        width = buffer.shape[2]
        columns = pl.ds(pl.multiple_of(group * width, width), width)
        return pltpu.make_async_copy(source.at[:, columns], buffer.at[group], arrived.at[which, group])

    for group in range(HK):
        for which in range(len(arguments)):
            fetch(which, group).start()

    doc_row = doc_ref[...] - first_ref[0]
    columns = lax.broadcasted_iota(jnp.int32, (1, rows), 1)
    cos_t, sin_t = half_tables(columns - doc_row)
    half_ref[0] = cos_t * SCORE_SCALE
    half_ref[1] = sin_t * SCORE_SCALE
    cos_ref[...], sin_ref[...] = upright(cos_t, sin_t)
    reach = doc_row[:, 0:1]
    notes_ref[0:1, :] = doc_row.astype(F32)
    for distance in range(1, FETCH + 1):
        listed = jnp.where(list_ref[:, distance - 1 : distance] == 1, 1.0, 0.0)
        notes_ref[distance : distance + 1, :] = jnp.broadcast_to(listed, (1, rows))
    cos1_ref[...], sin1_ref[...] = upright(*half_tables(columns - rows - reach))
    cos2_ref[...], sin2_ref[...] = upright(*half_tables(columns - 2 * rows - reach))
    key_idx = lax.broadcasted_iota(jnp.int32, (rows, rows), 0)
    query_idx = lax.broadcasted_iota(jnp.int32, (rows, rows), 1)
    mask = (key_idx <= query_idx) & (key_idx >= doc_row)
    bias = jnp.where(mask, 0.0, NEG_LARGE)
    bias = jnp.concatenate([bias] * PAIR, axis=1)
    ones = jnp.ones((8, HD), BF16)

    @pl.loop(0, HK)
    def _(group):
        for which in range(len(arguments)):
            fetch(which, group).wait()
        cosine = cos_ref[...]
        signed_sine = sin_ref[...]
        k_rot = rotate(k_ref[group].astype(F32), cosine, signed_sine)
        kt_ref[group] = k_rot.T.astype(BF16)
        left = block_diagonal(k_rot.astype(BF16), v_ref[group])

        def products(first):
            pair = group * (RATIO // PAIR) + first // PAIR
            for i in range(PAIR):
                rows_of = slice(i * rows, (i + 1) * rows)
                q_rot = rotate(q_ref[group, :, head_columns(first + i)].astype(F32), cosine, signed_sine)
                qg_ref[pair, rows_of, :HD] = q_rot.astype(BF16)
            grads = stack_heads(g_ref, group, first)
            qg_ref[pair, :, HD:] = grads
            product = grads.astype(F32) * stack_heads(o_ref, group, first).astype(F32)
            high = product.astype(BF16)
            low = (product - high.astype(F32)).astype(BF16)
            delta = (dot_nt(ones, high) + dot_nt(ones, low))[0:1]
            both = dot_nt(left, qg_ref[pair])
            return both[:rows], both[rows:], delta

        def finish(first, scores, dprob, delta):
            at = slice(first * HD, (first + PAIR) * HD)
            scores = scores + bias
            largest = jnp.max(scores, axis=0, keepdims=True)
            prob = jnp.exp2((scores - largest) * EXP2_SCALE)
            total = jnp.sum(prob, axis=0, keepdims=True)
            dscore = (prob * (dprob - delta)).astype(BF16)
            prob_ref[group, :, at] = prob.astype(BF16)
            ds_ref[group, :, at] = dscore
            stat_ref[group, 0:1, at] = largest
            stat_ref[group, 1:2, at] = total
            stat_ref[group, 2:3, at] = delta

        ahead = products(0)
        for first in range(0, RATIO, PAIR):
            now = ahead
            if first + PAIR < RATIO:
                ahead = products(first + PAIR)
            finish(first, *now)


def reach_bias(notes_ref, distance):
    rows = notes_ref.shape[1]
    key_idx = lax.broadcasted_iota(jnp.int32, (rows, PAIR * rows), 0).astype(F32) - distance * rows
    reach = notes_ref[0:1, 0:1]
    listed = notes_ref[distance : distance + 1, 0:1]
    return jnp.where((key_idx >= reach) & (listed > 0.0), 0.0, NEG_LARGE)


def reached(notes_ref):
    doc_row = notes_ref[0:1, :]
    return jnp.concatenate([doc_row == doc_row[:, 0:1]] * PAIR, axis=1)


def softmax_step(scores, stat_ref, group, at, in_reach):
    before = stat_ref[group, 0:1, at]
    largest = jnp.maximum(before, jnp.max(scores, axis=0, keepdims=True))
    prob = jnp.exp2((scores - jnp.where(in_reach, largest, -NEG_LARGE)) * EXP2_SCALE)
    largest = jnp.where(in_reach, largest, before)
    scale = jnp.exp2((before - largest) * EXP2_SCALE)
    total = stat_ref[group, 1:2, at] * scale + jnp.sum(prob, axis=0, keepdims=True)
    return prob, largest, total, scale


def staged(products, middle, finish):
    ahead = products(0)
    behind = None
    for first in range(0, RATIO, PAIR):
        now = ahead
        if first + PAIR < RATIO:
            ahead = products(first + PAIR)
        done = middle(first, *now)
        if behind is not None:
            finish(first - PAIR, behind)
        behind = done
    finish(RATIO - PAIR, behind)


def store_query_grad(dq_ref, group, first, dq, half_ref):
    cos_t = jnp.concatenate([half_ref[0]] * PAIR, axis=1)
    sin_t = jnp.concatenate([half_ref[1]] * PAIR, axis=1)
    upper, lower = dq[:HALF], dq[HALF:]
    dq = jnp.concatenate([upper * cos_t + lower * sin_t, lower * cos_t - upper * sin_t], axis=0).astype(BF16)
    for i in range(PAIR):
        lanes = pl.ds(pl.multiple_of((group * RATIO + first + i) * HD, HD), HD)
        dq_ref[0, :, lanes] = dq[:, head_columns(i)].T


def key_products(qg_ref, group, dscore, prob):
    dk = dot_nn(dscore, group_rows(qg_ref, group, slice(HD))) * SCORE_SCALE
    dv = dot_nn(prob, group_rows(qg_ref, group, slice(HD, 2 * HD)))
    return dk.astype(BF16), dv.astype(BF16)


def near_kernel(
    notes_ref, qg_ref, kv_ref, ds0_ref, kt0_ref, stat_ref, half_ref, cos_ref, sin_ref,
    dq_ref, ret2_ref, ret1_ref, scale_ref, own_ref, prob_ref, ds_ref, kt_ref, next_ref,
):
    rows = notes_ref.shape[1]
    in_reach = reached(notes_ref)
    bias = reach_bias(notes_ref, 1)

    def attend(last):
        @pl.loop(0, HK, unroll=2)
        def _(group):
            k_rot = rotate(kv_ref[0, group].astype(F32), cos_ref[...], sin_ref[...])
            k_rot_t = k_rot.T.astype(BF16)
            left = block_diagonal(k_rot.astype(BF16), kv_ref[1, group])
            both_t = jnp.concatenate([k_rot_t, kt0_ref[group]], axis=1)

            def products(first):
                both = dot_nt(left, qg_ref[group * (RATIO // PAIR) + first // PAIR])
                return both[:rows], both[rows:]

            def middle(first, scores, dprob):
                at = slice(first * HD, (first + PAIR) * HD)
                prob, largest, total, scale = softmax_step(scores + bias, stat_ref, group, at, in_reach)
                delta = stat_ref[group, 2:3, at]
                if last:
                    inverse = 1.0 / total
                    scale = scale * inverse
                    prob = prob * inverse
                    scale_ref[group, 0:1, at] = scale
                prob = prob.astype(BF16)
                dscore = prob * (dprob - delta).astype(BF16)
                prob_ref[group, :, at] = prob
                ds_ref[group, :, at] = dscore
                if last:
                    own_dscore = ds0_ref[group, :, at] * scale.astype(BF16)
                    own_ref[group, :, at] = own_dscore
                    return jnp.concatenate([dscore, own_dscore], axis=0)
                next_ref[group, 0:1, at] = largest
                next_ref[group, 1:2, at] = total
                next_ref[group, 2:3, at] = delta
                next_ref[group, 3:4, at] = scale
                return None

            def finish(first, dscore):
                if last:
                    store_query_grad(dq_ref, group, first, dot_nn(both_t, dscore), half_ref)

            staged(products, middle, finish)
            if last:
                ret1_ref[0, group], ret1_ref[1, group] = key_products(qg_ref, group, ds_ref[group], prob_ref[group])
                ret2_ref[0, group] = jnp.zeros((rows, HD), BF16)
                ret2_ref[1, group] = jnp.zeros((rows, HD), BF16)
            else:
                kt_ref[group] = k_rot_t

    goes_on = jnp.max(notes_ref[2:3, :]) > 0.0
    pl.when(jnp.logical_not(goes_on))(lambda: attend(True))
    pl.when(goes_on)(lambda: attend(False))


def far_kernel(
    notes_ref, qg_ref, kv_ref, ds0_ref, kt0_ref, half_ref, cos_ref, sin_ref,
    prob1_ref, ds1_ref, kt1_ref, stat_ref, *refs,
):
    dq_ref, ret2_ref, ret1_ref, scale_ref, own_ref, prob_buf, ds_buf = refs[5:]
    rows = notes_ref.shape[1]

    def attend(skipped):
        used = rows - skipped
        in_reach = reached(notes_ref)
        bias = reach_bias(notes_ref, 2)[skipped:]

        @pl.loop(0, HK, unroll=2)
        def _(group):
            k_rot = rotate(kv_ref[0, group, skipped:, :].astype(F32), cos_ref[skipped:, :], sin_ref[skipped:, :])
            left = block_diagonal(k_rot.astype(BF16), kv_ref[1, group, skipped:, :])
            k_rot_t = k_rot.T.astype(BF16)
            near_t = jnp.concatenate([kt1_ref[group], kt0_ref[group]], axis=1)

            def products(first):
                both = dot_nt(left, qg_ref[group * (RATIO // PAIR) + first // PAIR])
                return both[:used], both[used:]

            def middle(first, scores, dprob):
                at = slice(first * HD, (first + PAIR) * HD)
                prob, _, total, scale = softmax_step(scores + bias, stat_ref, group, at, in_reach)
                inverse = 1.0 / total
                near_scale = scale * inverse
                own_scale = near_scale * stat_ref[group, 3:4, at]
                scale_ref[group, 0:1, at] = own_scale
                prob = (prob * inverse).astype(BF16)
                dscore = prob * (dprob - stat_ref[group, 2:3, at]).astype(BF16)
                near_scale = near_scale.astype(BF16)
                near_dscore = ds1_ref[group, :, at] * near_scale
                own_dscore = ds0_ref[group, :, at] * own_scale.astype(BF16)
                own_ref[group, :, at] = own_dscore
                prob_buf[:used, at] = prob
                prob_buf[used : used + rows, at] = prob1_ref[group, :, at] * near_scale
                ds_buf[:used, at] = dscore
                ds_buf[used : used + rows, at] = near_dscore
                return dscore, jnp.concatenate([near_dscore, own_dscore], axis=0)

            def finish(first, dscores):
                dq = dot_nn(near_t, dscores[1]) + dot_nn(k_rot_t, dscores[0])
                store_query_grad(dq_ref, group, first, dq, half_ref)

            staged(products, middle, finish)
            grads = key_products(qg_ref, group, ds_buf[: used + rows, :], prob_buf[: used + rows, :])
            for which, grad in enumerate(grads):
                ret1_ref[which, group] = grad[used:]
                ret2_ref[which, group, skipped:, :] = grad[:used]
                if skipped:
                    ret2_ref[which, group, :skipped, :] = jnp.zeros((skipped, HD), BF16)

    @pl.when(jnp.max(notes_ref[2:3, :]) > 0.0)
    def _():
        farthest = jnp.min(notes_ref[0:1, :])
        pl.when(farthest >= -rows - rows // 2)(lambda: attend(rows // 2))
        pl.when(farthest < -rows - rows // 2)(lambda: attend(0))


def own_kv_kernel(qg_ref, prob_ref, ds_ref, scale_ref, dk_ref, dv_ref):
    @pl.loop(0, HK)
    def _(group):
        prob = (prob_ref[group].astype(F32) * scale_ref[group, 0:1, :]).astype(BF16)
        dk_ref[group] = dot_nn(ds_ref[group], group_rows(qg_ref, group, slice(HD))) * SCORE_SCALE
        dv_ref[group] = dot_nn(prob, group_rows(qg_ref, group, slice(HD, 2 * HD)))


def sum_kernel(
    dk_ref, dv_ref, ret2_ref, ret1_ref, cos_ref, sin_ref, dq_ref, key_hbm, value_hbm, handed_hbm, key_buf, value_buf, copied
):
    rows = dq_ref.shape[1]
    half = rows // 2
    copies = [
        pltpu.make_async_copy(dq_ref.at[:, pl.ds(i * half, half)], handed_hbm.at[:, pl.ds(i * half, half)], copied.at[i])
        for i in range(2)
    ]
    for copy in copies:
        copy.start()
    for group in range(HK):
        at = head_columns(group)
        dv = dv_ref[group] + ret1_ref[1, group].astype(F32) + ret2_ref[1, group].astype(F32)
        value_buf[0, :, at] = dv.astype(BF16)
    copies.append(pltpu.make_async_copy(value_buf, value_hbm, copied.at[2]))
    copies[-1].start()
    for group in range(HK):
        at = head_columns(group)
        dk = dk_ref[group] + ret1_ref[0, group].astype(F32) + ret2_ref[0, group].astype(F32)
        key_buf[0, :, at] = unrotate(dk, cos_ref[...], sin_ref[...]).astype(BF16)
    copies.append(pltpu.make_async_copy(key_buf, key_hbm, copied.at[3]))
    copies[-1].start()
    for copy in copies:
        copy.wait()


def cost(flops, moved, exps=0):
    return pl.CostEstimate(flops=int(flops), bytes_accessed=int(moved), transcendentals=int(exps))


def shards(query_heads, key_heads, value_heads, attn_output, output_grad, doc_start, fetch_list):
    rows = query_heads.shape[1]
    wide = RATIO * HD
    kv_width = HK * HD
    first_row = (lax.axis_index("ctx") * rows).astype(jnp.int32).reshape(1)
    doc_row = doc_start.reshape(1, rows)
    smem = pl.BlockSpec(memory_space=pltpu.SMEM)
    vmem = pl.BlockSpec(memory_space=pltpu.VMEM)
    hbm = pl.BlockSpec(memory_space=pltpu.HBM)
    params = pltpu.CompilerParams(vmem_limit_bytes=40 * 1024 * 1024)
    shape = jax.ShapeDtypeStruct
    block_flops = 2 * HQ * rows * rows * HD
    arguments = [
        pltpu.with_memory_space_constraint(x[0], pltpu.HBM)
        for x in (query_heads, key_heads, value_heads, attn_output, output_grad)
    ]

    kv = pl.pallas_call(
        pack_kernel,
        in_specs=[hbm, hbm],
        out_specs=vmem,
        out_shape=shape((2, HK, rows, HD), BF16),
        scratch_shapes=[pltpu.SemaphoreType.DMA((2, HK))],
        compiler_params=params,
        cost_estimate=cost(0, 2**19),
        name="pack_keys",
    )(arguments[1], arguments[2])
    kv2 = from_behind(kv, "ctx", 2)
    kv1 = from_behind(kv, "ctx", 1)

    notes, qg, prob0, ds0, k_own_t, stat, half, cos, sin, cos1, sin1, cos2, sin2 = pl.pallas_call(
        own_kernel,
        in_specs=[smem, vmem, vmem] + [hbm] * 5,
        out_specs=[vmem] * 13,
        out_shape=[
            shape((8, rows), F32),
            shape((HQ // PAIR, PAIR * rows, 2 * HD), BF16),
            shape((HK, rows, RATIO * rows), BF16),
            shape((HK, rows, RATIO * rows), BF16),
            shape((HK, HD, rows), BF16),
            shape((HK, 8, RATIO * rows), F32),
            shape((2, HALF, rows), F32),
            shape((rows, HD), F32),
            shape((rows, HD), F32),
            shape((rows, HD), F32),
            shape((rows, HD), F32),
            shape((rows, HD), F32),
            shape((rows, HD), F32),
        ],
        scratch_shapes=[
            pltpu.VMEM((HK, rows, wide), BF16),
            pltpu.VMEM((HK, rows, HD), BF16),
            pltpu.VMEM((HK, rows, HD), BF16),
            pltpu.VMEM((HK, rows, wide), BF16),
            pltpu.VMEM((HK, rows, wide), BF16),
            pltpu.SemaphoreType.DMA((5, HK)),
        ],
        compiler_params=params,
        cost_estimate=cost(3 * block_flops, 9 * 2**20, HQ * rows * rows),
        name="own_block",
    )(first_row, *(pltpu.with_memory_space_constraint(x, pltpu.HBM) for x in (fetch_list, doc_row)), *arguments)

    results = [
        shape((1, rows, HQ * HD), BF16),
        shape((2, HK, rows, HD), BF16),
        shape((2, HK, rows, HD), BF16),
        shape((HK, 8, RATIO * rows), F32),
        shape((HK, rows, RATIO * rows), BF16),
    ]
    *settled, prob1, ds1, k_near_t, stat1 = pl.pallas_call(
        near_kernel,
        in_specs=[vmem] * 9,
        out_specs=[vmem] * 9,
        out_shape=results
        + [
            shape((HK, rows, RATIO * rows), BF16),
            shape((HK, rows, RATIO * rows), BF16),
            shape((HK, HD, rows), BF16),
            shape((HK, 8, RATIO * rows), F32),
        ],
        compiler_params=params,
        cost_estimate=cost(5 * block_flops, 9 * 2**20, HQ * rows * rows),
        name="near_block",
    )(notes, qg, kv1, ds0, k_own_t, stat, half, cos1, sin1)

    dq, ret2, ret1, scale, ds_own = pl.pallas_call(
        far_kernel,
        in_specs=[vmem] * 17,
        out_specs=[vmem] * 5,
        out_shape=results,
        scratch_shapes=[
            pltpu.VMEM((FETCH * rows, RATIO * rows), BF16),
            pltpu.VMEM((FETCH * rows, RATIO * rows), BF16),
        ],
        input_output_aliases={12 + i: i for i in range(5)},
        compiler_params=params,
        cost_estimate=cost(5 * block_flops, 9 * 2**20, HQ * rows * rows),
        name="far_block",
    )(notes, qg, kv2, ds0, k_own_t, half, cos2, sin2, prob1, ds1, k_near_t, stat1, *settled)
    arrived1 = from_behind(ret1, "ctx", -1)
    arrived2 = from_behind(ret2, "ctx", -2)
    dq_next = from_behind(dq, "section", -1)

    dk0, dv0 = pl.pallas_call(
        own_kv_kernel,
        in_specs=[vmem] * 4,
        out_specs=[vmem] * 2,
        out_shape=[shape((HK, rows, HD), F32), shape((HK, rows, HD), F32)],
        compiler_params=params,
        cost_estimate=cost(2 * block_flops, 5 * 2**20),
        name="own_keys",
    )(qg, prob0, ds_own, scale)

    key_grad, value_grad, handed_grad = pl.pallas_call(
        sum_kernel,
        in_specs=[vmem] * 6 + [pl.BlockSpec(memory_space=pl.ANY)],
        out_specs=[hbm] * 3,
        out_shape=[
            shape((1, rows, kv_width), BF16),
            shape((1, rows, kv_width), BF16),
            shape((1, rows, HQ * HD), BF16),
        ],
        scratch_shapes=[
            pltpu.VMEM((1, rows, kv_width), BF16),
            pltpu.VMEM((1, rows, kv_width), BF16),
            pltpu.SemaphoreType.DMA((4,)),
        ],
        compiler_params=params,
        cost_estimate=cost(0, 3 * 2**20),
        name="sum_keys",
    )(dk0, dv0, arrived2, arrived1, cos, sin, dq_next)
    return (handed_grad, key_grad, value_grad)


def solution(mesh):
    return jax.shard_map(
        shards,
        mesh=mesh,
        in_specs=(
            P("section", "ctx", None),
            P("section", "ctx", None),
            P("section", "ctx", None),
            P("section", "ctx", None),
            P("section", "ctx", None),
            P("ctx"),
            P("ctx", None),
        ),
        out_specs=(P("section", "ctx", None), P("section", "ctx", None), P("section", "ctx", None)),
        check_vma=False,
    )
```

```python
import math

import jax
import jax.numpy as jnp
from jax import lax
from jax.experimental import pallas as pl
from jax.experimental.pallas import tpu as pltpu
from jax.sharding import PartitionSpec as P

HQ = 32
HK = 4
HD = 128
RATIO = HQ // HK
HALF = HD // 2
FETCH = 2
QUAD = 4
TILES = 4

ROPE_BASE = 1000000.0
TRAINED_CONTEXT = 32768.0
YARN_FACTOR = 4.0
NEG_LARGE = -1e30
SCORE_SCALE = HD ** (-0.5)
EXP2_SCALE = SCORE_SCALE / math.log(2.0)

F32 = jnp.float32
BF16 = jnp.bfloat16


def from_behind(value, axis, steps):
    count = lax.axis_size(axis)
    initial, last = (max(0, -steps), min(count, count - steps))
    return lax.ppermute(value, axis, [(source, source + steps) for source in range(initial, last)])


def dot_nn(left, right):
    return lax.dot_general(left, right, (((1,), (0,)), ((), ())), preferred_element_type=F32)


def dot_nt(left, right):
    return lax.dot_general(left, right, (((1,), (1,)), ((), ())), preferred_element_type=F32)


def frequencies(rows, columns):
    def correction(rotations):
        return HD * math.log(TRAINED_CONTEXT / (rotations * 2.0 * math.pi)) / (2.0 * math.log(ROPE_BASE))

    lower_dim = max(math.floor(correction(32.0)), 0)
    upper_dim = min(math.ceil(correction(1.0)), HD - 1)
    spread_dims = max(upper_dim - lower_dim, 0.001)
    indices = lax.broadcasted_iota(jnp.int32, (rows, columns), 0).astype(F32)
    extrapolated = jnp.exp(indices * F32(-2.0 / HD * math.log(ROPE_BASE)))
    ramp_weight = jnp.clip((indices - lower_dim) / spread_dims, 0.0, 1.0)
    return extrapolated / YARN_FACTOR * ramp_weight + extrapolated * (1.0 - ramp_weight)


def half_tables(positions):
    factor = 0.1 * math.log(YARN_FACTOR) + 1.0
    angles = frequencies(HALF, positions.shape[1]) * positions.astype(F32)
    return jnp.cos(angles) * factor, jnp.sin(angles) * factor


def upright(cos_t, sin_t):
    cosine = jnp.concatenate([cos_t, cos_t], axis=0).T
    signed_sine = jnp.concatenate([sin_t, -sin_t], axis=0).T
    return cosine, signed_sine


def rotate(values, cosine, signed_sine):
    return values * cosine - pltpu.roll(values, HALF, 1) * signed_sine


def unrotate(values, cosine, signed_sine):
    return values * cosine + pltpu.roll(values, HALF, 1) * signed_sine


def head_columns(head):
    return slice(head * HD, (head + 1) * HD)


def stack_heads(ref, group, first, half):
    rows = ref.shape[1] // 2
    at = slice(half * rows, (half + 1) * rows)
    return jnp.concatenate([ref[group, at, head_columns(first + i)] for i in range(QUAD)], axis=0)


def four_times(value, half):
    columns = value.shape[1] // 2
    return jnp.concatenate([value[:, half * columns : (half + 1) * columns]] * QUAD, axis=1)


def block_diagonal(upper, lower):
    zero = jnp.zeros_like(upper)
    return jnp.concatenate(
        [jnp.concatenate([upper, zero], axis=1), jnp.concatenate([zero, lower], axis=1)], axis=0
    )


def group_rows(ref, group, columns, tiles=TILES):
    return jnp.concatenate([ref[group * TILES + i, :, columns] for i in range(tiles)], axis=0)


def tile_columns(tile):
    width = RATIO * HD // TILES
    return slice(tile * width, (tile + 1) * width)


def pack_kernel(k_hbm, v_hbm, kv_ref, arrived):
    copies = [
        pltpu.make_async_copy(source.at[:, head_columns(group)], kv_ref.at[which, group], arrived.at[which, group])
        for which, source in enumerate((k_hbm, v_hbm))
        for group in range(HK)
    ]
    for copy in copies:
        copy.start()
    for copy in copies:
        copy.wait()


def own_kernel(
    first_ref, list_ref, doc_ref, q_hbm, k_hbm, v_hbm, o_hbm, g_hbm,
    notes_ref, qg_ref, prob_ref, ds_ref, kt_ref, stat_ref, half_ref, cos_ref, sin_ref, cos1_ref, sin1_ref, cos2_ref, sin2_ref,
    q_ref, k_ref, v_ref, o_ref, g_ref, arrived,
):
    rows = q_hbm.shape[0]
    arguments = ((k_hbm, k_ref), (q_hbm, q_ref), (v_hbm, v_ref), (g_hbm, g_ref), (o_hbm, o_ref))

    def fetch(which, group):
        source, buffer = arguments[which]
        width = buffer.shape[2]
        columns = pl.ds(pl.multiple_of(group * width, width), width)
        return pltpu.make_async_copy(source.at[:, columns], buffer.at[group], arrived.at[which, group])

    for group in range(HK):
        for which in range(len(arguments)):
            fetch(which, group).start()

    doc_row = doc_ref[...] - first_ref[0]
    columns = lax.broadcasted_iota(jnp.int32, (1, rows), 1)
    cos_t, sin_t = half_tables(columns - doc_row)
    cos_ref[...], sin_ref[...] = upright(cos_t, sin_t)
    reach = doc_row[:, 0:1]
    lanes = notes_ref.shape[1]
    for half in range(2):
        notes_ref[half : half + 1, :] = four_times(doc_row.astype(F32), half)
        half_ref[half, 0] = four_times(cos_t * SCORE_SCALE, half)
        half_ref[half, 1] = four_times(sin_t * SCORE_SCALE, half)
    for distance in range(1, FETCH + 1):
        listed = jnp.where(list_ref[:, distance - 1 : distance] == 1, 1.0, 0.0)
        notes_ref[distance + 1 : distance + 2, :] = jnp.broadcast_to(listed, (1, lanes))
    cos1_ref[...], sin1_ref[...] = upright(*half_tables(columns - rows - reach))
    cos2_ref[...], sin2_ref[...] = upright(*half_tables(columns - 2 * rows - reach))
    key_idx = lax.broadcasted_iota(jnp.int32, (rows, rows), 0)
    query_idx = lax.broadcasted_iota(jnp.int32, (rows, rows), 1)
    mask = (key_idx <= query_idx) & (key_idx >= doc_row)
    bias = jnp.where(mask, 0.0, NEG_LARGE)
    bias = [four_times(bias, half) for half in range(2)]
    ones = jnp.ones((8, HD), BF16)

    @pl.loop(0, HK)
    def _(group):
        for which in range(len(arguments)):
            fetch(which, group).wait()
        k_rot = rotate(k_ref[group].astype(F32), cos_ref[...], sin_ref[...])
        kt_ref[group] = k_rot.T.astype(BF16)
        left = block_diagonal(k_rot.astype(BF16), v_ref[group])

        def products(tile):
            half, quad = divmod(tile, 2)
            at = slice(half * rows // 2, (half + 1) * rows // 2)
            cosine = jnp.concatenate([cos_ref[at, :]] * QUAD, axis=0)
            signed_sine = jnp.concatenate([sin_ref[at, :]] * QUAD, axis=0)
            queries = stack_heads(q_ref, group, quad * QUAD, half).astype(F32)
            qg_ref[group * TILES + tile, :, :HD] = rotate(queries, cosine, signed_sine).astype(BF16)
            grads = stack_heads(g_ref, group, quad * QUAD, half)
            qg_ref[group * TILES + tile, :, HD:] = grads
            product = grads.astype(F32) * stack_heads(o_ref, group, quad * QUAD, half).astype(F32)
            high = product.astype(BF16)
            low = (product - high.astype(F32)).astype(BF16)
            delta = (dot_nt(ones, high) + dot_nt(ones, low))[0:1]
            both = dot_nt(left, qg_ref[group * TILES + tile])
            return both[:rows], both[rows:], delta

        def finish(tile, scores, dprob, delta):
            at = tile_columns(tile)
            scores = scores + bias[tile // 2]
            largest = jnp.max(scores, axis=0, keepdims=True)
            prob = jnp.exp2((scores - largest) * EXP2_SCALE)
            prob_ref[group, :, at] = prob.astype(BF16)
            ds_ref[group, :, at] = (prob * (dprob - delta)).astype(BF16)
            stat_ref[group, 0:1, at] = largest
            stat_ref[group, 1:2, at] = jnp.sum(prob, axis=0, keepdims=True)
            stat_ref[group, 2:3, at] = delta

        ahead = products(0)
        for tile in range(TILES):
            now = ahead
            if tile + 1 < TILES:
                ahead = products(tile + 1)
            finish(tile, *now)


def reach_bias(notes_ref, distance, rows):
    key_idx = lax.broadcasted_iota(jnp.int32, (rows, notes_ref.shape[1]), 0).astype(F32) - distance * rows
    listed = notes_ref[distance + 1 : distance + 2, 0:1]
    return jnp.where((key_idx >= notes_ref[0:1, 0:1]) & (listed > 0.0), 0.0, NEG_LARGE)


def reached(notes_ref):
    return [notes_ref[half : half + 1, :] == notes_ref[0:1, 0:1] for half in range(2)]


def high_reached(notes_ref):
    return jnp.max(jnp.where(notes_ref[1:2, :] == notes_ref[0:1, 0:1], 1.0, 0.0)) > 0.0


def goes_on(notes_ref):
    return jnp.max(notes_ref[3:4, :]) > 0.0


def softmax_step(scores, stat_ref, group, at, in_reach):
    before = stat_ref[group, 0:1, at]
    largest = jnp.maximum(before, jnp.max(scores, axis=0, keepdims=True))
    prob = jnp.exp2((scores - jnp.where(in_reach, largest, -NEG_LARGE)) * EXP2_SCALE)
    largest = jnp.where(in_reach, largest, before)
    scale = jnp.exp2((before - largest) * EXP2_SCALE)
    total = stat_ref[group, 1:2, at] * scale + jnp.sum(prob, axis=0, keepdims=True)
    return prob, largest, total, scale


def staged(tiles, products, middle, finish):
    ahead = products(0)
    behind = None
    for tile in range(tiles):
        now = ahead
        if tile + 1 < tiles:
            ahead = products(tile + 1)
        done = middle(tile, *now)
        if behind is not None:
            finish(tile - 1, behind)
        behind = done
    finish(tiles - 1, behind)


def store_query_grad(dq_ref, group, tile, dq, half_ref):
    half, quad = divmod(tile, 2)
    rows = dq_ref.shape[1] // 2
    cos_t, sin_t = half_ref[half, 0], half_ref[half, 1]
    upper, lower = dq[:HALF], dq[HALF:]
    dq = jnp.concatenate([upper * cos_t + lower * sin_t, lower * cos_t - upper * sin_t], axis=0).astype(BF16)
    dq = dq.T
    for i in range(QUAD):
        head = group * RATIO + quad * QUAD + i
        dq_ref[0, half * rows : (half + 1) * rows, head_columns(head)] = dq[i * rows : (i + 1) * rows]


def own_alone(dq_ref, scale_ref, own_ref, ds0_ref, kt0_ref, stat_ref, half_ref, group, tiles):
    for tile in tiles:
        at = tile_columns(tile)
        scale = 1.0 / stat_ref[group, 1:2, at]
        scale_ref[group, 0:1, at] = scale
        dscore = ds0_ref[group, :, at] * scale.astype(BF16)
        own_ref[group, :, at] = dscore
        store_query_grad(dq_ref, group, tile, dot_nn(kt0_ref[group], dscore), half_ref)


def key_products(qg_ref, group, tiles, dscore, prob):
    dk = dot_nn(dscore, group_rows(qg_ref, group, slice(HD), tiles)) * SCORE_SCALE
    dv = dot_nn(prob, group_rows(qg_ref, group, slice(HD, 2 * HD), tiles))
    return dk.astype(BF16), dv.astype(BF16)


def near_kernel(
    notes_ref, qg_ref, kv_ref, ds0_ref, kt0_ref, stat_ref, half_ref, cos_ref, sin_ref,
    dq_ref, ret2_ref, ret1_ref, scale_ref, own_ref, prob_ref, ds_ref, kt_ref, next_ref,
):
    rows = kv_ref.shape[2]

    def attend(last, tiles):
        in_reach = reached(notes_ref)
        bias = reach_bias(notes_ref, 1, rows)
        for group in range(HK):
            one_group(last, tiles, in_reach, bias, group)

    def one_group(last, tiles, in_reach, bias, group):
        k_rot = rotate(kv_ref[0, group].astype(F32), cos_ref[...], sin_ref[...])
        k_rot_t = k_rot.T.astype(BF16)
        left = block_diagonal(k_rot.astype(BF16), kv_ref[1, group])
        both_t = jnp.concatenate([k_rot_t, kt0_ref[group]], axis=1)

        def products(tile):
            both = dot_nt(left, qg_ref[group * TILES + tile])
            return both[:rows], both[rows:]

        def middle(tile, scores, dprob):
            at = tile_columns(tile)
            prob, largest, total, scale = softmax_step(scores + bias, stat_ref, group, at, in_reach[tile // 2])
            delta = stat_ref[group, 2:3, at]
            if last:
                inverse = 1.0 / total
                scale = scale * inverse
                prob = prob * inverse
                scale_ref[group, 0:1, at] = scale
            prob = prob.astype(BF16)
            dscore = prob * (dprob - delta).astype(BF16)
            prob_ref[group, :, at] = prob
            ds_ref[group, :, at] = dscore
            if last:
                own_dscore = ds0_ref[group, :, at] * scale.astype(BF16)
                own_ref[group, :, at] = own_dscore
                return jnp.concatenate([dscore, own_dscore], axis=0)
            next_ref[group, 0:1, at] = largest
            next_ref[group, 1:2, at] = total
            next_ref[group, 2:3, at] = delta
            next_ref[group, 3:4, at] = scale
            return None

        def finish(tile, dscore):
            if last:
                store_query_grad(dq_ref, group, tile, dot_nn(both_t, dscore), half_ref)

        staged(tiles, products, middle, finish)
        if last:
            own_alone(
                dq_ref, scale_ref, own_ref, ds0_ref, kt0_ref, stat_ref, half_ref, group, range(tiles, TILES)
            )
            used = slice(0, tile_columns(tiles - 1).stop)
            grads = key_products(qg_ref, group, tiles, ds_ref[group, :, used], prob_ref[group, :, used])
            for which, grad in enumerate(grads):
                ret1_ref[which, group] = grad
                ret2_ref[which, group] = jnp.zeros((rows, HD), BF16)
        else:
            kt_ref[group] = k_rot_t
            for tile in range(tiles, TILES):
                next_ref[group, 1:2, tile_columns(tile)] = stat_ref[group, 1:2, tile_columns(tile)]

    further, wide = goes_on(notes_ref), high_reached(notes_ref)
    for last in (True, False):
        for tiles in (TILES // 2, TILES):
            chosen = (further != last) & (wide == (tiles == TILES))
            pl.when(chosen)(lambda last=last, tiles=tiles: attend(last, tiles))


def far_kernel(
    notes_ref, qg_ref, kv_ref, ds0_ref, kt0_ref, half_ref, cos_ref, sin_ref,
    prob1_ref, ds1_ref, kt1_ref, stat_ref, *refs,
):
    dq_ref, ret2_ref, ret1_ref, scale_ref, own_ref, prob_buf, ds_buf = refs[5:]
    rows = kv_ref.shape[2]

    def attend(skipped, tiles):
        in_reach = reached(notes_ref)
        bias = reach_bias(notes_ref, 2, rows)[skipped:]
        for group in range(HK):
            one_group(skipped, tiles, in_reach, bias, group)

    def one_group(skipped, tiles, in_reach, bias, group):
        used = rows - skipped
        k_rot = rotate(kv_ref[0, group, skipped:, :].astype(F32), cos_ref[skipped:, :], sin_ref[skipped:, :])
        left = block_diagonal(k_rot.astype(BF16), kv_ref[1, group, skipped:, :])
        k_rot_t = k_rot.T.astype(BF16)
        near_t = jnp.concatenate([kt1_ref[group], kt0_ref[group]], axis=1)

        def products(tile):
            both = dot_nt(left, qg_ref[group * TILES + tile])
            return both[:used], both[used:]

        def middle(tile, scores, dprob):
            at = tile_columns(tile)
            prob, _, total, scale = softmax_step(scores + bias, stat_ref, group, at, in_reach[tile // 2])
            inverse = 1.0 / total
            near_scale = scale * inverse
            own_scale = near_scale * stat_ref[group, 3:4, at]
            scale_ref[group, 0:1, at] = own_scale
            prob = (prob * inverse).astype(BF16)
            dscore = prob * (dprob - stat_ref[group, 2:3, at]).astype(BF16)
            near_scale = near_scale.astype(BF16)
            near_dscore = ds1_ref[group, :, at] * near_scale
            own_dscore = ds0_ref[group, :, at] * own_scale.astype(BF16)
            own_ref[group, :, at] = own_dscore
            prob_buf[:used, at] = prob
            prob_buf[used : used + rows, at] = prob1_ref[group, :, at] * near_scale
            ds_buf[:used, at] = dscore
            ds_buf[used : used + rows, at] = near_dscore
            return dscore, jnp.concatenate([near_dscore, own_dscore], axis=0)

        def finish(tile, dscores):
            dq = dot_nn(near_t, dscores[1]) + dot_nn(k_rot_t, dscores[0])
            store_query_grad(dq_ref, group, tile, dq, half_ref)

        staged(tiles, products, middle, finish)
        own_alone(
            dq_ref, scale_ref, own_ref, ds0_ref, kt0_ref, stat_ref, half_ref, group, range(tiles, TILES)
        )
        columns = slice(0, tile_columns(tiles - 1).stop)
        grads = key_products(qg_ref, group, tiles, ds_buf[: used + rows, columns], prob_buf[: used + rows, columns])
        for which, grad in enumerate(grads):
            ret1_ref[which, group] = grad[used:]
            ret2_ref[which, group, skipped:, :] = grad[:used]
            if skipped:
                ret2_ref[which, group, :skipped, :] = jnp.zeros((skipped, HD), BF16)

    @pl.when(goes_on(notes_ref))
    def _():
        wide = high_reached(notes_ref)
        pl.when(wide)(lambda: attend(rows // 2, TILES))
        pl.when(jnp.logical_not(wide))(lambda: attend(0, TILES // 2))


def own_kv_kernel(qg_ref, prob_ref, ds_ref, scale_ref, dk_ref, dv_ref):
    @pl.loop(0, HK)
    def _(group):
        prob = (prob_ref[group].astype(F32) * scale_ref[group, 0:1, :]).astype(BF16)
        dk_ref[group] = dot_nn(ds_ref[group], group_rows(qg_ref, group, slice(HD))) * SCORE_SCALE
        dv_ref[group] = dot_nn(prob, group_rows(qg_ref, group, slice(HD, 2 * HD)))


def sum_kernel(
    dk_ref, dv_ref, ret2_ref, ret1_ref, cos_ref, sin_ref, dq_ref, key_hbm, value_hbm, handed_hbm, key_buf, value_buf, copied
):
    rows = dq_ref.shape[1]
    half = rows // 2
    copies = [
        pltpu.make_async_copy(dq_ref.at[:, pl.ds(i * half, half)], handed_hbm.at[:, pl.ds(i * half, half)], copied.at[i])
        for i in range(2)
    ]
    for copy in copies:
        copy.start()
    for group in range(HK):
        at = head_columns(group)
        dv = dv_ref[group] + ret1_ref[1, group].astype(F32) + ret2_ref[1, group].astype(F32)
        value_buf[0, :, at] = dv.astype(BF16)
    copies.append(pltpu.make_async_copy(value_buf, value_hbm, copied.at[2]))
    copies[-1].start()
    for group in range(HK):
        at = head_columns(group)
        dk = dk_ref[group] + ret1_ref[0, group].astype(F32) + ret2_ref[0, group].astype(F32)
        key_buf[0, :, at] = unrotate(dk, cos_ref[...], sin_ref[...]).astype(BF16)
    copies.append(pltpu.make_async_copy(key_buf, key_hbm, copied.at[3]))
    copies[-1].start()
    for copy in copies:
        copy.wait()


def cost(flops, moved, exps=0):
    return pl.CostEstimate(flops=int(flops), bytes_accessed=int(moved), transcendentals=int(exps))


def shards(query_heads, key_heads, value_heads, attn_output, output_grad, doc_start, fetch_list):
    rows = query_heads.shape[1]
    wide = RATIO * HD
    kv_width = HK * HD
    first_row = (lax.axis_index("ctx") * rows).astype(jnp.int32).reshape(1)
    doc_row = doc_start.reshape(1, rows)
    smem = pl.BlockSpec(memory_space=pltpu.SMEM)
    vmem = pl.BlockSpec(memory_space=pltpu.VMEM)
    hbm = pl.BlockSpec(memory_space=pltpu.HBM)
    params = pltpu.CompilerParams(vmem_limit_bytes=40 * 1024 * 1024)
    shape = jax.ShapeDtypeStruct
    block_flops = 2 * HQ * rows * rows * HD
    arguments = [
        pltpu.with_memory_space_constraint(x[0], pltpu.HBM)
        for x in (query_heads, key_heads, value_heads, attn_output, output_grad)
    ]

    kv = pl.pallas_call(
        pack_kernel,
        in_specs=[hbm, hbm],
        out_specs=vmem,
        out_shape=shape((2, HK, rows, HD), BF16),
        scratch_shapes=[pltpu.SemaphoreType.DMA((2, HK))],
        compiler_params=params,
        cost_estimate=cost(0, 2**19),
        name="pack_keys",
    )(arguments[1], arguments[2])
    kv2 = from_behind(kv, "ctx", 2)
    kv1 = from_behind(kv, "ctx", 1)

    notes, qg, prob0, ds0, k_own_t, stat, half, cos, sin, cos1, sin1, cos2, sin2 = pl.pallas_call(
        own_kernel,
        in_specs=[smem, vmem, vmem] + [hbm] * 5,
        out_specs=[vmem] * 13,
        out_shape=[
            shape((8, QUAD * rows // 2), F32),
            shape((HK * TILES, QUAD * rows // 2, 2 * HD), BF16),
            shape((HK, rows, RATIO * rows), BF16),
            shape((HK, rows, RATIO * rows), BF16),
            shape((HK, HD, rows), BF16),
            shape((HK, 8, RATIO * rows), F32),
            shape((2, 2, HALF, QUAD * rows // 2), F32),
            shape((rows, HD), F32),
            shape((rows, HD), F32),
            shape((rows, HD), F32),
            shape((rows, HD), F32),
            shape((rows, HD), F32),
            shape((rows, HD), F32),
        ],
        scratch_shapes=[
            pltpu.VMEM((HK, rows, wide), BF16),
            pltpu.VMEM((HK, rows, HD), BF16),
            pltpu.VMEM((HK, rows, HD), BF16),
            pltpu.VMEM((HK, rows, wide), BF16),
            pltpu.VMEM((HK, rows, wide), BF16),
            pltpu.SemaphoreType.DMA((5, HK)),
        ],
        compiler_params=params,
        cost_estimate=cost(3 * block_flops, 9 * 2**20, HQ * rows * rows),
        name="own_block",
    )(first_row, *(pltpu.with_memory_space_constraint(x, pltpu.HBM) for x in (fetch_list, doc_row)), *arguments)

    results = [
        shape((1, rows, HQ * HD), BF16),
        shape((2, HK, rows, HD), BF16),
        shape((2, HK, rows, HD), BF16),
        shape((HK, 8, RATIO * rows), F32),
        shape((HK, rows, RATIO * rows), BF16),
    ]
    *settled, prob1, ds1, k_near_t, stat1 = pl.pallas_call(
        near_kernel,
        in_specs=[vmem] * 9,
        out_specs=[vmem] * 9,
        out_shape=results
        + [
            shape((HK, rows, RATIO * rows), BF16),
            shape((HK, rows, RATIO * rows), BF16),
            shape((HK, HD, rows), BF16),
            shape((HK, 8, RATIO * rows), F32),
        ],
        compiler_params=params,
        cost_estimate=cost(5 * block_flops, 9 * 2**20, HQ * rows * rows),
        name="near_block",
    )(notes, qg, kv1, ds0, k_own_t, stat, half, cos1, sin1)

    dq, ret2, ret1, scale, ds_own = pl.pallas_call(
        far_kernel,
        in_specs=[vmem] * 17,
        out_specs=[vmem] * 5,
        out_shape=results,
        scratch_shapes=[
            pltpu.VMEM((FETCH * rows, RATIO * rows), BF16),
            pltpu.VMEM((FETCH * rows, RATIO * rows), BF16),
        ],
        input_output_aliases={12 + i: i for i in range(5)},
        compiler_params=params,
        cost_estimate=cost(5 * block_flops, 9 * 2**20, HQ * rows * rows),
        name="far_block",
    )(notes, qg, kv2, ds0, k_own_t, half, cos2, sin2, prob1, ds1, k_near_t, stat1, *settled)
    arrived1 = from_behind(ret1, "ctx", -1)
    arrived2 = from_behind(ret2, "ctx", -2)
    dq_next = from_behind(dq, "section", -1)

    dk0, dv0 = pl.pallas_call(
        own_kv_kernel,
        in_specs=[vmem] * 4,
        out_specs=[vmem] * 2,
        out_shape=[shape((HK, rows, HD), F32), shape((HK, rows, HD), F32)],
        compiler_params=params,
        cost_estimate=cost(2 * block_flops, 5 * 2**20),
        name="own_keys",
    )(qg, prob0, ds_own, scale)

    key_grad, value_grad, handed_grad = pl.pallas_call(
        sum_kernel,
        in_specs=[vmem] * 6 + [pl.BlockSpec(memory_space=pl.ANY)],
        out_specs=[hbm] * 3,
        out_shape=[
            shape((1, rows, kv_width), BF16),
            shape((1, rows, kv_width), BF16),
            shape((1, rows, HQ * HD), BF16),
        ],
        scratch_shapes=[
            pltpu.VMEM((1, rows, kv_width), BF16),
            pltpu.VMEM((1, rows, kv_width), BF16),
            pltpu.SemaphoreType.DMA((4,)),
        ],
        compiler_params=params,
        cost_estimate=cost(0, 3 * 2**20),
        name="sum_keys",
    )(dk0, dv0, arrived2, arrived1, cos, sin, dq_next)
    return (handed_grad, key_grad, value_grad)


def solution(mesh):
    return jax.shard_map(
        shards,
        mesh=mesh,
        in_specs=(
            P("section", "ctx", None),
            P("section", "ctx", None),
            P("section", "ctx", None),
            P("section", "ctx", None),
            P("section", "ctx", None),
            P("ctx"),
            P("ctx", None),
        ),
        out_specs=(P("section", "ctx", None), P("section", "ctx", None), P("section", "ctx", None)),
        check_vma=False,
    )
```

```python
import math

import jax
import jax.numpy as jnp
from jax import lax
from jax.experimental import pallas as pl
from jax.experimental.pallas import tpu as pltpu
from jax.sharding import PartitionSpec as P

HQ = 32
HK = 4
HD = 128
RATIO = HQ // HK
HALF = HD // 2
FETCH = 2
QUAD = 4
TILES = 4

ROPE_BASE = 1000000.0
TRAINED_CONTEXT = 32768.0
YARN_FACTOR = 4.0
NEG_LARGE = -1e30
SCORE_SCALE = HD ** (-0.5)
EXP2_SCALE = SCORE_SCALE / math.log(2.0)

F32 = jnp.float32
BF16 = jnp.bfloat16


def from_behind(value, axis, steps):
    count = lax.axis_size(axis)
    initial, last = (max(0, -steps), min(count, count - steps))
    return lax.ppermute(value, axis, [(source, source + steps) for source in range(initial, last)])


def dot_nn(left, right):
    return lax.dot_general(left, right, (((1,), (0,)), ((), ())), preferred_element_type=F32)


def dot_nt(left, right):
    return lax.dot_general(left, right, (((1,), (1,)), ((), ())), preferred_element_type=F32)


def frequencies(rows, columns):
    def correction(rotations):
        return HD * math.log(TRAINED_CONTEXT / (rotations * 2.0 * math.pi)) / (2.0 * math.log(ROPE_BASE))

    lower_dim = max(math.floor(correction(32.0)), 0)
    upper_dim = min(math.ceil(correction(1.0)), HD - 1)
    spread_dims = max(upper_dim - lower_dim, 0.001)
    indices = lax.broadcasted_iota(jnp.int32, (rows, columns), 0).astype(F32)
    extrapolated = jnp.exp(indices * F32(-2.0 / HD * math.log(ROPE_BASE)))
    ramp_weight = jnp.clip((indices - lower_dim) / spread_dims, 0.0, 1.0)
    return extrapolated / YARN_FACTOR * ramp_weight + extrapolated * (1.0 - ramp_weight)


def half_tables(positions):
    factor = 0.1 * math.log(YARN_FACTOR) + 1.0
    angles = frequencies(HALF, positions.shape[1]) * positions.astype(F32)
    return jnp.cos(angles) * factor, jnp.sin(angles) * factor


def upright(cos_t, sin_t):
    cosine = jnp.concatenate([cos_t, cos_t], axis=0).T
    signed_sine = jnp.concatenate([sin_t, -sin_t], axis=0).T
    return cosine, signed_sine


def rotate(values, cosine, signed_sine):
    return values * cosine - pltpu.roll(values, HALF, 1) * signed_sine


def unrotate(values, cosine, signed_sine):
    return values * cosine + pltpu.roll(values, HALF, 1) * signed_sine


def head_columns(head):
    return slice(head * HD, (head + 1) * HD)


def stack_heads(ref, group, first, half):
    rows = ref.shape[1] // 2
    at = slice(half * rows, (half + 1) * rows)
    return jnp.concatenate([ref[group, at, head_columns(first + i)] for i in range(QUAD)], axis=0)


def four_times(value, half):
    columns = value.shape[1] // 2
    return jnp.concatenate([value[:, half * columns : (half + 1) * columns]] * QUAD, axis=1)


def block_diagonal(upper, lower):
    zero = jnp.zeros_like(upper)
    return jnp.concatenate(
        [jnp.concatenate([upper, zero], axis=1), jnp.concatenate([zero, lower], axis=1)], axis=0
    )


def group_rows(ref, group, columns, tiles=TILES):
    return jnp.concatenate([ref[group * TILES + i, :, columns] for i in range(tiles)], axis=0)


def tile_columns(tile):
    width = RATIO * HD // TILES
    return slice(tile * width, (tile + 1) * width)


def pack_kernel(k_hbm, v_hbm, kv_ref, arrived):
    copies = [
        pltpu.make_async_copy(source, kv_ref.at[which], arrived.at[which])
        for which, source in enumerate((k_hbm, v_hbm))
    ]
    for copy in copies:
        copy.start()
    for copy in copies:
        copy.wait()


def own_kernel(
    first_ref, list_ref, doc_ref, q_hbm, k_hbm, v_hbm, o_hbm, g_hbm,
    notes_ref, qg_ref, prob_ref, ds_ref, kt_ref, stat_ref, half_ref, cos_ref, sin_ref, cos1_ref, sin1_ref, cos2_ref, sin2_ref,
    q_ref, k_ref, v_ref, o_ref, g_ref, arrived,
):
    rows = q_hbm.shape[0]
    arguments = ((k_hbm, k_ref), (q_hbm, q_ref), (v_hbm, v_ref), (g_hbm, g_ref), (o_hbm, o_ref))

    def fetch(which, group):
        source, buffer = arguments[which]
        width = buffer.shape[2]
        columns = pl.ds(pl.multiple_of(group * width, width), width)
        return pltpu.make_async_copy(source.at[:, columns], buffer.at[group], arrived.at[which, group])

    for group in range(HK):
        for which in range(len(arguments)):
            fetch(which, group).start()

    doc_row = doc_ref[...] - first_ref[0]
    columns = lax.broadcasted_iota(jnp.int32, (1, rows), 1)
    cos_t, sin_t = half_tables(columns - doc_row)
    cos_ref[...], sin_ref[...] = upright(cos_t, sin_t)
    reach = doc_row[:, 0:1]
    lanes = notes_ref.shape[1]
    for half in range(2):
        notes_ref[half : half + 1, :] = four_times(doc_row.astype(F32), half)
        half_ref[half, 0] = four_times(cos_t * SCORE_SCALE, half)
        half_ref[half, 1] = four_times(sin_t * SCORE_SCALE, half)
    for distance in range(1, FETCH + 1):
        listed = jnp.where(list_ref[:, distance - 1 : distance] == 1, 1.0, 0.0)
        notes_ref[distance + 1 : distance + 2, :] = jnp.broadcast_to(listed, (1, lanes))
    cos1_ref[...], sin1_ref[...] = upright(*half_tables(columns - rows - reach))
    cos2_ref[...], sin2_ref[...] = upright(*half_tables(columns - 2 * rows - reach))
    key_idx = lax.broadcasted_iota(jnp.int32, (rows, rows), 0)
    query_idx = lax.broadcasted_iota(jnp.int32, (rows, rows), 1)
    mask = (key_idx <= query_idx) & (key_idx >= doc_row)
    bias = jnp.where(mask, 0.0, NEG_LARGE)
    bias = [four_times(bias, half) for half in range(2)]
    ones = jnp.ones((8, HD), BF16)

    @pl.loop(0, HK)
    def _(group):
        for which in range(len(arguments)):
            fetch(which, group).wait()
        k_rot = rotate(k_ref[group].astype(F32), cos_ref[...], sin_ref[...])
        kt_ref[group] = k_rot.T.astype(BF16)
        left = block_diagonal(k_rot.astype(BF16), v_ref[group])

        def products(tile):
            half, quad = divmod(tile, 2)
            at = slice(half * rows // 2, (half + 1) * rows // 2)
            cosine = jnp.concatenate([cos_ref[at, :]] * QUAD, axis=0)
            signed_sine = jnp.concatenate([sin_ref[at, :]] * QUAD, axis=0)
            queries = stack_heads(q_ref, group, quad * QUAD, half).astype(F32)
            qg_ref[group * TILES + tile, :, :HD] = rotate(queries, cosine, signed_sine).astype(BF16)
            grads = stack_heads(g_ref, group, quad * QUAD, half)
            qg_ref[group * TILES + tile, :, HD:] = grads
            product = grads.astype(F32) * stack_heads(o_ref, group, quad * QUAD, half).astype(F32)
            high = product.astype(BF16)
            low = (product - high.astype(F32)).astype(BF16)
            delta = (dot_nt(ones, high) + dot_nt(ones, low))[0:1]
            both = dot_nt(left, qg_ref[group * TILES + tile])
            return both[:rows], both[rows:], delta

        def finish(tile, scores, dprob, delta):
            at = tile_columns(tile)
            scores = scores + bias[tile // 2]
            largest = jnp.max(scores, axis=0, keepdims=True)
            prob = jnp.exp2((scores - largest) * EXP2_SCALE)
            prob_ref[group, :, at] = prob.astype(BF16)
            ds_ref[group, :, at] = (prob * (dprob - delta)).astype(BF16)
            stat_ref[group, 0:1, at] = largest
            stat_ref[group, 1:2, at] = jnp.sum(prob, axis=0, keepdims=True)
            stat_ref[group, 2:3, at] = delta

        ahead = products(0)
        for tile in range(TILES):
            now = ahead
            if tile + 1 < TILES:
                ahead = products(tile + 1)
            finish(tile, *now)


def reach_bias(notes_ref, distance, rows):
    key_idx = lax.broadcasted_iota(jnp.int32, (rows, notes_ref.shape[1]), 0).astype(F32) - distance * rows
    listed = notes_ref[distance + 1 : distance + 2, 0:1]
    return jnp.where((key_idx >= notes_ref[0:1, 0:1]) & (listed > 0.0), 0.0, NEG_LARGE)


def reached(notes_ref):
    return [notes_ref[half : half + 1, :] == notes_ref[0:1, 0:1] for half in range(2)]


def high_reached(notes_ref):
    return jnp.max(jnp.where(notes_ref[1:2, :] == notes_ref[0:1, 0:1], 1.0, 0.0)) > 0.0


def goes_on(notes_ref):
    return jnp.max(notes_ref[3:4, :]) > 0.0


def softmax_step(scores, stat_ref, group, at, in_reach):
    before = stat_ref[group, 0:1, at]
    largest = jnp.maximum(before, jnp.max(scores, axis=0, keepdims=True))
    prob = jnp.exp2((scores - jnp.where(in_reach, largest, -NEG_LARGE)) * EXP2_SCALE)
    largest = jnp.where(in_reach, largest, before)
    scale = jnp.exp2((before - largest) * EXP2_SCALE)
    total = stat_ref[group, 1:2, at] * scale + jnp.sum(prob, axis=0, keepdims=True)
    return prob, largest, total, scale


def staged(tiles, products, middle, finish):
    ahead = products(0)
    behind = None
    for tile in range(tiles):
        now = ahead
        if tile + 1 < tiles:
            ahead = products(tile + 1)
        done = middle(tile, *now)
        if behind is not None:
            finish(tile - 1, behind)
        behind = done
    finish(tiles - 1, behind)


def store_query_grad(dq_ref, group, tile, dq, half_ref):
    half, quad = divmod(tile, 2)
    rows = dq_ref.shape[1] // 2
    cos_t, sin_t = half_ref[half, 0], half_ref[half, 1]
    upper, lower = dq[:HALF], dq[HALF:]
    dq = jnp.concatenate([upper * cos_t + lower * sin_t, lower * cos_t - upper * sin_t], axis=0).astype(BF16)
    dq = dq.T
    for i in range(QUAD):
        head = group * RATIO + quad * QUAD + i
        dq_ref[0, half * rows : (half + 1) * rows, head_columns(head)] = dq[i * rows : (i + 1) * rows]


def own_alone(dq_ref, scale_ref, own_ref, ds0_ref, kt0_ref, stat_ref, half_ref, group, tiles):
    for tile in tiles:
        at = tile_columns(tile)
        scale = 1.0 / stat_ref[group, 1:2, at]
        scale_ref[group, 0:1, at] = scale
        dscore = ds0_ref[group, :, at] * scale.astype(BF16)
        own_ref[group, :, at] = dscore
        store_query_grad(dq_ref, group, tile, dot_nn(kt0_ref[group], dscore), half_ref)


def key_products(qg_ref, group, tiles, dscore, prob):
    dk = dot_nn(dscore, group_rows(qg_ref, group, slice(HD), tiles)) * SCORE_SCALE
    dv = dot_nn(prob, group_rows(qg_ref, group, slice(HD, 2 * HD), tiles))
    return dk.astype(BF16), dv.astype(BF16)


def near_kernel(
    notes_ref, qg_ref, kv_ref, ds0_ref, kt0_ref, stat_ref, half_ref, cos_ref, sin_ref,
    dq_ref, ret2_ref, ret1_ref, scale_ref, own_ref, prob_ref, ds_ref, kt_ref, next_ref,
):
    rows = kv_ref.shape[1]

    def attend(last, tiles):
        in_reach = reached(notes_ref)
        bias = reach_bias(notes_ref, 1, rows)
        for group in range(HK):
            one_group(last, tiles, in_reach, bias, group)

    def one_group(last, tiles, in_reach, bias, group):
        k_rot = rotate(kv_ref[0, :, head_columns(group)].astype(F32), cos_ref[...], sin_ref[...])
        k_rot_t = k_rot.T.astype(BF16)
        left = block_diagonal(k_rot.astype(BF16), kv_ref[1, :, head_columns(group)])
        both_t = jnp.concatenate([k_rot_t, kt0_ref[group]], axis=1)

        def products(tile):
            both = dot_nt(left, qg_ref[group * TILES + tile])
            return both[:rows], both[rows:]

        def middle(tile, scores, dprob):
            at = tile_columns(tile)
            prob, largest, total, scale = softmax_step(scores + bias, stat_ref, group, at, in_reach[tile // 2])
            delta = stat_ref[group, 2:3, at]
            if last:
                inverse = 1.0 / total
                scale = scale * inverse
                prob = prob * inverse
                scale_ref[group, 0:1, at] = scale
            prob = prob.astype(BF16)
            dscore = prob * (dprob - delta).astype(BF16)
            prob_ref[group, :, at] = prob
            ds_ref[group, :, at] = dscore
            if last:
                own_dscore = ds0_ref[group, :, at] * scale.astype(BF16)
                own_ref[group, :, at] = own_dscore
                return jnp.concatenate([dscore, own_dscore], axis=0)
            next_ref[group, 0:1, at] = largest
            next_ref[group, 1:2, at] = total
            next_ref[group, 2:3, at] = delta
            next_ref[group, 3:4, at] = scale
            return None

        def finish(tile, dscore):
            if last:
                store_query_grad(dq_ref, group, tile, dot_nn(both_t, dscore), half_ref)

        staged(tiles, products, middle, finish)
        if last:
            own_alone(
                dq_ref, scale_ref, own_ref, ds0_ref, kt0_ref, stat_ref, half_ref, group, range(tiles, TILES)
            )
            used = slice(0, tile_columns(tiles - 1).stop)
            grads = key_products(qg_ref, group, tiles, ds_ref[group, :, used], prob_ref[group, :, used])
            for which, grad in enumerate(grads):
                ret1_ref[which, group] = grad
                ret2_ref[which, group] = jnp.zeros((rows, HD), BF16)
        else:
            kt_ref[group] = k_rot_t
            for tile in range(tiles, TILES):
                next_ref[group, 1:2, tile_columns(tile)] = stat_ref[group, 1:2, tile_columns(tile)]

    further, wide = goes_on(notes_ref), high_reached(notes_ref)
    for last in (True, False):
        for tiles in (TILES // 2, TILES):
            chosen = (further != last) & (wide == (tiles == TILES))
            pl.when(chosen)(lambda last=last, tiles=tiles: attend(last, tiles))


def far_kernel(
    notes_ref, qg_ref, kv_ref, ds0_ref, kt0_ref, half_ref, cos_ref, sin_ref,
    prob1_ref, ds1_ref, kt1_ref, stat_ref, *refs,
):
    dq_ref, scale_ref, own_ref, prob_ref, ds_ref = refs[3:]
    rows = kv_ref.shape[1]

    def attend(skipped, tiles):
        in_reach = reached(notes_ref)
        bias = reach_bias(notes_ref, 2, rows)[skipped:]
        for group in range(HK):
            one_group(skipped, tiles, in_reach, bias, group)

    def one_group(skipped, tiles, in_reach, bias, group):
        used = rows - skipped
        k_rot = rotate(kv_ref[0, skipped:, head_columns(group)].astype(F32), cos_ref[skipped:, :], sin_ref[skipped:, :])
        left = block_diagonal(k_rot.astype(BF16), kv_ref[1, skipped:, head_columns(group)])
        k_rot_t = k_rot.T.astype(BF16)
        near_t = jnp.concatenate([kt1_ref[group], kt0_ref[group]], axis=1)

        def products(tile):
            both = dot_nt(left, qg_ref[group * TILES + tile])
            return both[:used], both[used:]

        def middle(tile, scores, dprob):
            at = tile_columns(tile)
            prob, _, total, scale = softmax_step(scores + bias, stat_ref, group, at, in_reach[tile // 2])
            inverse = 1.0 / total
            near_scale = scale * inverse
            own_scale = near_scale * stat_ref[group, 3:4, at]
            scale_ref[group, 0:1, at] = own_scale
            prob = (prob * inverse).astype(BF16)
            dscore = prob * (dprob - stat_ref[group, 2:3, at]).astype(BF16)
            near_scale = near_scale.astype(BF16)
            near_dscore = ds1_ref[group, :, at] * near_scale
            own_dscore = ds0_ref[group, :, at] * own_scale.astype(BF16)
            own_ref[group, :, at] = own_dscore
            prob_ref[group, :used, at] = prob
            prob_ref[group, used : used + rows, at] = prob1_ref[group, :, at] * near_scale
            ds_ref[group, :used, at] = dscore
            ds_ref[group, used : used + rows, at] = near_dscore
            return dscore, jnp.concatenate([near_dscore, own_dscore], axis=0)

        def finish(tile, dscores):
            dq = dot_nn(near_t, dscores[1]) + dot_nn(k_rot_t, dscores[0])
            store_query_grad(dq_ref, group, tile, dq, half_ref)

        staged(tiles, products, middle, finish)
        own_alone(
            dq_ref, scale_ref, own_ref, ds0_ref, kt0_ref, stat_ref, half_ref, group, range(tiles, TILES)
        )

    far_cases(notes_ref, rows, attend)


def far_cases(notes_ref, rows, attend):
    @pl.when(goes_on(notes_ref))
    def _():
        wide = high_reached(notes_ref)
        pl.when(wide)(lambda: attend(rows // 2, TILES))
        pl.when(jnp.logical_not(wide))(lambda: attend(0, TILES // 2))


def far_keys_kernel(notes_ref, qg_ref, prob_ref, ds_ref, *refs):
    ret2_ref, ret1_ref = refs[2:]
    rows = ret1_ref.shape[2]

    def attend(skipped, tiles):
        used = rows - skipped
        columns = slice(0, tile_columns(tiles - 1).stop)
        for group in range(HK):
            grads = key_products(
                qg_ref, group, tiles, ds_ref[group, : used + rows, columns], prob_ref[group, : used + rows, columns]
            )
            for which, grad in enumerate(grads):
                ret1_ref[which, group] = grad[used:]
                ret2_ref[which, group, skipped:, :] = grad[:used]
                if skipped:
                    ret2_ref[which, group, :skipped, :] = jnp.zeros((skipped, HD), BF16)

    far_cases(notes_ref, rows, attend)


def own_kv_kernel(qg_ref, prob_ref, ds_ref, scale_ref, dk_ref, dv_ref):
    @pl.loop(0, HK)
    def _(group):
        prob = (prob_ref[group].astype(F32) * scale_ref[group, 0:1, :]).astype(BF16)
        dk_ref[group] = dot_nn(ds_ref[group], group_rows(qg_ref, group, slice(HD))) * SCORE_SCALE
        dv_ref[group] = dot_nn(prob, group_rows(qg_ref, group, slice(HD, 2 * HD)))


def sum_kernel(
    dk_ref, dv_ref, ret2_ref, ret1_ref, cos_ref, sin_ref, dq_ref, key_hbm, value_hbm, handed_hbm, key_buf, value_buf, copied
):
    rows = dq_ref.shape[1]
    half = rows // 2
    copies = [
        pltpu.make_async_copy(dq_ref.at[:, pl.ds(i * half, half)], handed_hbm.at[:, pl.ds(i * half, half)], copied.at[i])
        for i in range(2)
    ]
    for copy in copies:
        copy.start()
    for group in range(HK):
        at = head_columns(group)
        dv = dv_ref[group] + ret1_ref[1, group].astype(F32) + ret2_ref[1, group].astype(F32)
        value_buf[0, :, at] = dv.astype(BF16)
    copies.append(pltpu.make_async_copy(value_buf, value_hbm, copied.at[2]))
    copies[-1].start()
    for group in range(HK):
        at = head_columns(group)
        dk = dk_ref[group] + ret1_ref[0, group].astype(F32) + ret2_ref[0, group].astype(F32)
        key_buf[0, :, at] = unrotate(dk, cos_ref[...], sin_ref[...]).astype(BF16)
    copies.append(pltpu.make_async_copy(key_buf, key_hbm, copied.at[3]))
    copies[-1].start()
    for copy in copies:
        copy.wait()


def cost(flops, moved, exps=0):
    return pl.CostEstimate(flops=int(flops), bytes_accessed=int(moved), transcendentals=int(exps))


def shards(query_heads, key_heads, value_heads, attn_output, output_grad, doc_start, fetch_list):
    rows = query_heads.shape[1]
    wide = RATIO * HD
    kv_width = HK * HD
    first_row = (lax.axis_index("ctx") * rows).astype(jnp.int32).reshape(1)
    doc_row = doc_start.reshape(1, rows)
    smem = pl.BlockSpec(memory_space=pltpu.SMEM)
    vmem = pl.BlockSpec(memory_space=pltpu.VMEM)
    hbm = pl.BlockSpec(memory_space=pltpu.HBM)
    params = pltpu.CompilerParams(vmem_limit_bytes=40 * 1024 * 1024)
    shape = jax.ShapeDtypeStruct
    block_flops = 2 * HQ * rows * rows * HD
    arguments = [
        pltpu.with_memory_space_constraint(x[0], pltpu.HBM)
        for x in (query_heads, key_heads, value_heads, attn_output, output_grad)
    ]

    kv = pl.pallas_call(
        pack_kernel,
        in_specs=[hbm, hbm],
        out_specs=vmem,
        out_shape=shape((2, rows, kv_width), BF16),
        scratch_shapes=[pltpu.SemaphoreType.DMA((2,))],
        compiler_params=params,
        cost_estimate=cost(0, 2**19),
        name="pack_keys",
    )(arguments[1], arguments[2])
    kv2 = from_behind(kv, "ctx", 2)
    kv1 = from_behind(kv, "ctx", 1)

    notes, qg, prob0, ds0, k_own_t, stat, half, cos, sin, cos1, sin1, cos2, sin2 = pl.pallas_call(
        own_kernel,
        in_specs=[smem, vmem, vmem] + [hbm] * 5,
        out_specs=[vmem] * 13,
        out_shape=[
            shape((8, QUAD * rows // 2), F32),
            shape((HK * TILES, QUAD * rows // 2, 2 * HD), BF16),
            shape((HK, rows, RATIO * rows), BF16),
            shape((HK, rows, RATIO * rows), BF16),
            shape((HK, HD, rows), BF16),
            shape((HK, 8, RATIO * rows), F32),
            shape((2, 2, HALF, QUAD * rows // 2), F32),
            shape((rows, HD), F32),
            shape((rows, HD), F32),
            shape((rows, HD), F32),
            shape((rows, HD), F32),
            shape((rows, HD), F32),
            shape((rows, HD), F32),
        ],
        scratch_shapes=[
            pltpu.VMEM((HK, rows, wide), BF16),
            pltpu.VMEM((HK, rows, HD), BF16),
            pltpu.VMEM((HK, rows, HD), BF16),
            pltpu.VMEM((HK, rows, wide), BF16),
            pltpu.VMEM((HK, rows, wide), BF16),
            pltpu.SemaphoreType.DMA((5, HK)),
        ],
        compiler_params=params,
        cost_estimate=cost(3 * block_flops, 9 * 2**20, HQ * rows * rows),
        name="own_block",
    )(first_row, *(pltpu.with_memory_space_constraint(x, pltpu.HBM) for x in (fetch_list, doc_row)), *arguments)

    block = shape((HK, rows, RATIO * rows), BF16)
    both_blocks = shape((HK, FETCH * rows, RATIO * rows), BF16)
    statistics = shape((HK, 8, RATIO * rows), F32)
    query_parts = [shape((1, rows, HQ * HD), BF16), statistics, block]
    returns = [shape((2, HK, rows, HD), BF16)] * 2
    dq, ret2, ret1, scale, ds_own, prob1, ds1, k_near_t, stat1 = pl.pallas_call(
        near_kernel,
        in_specs=[vmem] * 9,
        out_specs=[vmem] * 9,
        out_shape=[query_parts[0], *returns, *query_parts[1:], block, block, shape((HK, HD, rows), BF16), statistics],
        compiler_params=params,
        cost_estimate=cost(5 * block_flops, 9 * 2**20, HQ * rows * rows),
        name="near_block",
    )(notes, qg, kv1, ds0, k_own_t, stat, half, cos1, sin1)

    dq, scale, ds_own, prob12, ds12 = pl.pallas_call(
        far_kernel,
        in_specs=[vmem] * 15,
        out_specs=[vmem] * 5,
        out_shape=[*query_parts, both_blocks, both_blocks],
        input_output_aliases={12: 0, 13: 1, 14: 2},
        compiler_params=params,
        cost_estimate=cost(3 * block_flops, 9 * 2**20, HQ * rows * rows),
        name="far_block",
    )(notes, qg, kv2, ds0, k_own_t, half, cos2, sin2, prob1, ds1, k_near_t, stat1, dq, scale, ds_own)
    handed = from_behind(dq, "section", -1)

    ret2, ret1 = pl.pallas_call(
        far_keys_kernel,
        in_specs=[vmem] * 6,
        out_specs=[vmem] * 2,
        out_shape=returns,
        input_output_aliases={4: 0, 5: 1},
        compiler_params=params,
        cost_estimate=cost(4 * block_flops, 9 * 2**20),
        name="far_keys",
    )(notes, qg, prob12, ds12, ret2, ret1)
    arrived1 = from_behind(ret1, "ctx", -1)
    arrived2 = from_behind(ret2, "ctx", -2)

    dk0, dv0 = pl.pallas_call(
        own_kv_kernel,
        in_specs=[vmem] * 4,
        out_specs=[vmem] * 2,
        out_shape=[shape((HK, rows, HD), F32), shape((HK, rows, HD), F32)],
        compiler_params=params,
        cost_estimate=cost(2 * block_flops, 5 * 2**20),
        name="own_keys",
    )(qg, prob0, ds_own, scale)

    key_grad, value_grad, handed_grad = pl.pallas_call(
        sum_kernel,
        in_specs=[vmem] * 6 + [pl.BlockSpec(memory_space=pl.ANY)],
        out_specs=[hbm] * 3,
        out_shape=[
            shape((1, rows, kv_width), BF16),
            shape((1, rows, kv_width), BF16),
            shape((1, rows, HQ * HD), BF16),
        ],
        scratch_shapes=[
            pltpu.VMEM((1, rows, kv_width), BF16),
            pltpu.VMEM((1, rows, kv_width), BF16),
            pltpu.SemaphoreType.DMA((4,)),
        ],
        compiler_params=params,
        cost_estimate=cost(0, 3 * 2**20),
        name="sum_keys",
    )(dk0, dv0, arrived2, arrived1, cos, sin, handed)
    return (handed_grad, key_grad, value_grad)


def solution(mesh):
    return jax.shard_map(
        shards,
        mesh=mesh,
        in_specs=(
            P("section", "ctx", None),
            P("section", "ctx", None),
            P("section", "ctx", None),
            P("section", "ctx", None),
            P("section", "ctx", None),
            P("ctx"),
            P("ctx", None),
        ),
        out_specs=(P("section", "ctx", None), P("section", "ctx", None), P("section", "ctx", None)),
        check_vma=False,
    )
```

```python
import math

import jax
import jax.numpy as jnp
from jax import lax
from jax.experimental import pallas as pl
from jax.experimental.pallas import tpu as pltpu
from jax.sharding import PartitionSpec as P

HQ = 32
HK = 4
HD = 128
RATIO = HQ // HK
HALF = HD // 2
FETCH = 2
QUAD = 4
EARLY = 3
TILES = 4

ROPE_BASE = 1000000.0
TRAINED_CONTEXT = 32768.0
YARN_FACTOR = 4.0
NEG_LARGE = -1e30
SCORE_SCALE = HD ** (-0.5)
EXP2_SCALE = SCORE_SCALE / math.log(2.0)

F32 = jnp.float32
BF16 = jnp.bfloat16


def from_behind(value, axis, steps):
    count = lax.axis_size(axis)
    initial, last = (max(0, -steps), min(count, count - steps))
    return lax.ppermute(value, axis, [(source, source + steps) for source in range(initial, last)])


def dot_nn(left, right):
    return lax.dot_general(left, right, (((1,), (0,)), ((), ())), preferred_element_type=F32)


def dot_nt(left, right):
    return lax.dot_general(left, right, (((1,), (1,)), ((), ())), preferred_element_type=F32)


def frequencies(rows, columns):
    def correction(rotations):
        return HD * math.log(TRAINED_CONTEXT / (rotations * 2.0 * math.pi)) / (2.0 * math.log(ROPE_BASE))

    lower_dim = max(math.floor(correction(32.0)), 0)
    upper_dim = min(math.ceil(correction(1.0)), HD - 1)
    spread_dims = max(upper_dim - lower_dim, 0.001)
    indices = lax.broadcasted_iota(jnp.int32, (rows, columns), 0).astype(F32)
    extrapolated = jnp.exp(indices * F32(-2.0 / HD * math.log(ROPE_BASE)))
    ramp_weight = jnp.clip((indices - lower_dim) / spread_dims, 0.0, 1.0)
    return extrapolated / YARN_FACTOR * ramp_weight + extrapolated * (1.0 - ramp_weight)


def half_tables(positions):
    factor = 0.1 * math.log(YARN_FACTOR) + 1.0
    angles = frequencies(HALF, positions.shape[1]) * positions.astype(F32)
    return jnp.cos(angles) * factor, jnp.sin(angles) * factor


def upright(cos_t, sin_t):
    cosine = jnp.concatenate([cos_t, cos_t], axis=0).T
    signed_sine = jnp.concatenate([sin_t, -sin_t], axis=0).T
    return cosine, signed_sine


def rotate(values, cosine, signed_sine):
    return values * cosine - pltpu.roll(values, HALF, 1) * signed_sine


def unrotate(values, cosine, signed_sine):
    return values * cosine + pltpu.roll(values, HALF, 1) * signed_sine


def head_columns(head):
    return slice(head * HD, (head + 1) * HD)


def stack_heads(ref, group, first, half):
    rows = ref.shape[1] // 2
    at = slice(half * rows, (half + 1) * rows)
    return jnp.concatenate([ref[group, at, head_columns(first + i)] for i in range(QUAD)], axis=0)


def four_times(value, half):
    columns = value.shape[1] // 2
    return jnp.concatenate([value[:, half * columns : (half + 1) * columns]] * QUAD, axis=1)


def block_diagonal(upper, lower):
    zero = jnp.zeros_like(upper)
    return jnp.concatenate(
        [jnp.concatenate([upper, zero], axis=1), jnp.concatenate([zero, lower], axis=1)], axis=0
    )


def group_rows(ref, group, columns, tiles=TILES):
    return jnp.concatenate([ref[group * TILES + i, :, columns] for i in range(tiles)], axis=0)


def tile_columns(tile):
    width = RATIO * HD // TILES
    return slice(tile * width, (tile + 1) * width)


def pack_kernel(k_hbm, v_hbm, kv_ref, arrived):
    copies = [
        pltpu.make_async_copy(source.at[:, head_columns(group)], kv_ref.at[which, group], arrived.at[which, group])
        for which, source in enumerate((k_hbm, v_hbm))
        for group in range(HK)
    ]
    for copy in copies:
        copy.start()
    for copy in copies:
        copy.wait()


def own_kernel(
    first_ref, list_ref, doc_ref, q_hbm, k_hbm, v_hbm, o_hbm, g_hbm,
    notes_ref, qg_ref, prob_ref, ds_ref, kt_ref, stat_ref, half_ref, cos_ref, sin_ref, cos1_ref, sin1_ref, cos2_ref, sin2_ref,
    q_ref, k_ref, v_ref, o_ref, g_ref, arrived,
):
    rows = q_hbm.shape[0]
    arguments = ((k_hbm, k_ref), (q_hbm, q_ref), (v_hbm, v_ref), (g_hbm, g_ref), (o_hbm, o_ref))

    def fetch(which, group):
        source, buffer = arguments[which]
        width = buffer.shape[2]
        columns = pl.ds(pl.multiple_of(group * width, width), width)
        return pltpu.make_async_copy(source.at[:, columns], buffer.at[group], arrived.at[which, group])

    for group in range(HK):
        for which in range(len(arguments)):
            fetch(which, group).start()

    doc_row = doc_ref[...] - first_ref[0]
    columns = lax.broadcasted_iota(jnp.int32, (1, rows), 1)
    cos_t, sin_t = half_tables(columns - doc_row)
    cos_ref[...], sin_ref[...] = upright(cos_t, sin_t)
    reach = doc_row[:, 0:1]
    lanes = notes_ref.shape[1]
    for half in range(2):
        notes_ref[half : half + 1, :] = four_times(doc_row.astype(F32), half)
        half_ref[half, 0] = four_times(cos_t * SCORE_SCALE, half)
        half_ref[half, 1] = four_times(sin_t * SCORE_SCALE, half)
    for distance in range(1, FETCH + 1):
        listed = jnp.where(list_ref[:, distance - 1 : distance] == 1, 1.0, 0.0)
        notes_ref[distance + 1 : distance + 2, :] = jnp.broadcast_to(listed, (1, lanes))
    cos1_ref[...], sin1_ref[...] = upright(*half_tables(columns - rows - reach))
    cos2_ref[...], sin2_ref[...] = upright(*half_tables(columns - 2 * rows - reach))
    key_idx = lax.broadcasted_iota(jnp.int32, (rows, rows), 0)
    query_idx = lax.broadcasted_iota(jnp.int32, (rows, rows), 1)
    mask = (key_idx <= query_idx) & (key_idx >= doc_row)
    bias = jnp.where(mask, 0.0, NEG_LARGE)
    bias = [four_times(bias, half) for half in range(2)]
    ones = jnp.ones((8, HD), BF16)

    @pl.loop(0, HK)
    def _(group):
        for which in range(len(arguments)):
            fetch(which, group).wait()
        k_rot = rotate(k_ref[group].astype(F32), cos_ref[...], sin_ref[...])
        kt_ref[group] = k_rot.T.astype(BF16)
        left = block_diagonal(k_rot.astype(BF16), v_ref[group])

        def products(tile):
            half, quad = divmod(tile, 2)
            at = slice(half * rows // 2, (half + 1) * rows // 2)
            cosine = jnp.concatenate([cos_ref[at, :]] * QUAD, axis=0)
            signed_sine = jnp.concatenate([sin_ref[at, :]] * QUAD, axis=0)
            queries = stack_heads(q_ref, group, quad * QUAD, half).astype(F32)
            qg_ref[group * TILES + tile, :, :HD] = rotate(queries, cosine, signed_sine).astype(BF16)
            grads = stack_heads(g_ref, group, quad * QUAD, half)
            qg_ref[group * TILES + tile, :, HD:] = grads
            product = grads.astype(F32) * stack_heads(o_ref, group, quad * QUAD, half).astype(F32)
            high = product.astype(BF16)
            low = (product - high.astype(F32)).astype(BF16)
            delta = (dot_nt(ones, high) + dot_nt(ones, low))[0:1]
            both = dot_nt(left, qg_ref[group * TILES + tile])
            return both[:rows], both[rows:], delta

        def finish(tile, scores, dprob, delta):
            at = tile_columns(tile)
            scores = scores + bias[tile // 2]
            largest = jnp.max(scores, axis=0, keepdims=True)
            prob = jnp.exp2((scores - largest) * EXP2_SCALE)
            prob_ref[group, :, at] = prob.astype(BF16)
            ds_ref[group, :, at] = (prob * (dprob - delta)).astype(BF16)
            stat_ref[group, 0:1, at] = largest
            stat_ref[group, 1:2, at] = jnp.sum(prob, axis=0, keepdims=True)
            stat_ref[group, 2:3, at] = delta

        ahead = products(0)
        for tile in range(TILES):
            now = ahead
            if tile + 1 < TILES:
                ahead = products(tile + 1)
            finish(tile, *now)


def reach_bias(notes_ref, distance, rows):
    key_idx = lax.broadcasted_iota(jnp.int32, (rows, notes_ref.shape[1]), 0).astype(F32) - distance * rows
    listed = notes_ref[distance + 1 : distance + 2, 0:1]
    return jnp.where((key_idx >= notes_ref[0:1, 0:1]) & (listed > 0.0), 0.0, NEG_LARGE)


def reached(notes_ref):
    return [notes_ref[half : half + 1, :] == notes_ref[0:1, 0:1] for half in range(2)]


def high_reached(notes_ref):
    return jnp.max(jnp.where(notes_ref[1:2, :] == notes_ref[0:1, 0:1], 1.0, 0.0)) > 0.0


def goes_on(notes_ref):
    return jnp.max(notes_ref[3:4, :]) > 0.0


def softmax_step(scores, stat_ref, group, at, in_reach):
    before = stat_ref[group, 0:1, at]
    largest = jnp.maximum(before, jnp.max(scores, axis=0, keepdims=True))
    prob = jnp.exp2((scores - jnp.where(in_reach, largest, -NEG_LARGE)) * EXP2_SCALE)
    largest = jnp.where(in_reach, largest, before)
    scale = jnp.exp2((before - largest) * EXP2_SCALE)
    total = stat_ref[group, 1:2, at] * scale + jnp.sum(prob, axis=0, keepdims=True)
    return prob, largest, total, scale


def staged(tiles, products, middle, finish):
    ahead = products(0)
    behind = None
    for tile in range(tiles):
        now = ahead
        if tile + 1 < tiles:
            ahead = products(tile + 1)
        done = middle(tile, *now)
        if behind is not None:
            finish(tile - 1, behind)
        behind = done
    finish(tiles - 1, behind)


def store_query_grad(dq_refs, group, tile, dq, half_ref):
    part, group = divmod(group, EARLY)
    dq_ref = dq_refs[part]
    half, quad = divmod(tile, 2)
    rows = dq_ref.shape[1] // 2
    cos_t, sin_t = half_ref[half, 0], half_ref[half, 1]
    upper, lower = dq[:HALF], dq[HALF:]
    dq = jnp.concatenate([upper * cos_t + lower * sin_t, lower * cos_t - upper * sin_t], axis=0).astype(BF16)
    dq = dq.T
    for i in range(QUAD):
        head = group * RATIO + quad * QUAD + i
        dq_ref[0, half * rows : (half + 1) * rows, head_columns(head)] = dq[i * rows : (i + 1) * rows]


def own_alone(dq_refs, scale_ref, own_ref, ds0_ref, kt0_ref, stat_ref, half_ref, group, tiles):
    for tile in tiles:
        at = tile_columns(tile)
        scale = 1.0 / stat_ref[group, 1:2, at]
        scale_ref[group, 0:1, at] = scale
        dscore = ds0_ref[group, :, at] * scale.astype(BF16)
        own_ref[group, :, at] = dscore
        store_query_grad(dq_refs, group, tile, dot_nn(kt0_ref[group], dscore), half_ref)


def key_products(qg_ref, group, tiles, dscore, prob):
    rows = dscore.shape[0]
    both = dot_nn(jnp.concatenate([dscore, prob], axis=0), group_rows(qg_ref, group, slice(2 * HD), tiles))
    return (both[:rows, :HD] * SCORE_SCALE).astype(BF16), both[rows:, HD:].astype(BF16)


def near_kernel(
    notes_ref, qg_ref, kv_ref, ds0_ref, kt0_ref, stat_ref, half_ref, cos_ref, sin_ref,
    dqa_ref, dqb_ref, ret2_ref, ret1_ref, scale_ref, own_ref, prob_ref, ds_ref, kt_ref, next_ref,
):
    dq_refs = (dqa_ref, dqb_ref)
    rows = kv_ref.shape[2]

    def attend(last, tiles):
        in_reach = reached(notes_ref)
        bias = reach_bias(notes_ref, 1, rows)
        for group in range(HK):
            one_group(last, tiles, in_reach, bias, group)

    def one_group(last, tiles, in_reach, bias, group):
        k_rot = rotate(kv_ref[0, group].astype(F32), cos_ref[...], sin_ref[...])
        k_rot_t = k_rot.T.astype(BF16)
        left = block_diagonal(k_rot.astype(BF16), kv_ref[1, group])
        both_t = jnp.concatenate([k_rot_t, kt0_ref[group]], axis=1)

        def products(tile):
            both = dot_nt(left, qg_ref[group * TILES + tile])
            return both[:rows], both[rows:]

        def middle(tile, scores, dprob):
            at = tile_columns(tile)
            prob, largest, total, scale = softmax_step(scores + bias, stat_ref, group, at, in_reach[tile // 2])
            delta = stat_ref[group, 2:3, at]
            if last:
                inverse = 1.0 / total
                scale = scale * inverse
                prob = prob * inverse
                scale_ref[group, 0:1, at] = scale
            prob = prob.astype(BF16)
            dscore = prob * (dprob - delta).astype(BF16)
            prob_ref[group, :, at] = prob
            ds_ref[group, :, at] = dscore
            if last:
                own_dscore = ds0_ref[group, :, at] * scale.astype(BF16)
                own_ref[group, :, at] = own_dscore
                return jnp.concatenate([dscore, own_dscore], axis=0)
            next_ref[group, 0:1, at] = largest
            next_ref[group, 1:2, at] = total
            next_ref[group, 2:3, at] = delta
            next_ref[group, 3:4, at] = scale
            return None

        def finish(tile, dscore):
            if last:
                store_query_grad(dq_refs, group, tile, dot_nn(both_t, dscore), half_ref)

        staged(tiles, products, middle, finish)
        if last:
            own_alone(
                dq_refs, scale_ref, own_ref, ds0_ref, kt0_ref, stat_ref, half_ref, group, range(tiles, TILES)
            )
            used = slice(0, tile_columns(tiles - 1).stop)
            grads = key_products(qg_ref, group, tiles, ds_ref[group, :, used], prob_ref[group, :, used])
            for which, grad in enumerate(grads):
                ret1_ref[which, group] = grad
                ret2_ref[which, group] = jnp.zeros((rows, HD), BF16)
        else:
            kt_ref[group] = k_rot_t
            for tile in range(tiles, TILES):
                next_ref[group, 1:2, tile_columns(tile)] = stat_ref[group, 1:2, tile_columns(tile)]

    further, wide = goes_on(notes_ref), high_reached(notes_ref)
    for last in (True, False):
        for tiles in (TILES // 2, TILES):
            chosen = (further != last) & (wide == (tiles == TILES))
            pl.when(chosen)(lambda last=last, tiles=tiles: attend(last, tiles))


def far_kernel(
    notes_ref, qg_ref, kv_ref, ds0_ref, kt0_ref, half_ref, cos_ref, sin_ref,
    prob1_ref, ds1_ref, kt1_ref, stat_ref, *refs,
):
    *dq_refs, ret2_ref, ret1_ref, scale_ref, own_ref, prob_buf, ds_buf = refs[6:]
    rows = kv_ref.shape[2]

    def attend(skipped, tiles):
        in_reach = reached(notes_ref)
        bias = reach_bias(notes_ref, 2, rows)[skipped:]
        for group in range(HK):
            one_group(skipped, tiles, in_reach, bias, group)

    def one_group(skipped, tiles, in_reach, bias, group):
        used = rows - skipped
        k_rot = rotate(kv_ref[0, group, skipped:, :].astype(F32), cos_ref[skipped:, :], sin_ref[skipped:, :])
        left = block_diagonal(k_rot.astype(BF16), kv_ref[1, group, skipped:, :])
        k_rot_t = k_rot.T.astype(BF16)
        near_t = jnp.concatenate([kt1_ref[group], kt0_ref[group]], axis=1)

        def products(tile):
            both = dot_nt(left, qg_ref[group * TILES + tile])
            return both[:used], both[used:]

        def middle(tile, scores, dprob):
            at = tile_columns(tile)
            prob, _, total, scale = softmax_step(scores + bias, stat_ref, group, at, in_reach[tile // 2])
            inverse = 1.0 / total
            near_scale = scale * inverse
            own_scale = near_scale * stat_ref[group, 3:4, at]
            scale_ref[group, 0:1, at] = own_scale
            prob = (prob * inverse).astype(BF16)
            dscore = prob * (dprob - stat_ref[group, 2:3, at]).astype(BF16)
            near_scale = near_scale.astype(BF16)
            near_dscore = ds1_ref[group, :, at] * near_scale
            own_dscore = ds0_ref[group, :, at] * own_scale.astype(BF16)
            own_ref[group, :, at] = own_dscore
            prob_buf[:used, at] = prob
            prob_buf[used : used + rows, at] = prob1_ref[group, :, at] * near_scale
            ds_buf[:used, at] = dscore
            ds_buf[used : used + rows, at] = near_dscore
            return dscore, jnp.concatenate([near_dscore, own_dscore], axis=0)

        def finish(tile, dscores):
            dq = dot_nn(near_t, dscores[1]) + dot_nn(k_rot_t, dscores[0])
            store_query_grad(dq_refs, group, tile, dq, half_ref)

        staged(tiles, products, middle, finish)
        own_alone(
            dq_refs, scale_ref, own_ref, ds0_ref, kt0_ref, stat_ref, half_ref, group, range(tiles, TILES)
        )
        columns = slice(0, tile_columns(tiles - 1).stop)
        grads = key_products(qg_ref, group, tiles, ds_buf[: used + rows, columns], prob_buf[: used + rows, columns])
        for which, grad in enumerate(grads):
            ret1_ref[which, group] = grad[used:]
            ret2_ref[which, group, skipped:, :] = grad[:used]
            if skipped:
                ret2_ref[which, group, :skipped, :] = jnp.zeros((skipped, HD), BF16)

    @pl.when(goes_on(notes_ref))
    def _():
        wide = high_reached(notes_ref)
        pl.when(wide)(lambda: attend(rows // 2, TILES))
        pl.when(jnp.logical_not(wide))(lambda: attend(0, TILES // 2))


def own_kv_kernel(qg_ref, prob_ref, ds_ref, scale_ref, dk_ref, dv_ref):
    @pl.loop(0, HK)
    def _(group):
        prob = (prob_ref[group].astype(F32) * scale_ref[group, 0:1, :]).astype(BF16)
        dk_ref[group] = dot_nn(ds_ref[group], group_rows(qg_ref, group, slice(HD))) * SCORE_SCALE
        dv_ref[group] = dot_nn(prob, group_rows(qg_ref, group, slice(HD, 2 * HD)))


def hand_kernel(dq_ref, handed_hbm, copied):
    rows, width = dq_ref.shape[1:]
    copies = []
    for i in range(2):
        at = pl.ds(i * rows // 2, rows // 2)
        copies.append(pltpu.make_async_copy(dq_ref.at[:, at], handed_hbm.at[:, at, pl.ds(0, width)], copied.at[i]))
    for copy in copies:
        copy.start()
    for copy in copies:
        copy.wait()


def sum_kernel(
    dk_ref, dv_ref, ret2_ref, ret1_ref, late_ref, cos_ref, sin_ref, handed_in,
    key_hbm, value_hbm, handed_hbm, key_buf, value_buf, copied,
):
    del handed_in
    width = late_ref.shape[2]
    rest = pl.ds(handed_hbm.shape[2] - width, width)
    copies = [pltpu.make_async_copy(late_ref, handed_hbm.at[:, :, rest], copied.at[0])]
    copies[0].start()
    for group in range(HK):
        at = head_columns(group)
        dv = dv_ref[group] + ret1_ref[1, group].astype(F32) + ret2_ref[1, group].astype(F32)
        value_buf[0, :, at] = dv.astype(BF16)
    copies.append(pltpu.make_async_copy(value_buf, value_hbm, copied.at[1]))
    copies[-1].start()
    for group in range(HK):
        at = head_columns(group)
        dk = dk_ref[group] + ret1_ref[0, group].astype(F32) + ret2_ref[0, group].astype(F32)
        key_buf[0, :, at] = unrotate(dk, cos_ref[...], sin_ref[...]).astype(BF16)
    copies.append(pltpu.make_async_copy(key_buf, key_hbm, copied.at[2]))
    copies[-1].start()
    for copy in copies:
        copy.wait()


def cost(flops, moved, exps=0):
    return pl.CostEstimate(flops=int(flops), bytes_accessed=int(moved), transcendentals=int(exps))


def shards(query_heads, key_heads, value_heads, attn_output, output_grad, doc_start, fetch_list):
    rows = query_heads.shape[1]
    wide = RATIO * HD
    kv_width = HK * HD
    first_row = (lax.axis_index("ctx") * rows).astype(jnp.int32).reshape(1)
    doc_row = doc_start.reshape(1, rows)
    smem = pl.BlockSpec(memory_space=pltpu.SMEM)
    vmem = pl.BlockSpec(memory_space=pltpu.VMEM)
    hbm = pl.BlockSpec(memory_space=pltpu.HBM)
    anywhere = pl.BlockSpec(memory_space=pl.ANY)
    params = pltpu.CompilerParams(vmem_limit_bytes=40 * 1024 * 1024)
    shape = jax.ShapeDtypeStruct
    block_flops = 2 * HQ * rows * rows * HD
    arguments = [
        pltpu.with_memory_space_constraint(x[0], pltpu.HBM)
        for x in (query_heads, key_heads, value_heads, attn_output, output_grad)
    ]

    kv = pl.pallas_call(
        pack_kernel,
        in_specs=[hbm, hbm],
        out_specs=vmem,
        out_shape=shape((2, HK, rows, HD), BF16),
        scratch_shapes=[pltpu.SemaphoreType.DMA((2, HK))],
        compiler_params=params,
        cost_estimate=cost(0, 2**19),
        name="pack_keys",
    )(arguments[1], arguments[2])
    kv2 = from_behind(kv, "ctx", 2)
    kv1 = from_behind(kv, "ctx", 1)

    notes, qg, prob0, ds0, k_own_t, stat, half, cos, sin, cos1, sin1, cos2, sin2 = pl.pallas_call(
        own_kernel,
        in_specs=[smem, vmem, vmem] + [hbm] * 5,
        out_specs=[vmem] * 13,
        out_shape=[
            shape((8, QUAD * rows // 2), F32),
            shape((HK * TILES, QUAD * rows // 2, 2 * HD), BF16),
            shape((HK, rows, RATIO * rows), BF16),
            shape((HK, rows, RATIO * rows), BF16),
            shape((HK, HD, rows), BF16),
            shape((HK, 8, RATIO * rows), F32),
            shape((2, 2, HALF, QUAD * rows // 2), F32),
            shape((rows, HD), F32),
            shape((rows, HD), F32),
            shape((rows, HD), F32),
            shape((rows, HD), F32),
            shape((rows, HD), F32),
            shape((rows, HD), F32),
        ],
        scratch_shapes=[
            pltpu.VMEM((HK, rows, wide), BF16),
            pltpu.VMEM((HK, rows, HD), BF16),
            pltpu.VMEM((HK, rows, HD), BF16),
            pltpu.VMEM((HK, rows, wide), BF16),
            pltpu.VMEM((HK, rows, wide), BF16),
            pltpu.SemaphoreType.DMA((5, HK)),
        ],
        compiler_params=params,
        cost_estimate=cost(3 * block_flops, 9 * 2**20, HQ * rows * rows),
        name="own_block",
    )(first_row, *(pltpu.with_memory_space_constraint(x, pltpu.HBM) for x in (fetch_list, doc_row)), *arguments)

    results = [
        shape((1, rows, EARLY * RATIO * HD), BF16),
        shape((1, rows, (HK - EARLY) * RATIO * HD), BF16),
        shape((2, HK, rows, HD), BF16),
        shape((2, HK, rows, HD), BF16),
        shape((HK, 8, RATIO * rows), F32),
        shape((HK, rows, RATIO * rows), BF16),
    ]
    *settled, prob1, ds1, k_near_t, stat1 = pl.pallas_call(
        near_kernel,
        in_specs=[vmem] * 9,
        out_specs=[vmem] * 10,
        out_shape=results
        + [
            shape((HK, rows, RATIO * rows), BF16),
            shape((HK, rows, RATIO * rows), BF16),
            shape((HK, HD, rows), BF16),
            shape((HK, 8, RATIO * rows), F32),
        ],
        compiler_params=params,
        cost_estimate=cost(5 * block_flops, 9 * 2**20, HQ * rows * rows),
        name="near_block",
    )(notes, qg, kv1, ds0, k_own_t, stat, half, cos1, sin1)

    dq_early, dq_late, ret2, ret1, scale, ds_own = pl.pallas_call(
        far_kernel,
        in_specs=[vmem] * 18,
        out_specs=[vmem] * 6,
        out_shape=results,
        scratch_shapes=[
            pltpu.VMEM((FETCH * rows, RATIO * rows), BF16),
            pltpu.VMEM((FETCH * rows, RATIO * rows), BF16),
        ],
        input_output_aliases={12 + i: i for i in range(6)},
        compiler_params=params,
        cost_estimate=cost(5 * block_flops, 9 * 2**20, HQ * rows * rows),
        name="far_block",
    )(notes, qg, kv2, ds0, k_own_t, half, cos2, sin2, prob1, ds1, k_near_t, stat1, *settled)
    arrived1 = from_behind(ret1, "ctx", -1)
    arrived2 = from_behind(ret2, "ctx", -2)
    early = from_behind(dq_early, "section", -1)
    late = from_behind(dq_late, "section", -1)

    dk0, dv0 = pl.pallas_call(
        own_kv_kernel,
        in_specs=[vmem] * 4,
        out_specs=[vmem] * 2,
        out_shape=[shape((HK, rows, HD), F32), shape((HK, rows, HD), F32)],
        compiler_params=params,
        cost_estimate=cost(2 * block_flops, 5 * 2**20),
        name="own_keys",
    )(qg, prob0, ds_own, scale)

    handed = pl.pallas_call(
        hand_kernel,
        in_specs=[anywhere],
        out_specs=hbm,
        out_shape=shape((1, rows, HQ * HD), BF16),
        scratch_shapes=[pltpu.SemaphoreType.DMA((2,))],
        compiler_params=params,
        cost_estimate=cost(0, 2 * 2**20),
        name="hand_on",
    )(early)

    key_grad, value_grad, handed_grad = pl.pallas_call(
        sum_kernel,
        in_specs=[vmem] * 4 + [anywhere] + [vmem] * 2 + [hbm],
        out_specs=[hbm] * 3,
        input_output_aliases={7: 2},
        out_shape=[
            shape((1, rows, kv_width), BF16),
            shape((1, rows, kv_width), BF16),
            shape((1, rows, HQ * HD), BF16),
        ],
        scratch_shapes=[
            pltpu.VMEM((1, rows, kv_width), BF16),
            pltpu.VMEM((1, rows, kv_width), BF16),
            pltpu.SemaphoreType.DMA((3,)),
        ],
        compiler_params=params,
        cost_estimate=cost(0, 3 * 2**20),
        name="sum_keys",
    )(dk0, dv0, arrived2, arrived1, late, cos, sin, handed)
    return (handed_grad, key_grad, value_grad)


def solution(mesh):
    return jax.shard_map(
        shards,
        mesh=mesh,
        in_specs=(
            P("section", "ctx", None),
            P("section", "ctx", None),
            P("section", "ctx", None),
            P("section", "ctx", None),
            P("section", "ctx", None),
            P("ctx"),
            P("ctx", None),
        ),
        out_specs=(P("section", "ctx", None), P("section", "ctx", None), P("section", "ctx", None)),
        check_vma=False,
    )
```

```python
import math

import jax
import jax.numpy as jnp
from jax import lax
from jax.experimental import pallas as pl
from jax.experimental.pallas import tpu as pltpu
from jax.sharding import PartitionSpec as P

HQ = 32
HK = 4
HD = 128
RATIO = HQ // HK
HALF = HD // 2
FETCH = 2
QUAD = 4
EARLY = 3
TILES = 4

ROPE_BASE = 1000000.0
TRAINED_CONTEXT = 32768.0
YARN_FACTOR = 4.0
NEG_LARGE = -1e30
SCORE_SCALE = HD ** (-0.5)
EXP2_SCALE = SCORE_SCALE / math.log(2.0)

F32 = jnp.float32
BF16 = jnp.bfloat16


def from_behind(value, axis, steps):
    count = lax.axis_size(axis)
    initial, last = (max(0, -steps), min(count, count - steps))
    return lax.ppermute(value, axis, [(source, source + steps) for source in range(initial, last)])


def dot_nn(left, right):
    return lax.dot_general(left, right, (((1,), (0,)), ((), ())), preferred_element_type=F32)


def dot_nt(left, right):
    return lax.dot_general(left, right, (((1,), (1,)), ((), ())), preferred_element_type=F32)


def frequencies(rows, columns):
    def correction(rotations):
        return HD * math.log(TRAINED_CONTEXT / (rotations * 2.0 * math.pi)) / (2.0 * math.log(ROPE_BASE))

    lower_dim = max(math.floor(correction(32.0)), 0)
    upper_dim = min(math.ceil(correction(1.0)), HD - 1)
    spread_dims = max(upper_dim - lower_dim, 0.001)
    indices = lax.broadcasted_iota(jnp.int32, (rows, columns), 0).astype(F32)
    extrapolated = jnp.exp(indices * F32(-2.0 / HD * math.log(ROPE_BASE)))
    ramp_weight = jnp.clip((indices - lower_dim) / spread_dims, 0.0, 1.0)
    return extrapolated / YARN_FACTOR * ramp_weight + extrapolated * (1.0 - ramp_weight)


def cos_sin(angles):
    turns = jnp.floor(angles * F32(2.0 / math.pi) + 0.5)
    rest = angles - turns * F32(1.5703125)
    rest = rest - turns * F32(4.837512969970703125e-4)
    rest = rest - turns * F32(7.54978995489188216e-8)
    square = rest * rest
    sine = rest + rest * square * (
        F32(-1.6666654611e-1) + square * (F32(8.3321608736e-3) + square * F32(-1.9515295891e-4))
    )
    cosine = (1.0 - 0.5 * square) + square * square * (
        F32(4.166664568298827e-2) + square * (F32(-1.388731625493765e-3) + square * F32(2.443315711809948e-5))
    )
    quarter = turns.astype(jnp.int32)
    swapped = (quarter & 1) == 1
    cos_value = jnp.where(swapped, sine, cosine)
    sin_value = jnp.where(swapped, cosine, sine)
    cos_value = jnp.where(((quarter + 1) & 2) == 2, -cos_value, cos_value)
    sin_value = jnp.where((quarter & 2) == 2, -sin_value, sin_value)
    return cos_value, sin_value


def half_tables(positions):
    factor = 0.1 * math.log(YARN_FACTOR) + 1.0
    cos_t, sin_t = cos_sin(frequencies(HALF, positions.shape[1]) * positions.astype(F32))
    return cos_t * factor, sin_t * factor


def shifted_tables(tables, shift):
    cos_t, sin_t = tables
    cos_s, sin_s = cos_sin(frequencies(HALF, cos_t.shape[1]) * F32(shift))
    return cos_t * cos_s + sin_t * sin_s, sin_t * cos_s - cos_t * sin_s


def upright(cos_t, sin_t):
    cosine = jnp.concatenate([cos_t, cos_t], axis=0).T
    signed_sine = jnp.concatenate([sin_t, -sin_t], axis=0).T
    return cosine, signed_sine


def rotate(values, cosine, signed_sine):
    return values * cosine - pltpu.roll(values, HALF, 1) * signed_sine


def unrotate(values, cosine, signed_sine):
    return values * cosine + pltpu.roll(values, HALF, 1) * signed_sine


def head_columns(head):
    return slice(head * HD, (head + 1) * HD)


def stack_heads(ref, group, first, half):
    rows = ref.shape[1] // 2
    at = slice(half * rows, (half + 1) * rows)
    return jnp.concatenate([ref[group, at, head_columns(first + i)] for i in range(QUAD)], axis=0)


def four_times(value, half):
    columns = value.shape[1] // 2
    return jnp.concatenate([value[:, half * columns : (half + 1) * columns]] * QUAD, axis=1)


def block_diagonal(upper, lower):
    zero = jnp.zeros_like(upper)
    return jnp.concatenate(
        [jnp.concatenate([upper, zero], axis=1), jnp.concatenate([zero, lower], axis=1)], axis=0
    )


def group_rows(ref, group, columns, tiles=TILES):
    return jnp.concatenate([ref[group * TILES + i, :, columns] for i in range(tiles)], axis=0)


def tile_columns(tile):
    width = RATIO * HD // TILES
    return slice(tile * width, (tile + 1) * width)


def pack_kernel(k_hbm, v_hbm, kv_ref, arrived):
    copies = [
        pltpu.make_async_copy(source.at[:, head_columns(group)], kv_ref.at[which, group], arrived.at[which, group])
        for which, source in enumerate((k_hbm, v_hbm))
        for group in range(HK)
    ]
    for copy in copies:
        copy.start()
    for copy in copies:
        copy.wait()


def own_kernel(
    first_ref, list_ref, doc_ref, q_hbm, k_hbm, v_hbm, o_hbm, g_hbm,
    notes_ref, qg_ref, prob_ref, ds_ref, kt_ref, stat_ref, half_ref, cos_ref, sin_ref, cos1_ref, sin1_ref, cos2_ref, sin2_ref,
    q_ref, k_ref, v_ref, o_ref, g_ref, arrived,
):
    rows = q_hbm.shape[0]
    arguments = ((k_hbm, k_ref), (q_hbm, q_ref), (v_hbm, v_ref), (g_hbm, g_ref), (o_hbm, o_ref))

    def fetch(which, group):
        source, buffer = arguments[which]
        width = buffer.shape[2]
        columns = pl.ds(pl.multiple_of(group * width, width), width)
        return pltpu.make_async_copy(source.at[:, columns], buffer.at[group], arrived.at[which, group])

    for group in range(HK):
        for which in range(len(arguments)):
            fetch(which, group).start()

    doc_row = doc_ref[...] - first_ref[0]
    columns = lax.broadcasted_iota(jnp.int32, (1, rows), 1)
    cos_t, sin_t = half_tables(columns - doc_row)
    cos_ref[...], sin_ref[...] = upright(cos_t, sin_t)
    reach = doc_row[:, 0:1]
    lanes = notes_ref.shape[1]
    for half in range(2):
        notes_ref[half : half + 1, :] = four_times(doc_row.astype(F32), half)
        half_ref[half, 0] = four_times(cos_t * SCORE_SCALE, half)
        half_ref[half, 1] = four_times(sin_t * SCORE_SCALE, half)
    for distance in range(1, FETCH + 1):
        listed = jnp.where(list_ref[:, distance - 1 : distance] == 1, 1.0, 0.0)
        notes_ref[distance + 1 : distance + 2, :] = jnp.broadcast_to(listed, (1, lanes))
    near_tables = half_tables(columns - rows - reach)
    cos1_ref[...], sin1_ref[...] = upright(*near_tables)
    cos2_ref[...], sin2_ref[...] = upright(*shifted_tables(near_tables, rows))
    key_idx = lax.broadcasted_iota(jnp.int32, (rows, rows), 0)
    query_idx = lax.broadcasted_iota(jnp.int32, (rows, rows), 1)
    mask = (key_idx <= query_idx) & (key_idx >= doc_row)
    bias = jnp.where(mask, 0.0, NEG_LARGE)
    bias = [four_times(bias, half) for half in range(2)]

    @pl.loop(0, HK)
    def _(group):
        for which in range(len(arguments)):
            fetch(which, group).wait()
        k_rot = rotate(k_ref[group].astype(F32), cos_ref[...], sin_ref[...])
        kt_ref[group] = k_rot.T.astype(BF16)
        left = block_diagonal(k_rot.astype(BF16), v_ref[group])

        def products(tile):
            half, quad = divmod(tile, 2)
            at = slice(half * rows // 2, (half + 1) * rows // 2)
            cosine = jnp.concatenate([cos_ref[at, :]] * QUAD, axis=0)
            signed_sine = jnp.concatenate([sin_ref[at, :]] * QUAD, axis=0)
            queries = stack_heads(q_ref, group, quad * QUAD, half).astype(F32)
            qg_ref[group * TILES + tile, :, :HD] = rotate(queries, cosine, signed_sine).astype(BF16)
            grads = stack_heads(g_ref, group, quad * QUAD, half)
            qg_ref[group * TILES + tile, :, HD:] = grads
            outputs = stack_heads(o_ref, group, quad * QUAD, half)
            delta = jnp.sum(grads.T.astype(F32) * outputs.T.astype(F32), axis=0, keepdims=True)
            both = dot_nt(left, qg_ref[group * TILES + tile])
            return both[:rows], both[rows:], delta

        def finish(tile, scores, dprob, delta):
            at = tile_columns(tile)
            scores = scores + bias[tile // 2]
            largest = jnp.max(scores, axis=0, keepdims=True)
            prob = jnp.exp2((scores - largest) * EXP2_SCALE)
            prob_ref[group, :, at] = prob.astype(BF16)
            ds_ref[group, :, at] = (prob * (dprob - delta)).astype(BF16)
            stat_ref[group, 0:1, at] = largest
            stat_ref[group, 1:2, at] = jnp.sum(prob, axis=0, keepdims=True)
            stat_ref[group, 2:3, at] = delta

        ahead = products(0)
        for tile in range(TILES):
            now = ahead
            if tile + 1 < TILES:
                ahead = products(tile + 1)
            finish(tile, *now)


def reach_bias(notes_ref, distance, rows):
    key_idx = lax.broadcasted_iota(jnp.int32, (rows, notes_ref.shape[1]), 0).astype(F32) - distance * rows
    listed = notes_ref[distance + 1 : distance + 2, 0:1]
    return jnp.where((key_idx >= notes_ref[0:1, 0:1]) & (listed > 0.0), 0.0, NEG_LARGE)


def reached(notes_ref):
    return [notes_ref[half : half + 1, :] == notes_ref[0:1, 0:1] for half in range(2)]


def high_reached(notes_ref):
    return jnp.max(jnp.where(notes_ref[1:2, :] == notes_ref[0:1, 0:1], 1.0, 0.0)) > 0.0


def goes_on(notes_ref):
    return jnp.max(notes_ref[3:4, :]) > 0.0


def softmax_step(scores, stat_ref, group, at, in_reach):
    before = stat_ref[group, 0:1, at]
    largest = jnp.maximum(before, jnp.max(scores, axis=0, keepdims=True))
    prob = jnp.exp2((scores - jnp.where(in_reach, largest, -NEG_LARGE)) * EXP2_SCALE)
    largest = jnp.where(in_reach, largest, before)
    scale = jnp.exp2((before - largest) * EXP2_SCALE)
    total = stat_ref[group, 1:2, at] * scale + jnp.sum(prob, axis=0, keepdims=True)
    return prob, largest, total, scale


def staged(tiles, products, middle, finish):
    ahead = products(0)
    behind = None
    for tile in range(tiles):
        now = ahead
        if tile + 1 < tiles:
            ahead = products(tile + 1)
        done = middle(tile, *now)
        if behind is not None:
            finish(tile - 1, behind)
        behind = done
    finish(tiles - 1, behind)


def store_query_grad(dq_refs, group, tile, dq, half_ref):
    part, group = divmod(group, EARLY)
    dq_ref = dq_refs[part]
    half, quad = divmod(tile, 2)
    rows = dq_ref.shape[1] // 2
    cos_t, sin_t = half_ref[half, 0], half_ref[half, 1]
    upper, lower = dq[:HALF], dq[HALF:]
    dq = jnp.concatenate([upper * cos_t + lower * sin_t, lower * cos_t - upper * sin_t], axis=0).astype(BF16)
    dq = dq.T
    for i in range(QUAD):
        head = group * RATIO + quad * QUAD + i
        dq_ref[0, half * rows : (half + 1) * rows, head_columns(head)] = dq[i * rows : (i + 1) * rows]


def own_alone(dq_refs, scale_ref, ds0_ref, kt0_ref, stat_ref, half_ref, group, tiles):
    for tile in tiles:
        at = tile_columns(tile)
        scale = 1.0 / stat_ref[group, 1:2, at]
        scale_ref[group, 0:1, at] = scale
        dscore = ds0_ref[group, :, at] * scale.astype(BF16)
        store_query_grad(dq_refs, group, tile, dot_nn(kt0_ref[group], dscore), half_ref)


def key_products(qg_ref, group, tiles, dscore, prob):
    rows = dscore.shape[0]
    both = dot_nn(jnp.concatenate([dscore, prob], axis=0), group_rows(qg_ref, group, slice(2 * HD), tiles))
    return (both[:rows, :HD] * SCORE_SCALE).astype(BF16), both[rows:, HD:].astype(BF16)


def near_kernel(
    notes_ref, qg_ref, kv_ref, ds0_ref, kt0_ref, stat_ref, half_ref, cos_ref, sin_ref,
    dqa_ref, dqb_ref, ret2_ref, ret1_ref, scale_ref, prob_ref, ds_ref, sum_ref, next_ref,
):
    dq_refs = (dqa_ref, dqb_ref)
    rows = kv_ref.shape[2]

    def attend(last, tiles):
        in_reach = reached(notes_ref)
        bias = reach_bias(notes_ref, 1, rows)
        for group in range(HK):
            one_group(last, tiles, in_reach, bias, group)

    def one_group(last, tiles, in_reach, bias, group):
        k_rot = rotate(kv_ref[0, group].astype(F32), cos_ref[...], sin_ref[...])
        k_rot_t = k_rot.T.astype(BF16)
        left = block_diagonal(k_rot.astype(BF16), kv_ref[1, group])
        both_t = jnp.concatenate([k_rot_t, kt0_ref[group]], axis=1)

        def products(tile):
            both = dot_nt(left, qg_ref[group * TILES + tile])
            return both[:rows], both[rows:]

        def middle(tile, scores, dprob):
            at = tile_columns(tile)
            prob, largest, total, scale = softmax_step(scores + bias, stat_ref, group, at, in_reach[tile // 2])
            delta = stat_ref[group, 2:3, at]
            if last:
                inverse = 1.0 / total
                scale = scale * inverse
                prob = prob * inverse
                scale_ref[group, 0:1, at] = scale
            prob = prob.astype(BF16)
            dscore = prob * (dprob - delta).astype(BF16)
            prob_ref[group, :, at] = prob
            ds_ref[group, :, at] = dscore
            if not last:
                keep_statistics(at, largest, total, delta, scale)
            return jnp.concatenate([dscore, ds0_ref[group, :, at] * scale.astype(BF16)], axis=0)

        def keep_statistics(at, largest, total, delta, scale):
            next_ref[group, 0:1, at] = largest
            next_ref[group, 1:2, at] = total
            next_ref[group, 2:3, at] = delta
            next_ref[group, 3:4, at] = scale

        def finish(tile, dscore):
            dq = dot_nn(both_t, dscore)
            if last:
                store_query_grad(dq_refs, group, tile, dq, half_ref)
            else:
                sum_ref[group, :, tile_columns(tile)] = dq

        staged(tiles, products, middle, finish)
        own_alone(dq_refs, scale_ref, ds0_ref, kt0_ref, stat_ref, half_ref, group, range(tiles, TILES))
        if last:
            used = slice(0, tile_columns(tiles - 1).stop)
            grads = key_products(qg_ref, group, tiles, ds_ref[group, :, used], prob_ref[group, :, used])
            for which, grad in enumerate(grads):
                ret1_ref[which, group] = grad
                ret2_ref[which, group] = jnp.zeros((rows, HD), BF16)

    further, wide = goes_on(notes_ref), high_reached(notes_ref)
    for last in (True, False):
        for tiles in (TILES // 2, TILES):
            chosen = (further != last) & (wide == (tiles == TILES))
            pl.when(chosen)(lambda last=last, tiles=tiles: attend(last, tiles))


def far_kernel(
    notes_ref, qg_ref, kv_ref, half_ref, cos_ref, sin_ref, prob1_ref, ds1_ref, sum_ref, stat_ref, *refs,
):
    *dq_refs, ret2_ref, ret1_ref, scale_ref, prob_buf, ds_buf = refs[5:]
    rows = kv_ref.shape[2]

    def attend(skipped, tiles):
        in_reach = reached(notes_ref)
        bias = reach_bias(notes_ref, 2, rows)[skipped:]
        for group in range(HK):
            one_group(skipped, tiles, in_reach, bias, group)

    def one_group(skipped, tiles, in_reach, bias, group):
        used = rows - skipped
        k_rot = rotate(kv_ref[0, group, skipped:, :].astype(F32), cos_ref[skipped:, :], sin_ref[skipped:, :])
        left = block_diagonal(k_rot.astype(BF16), kv_ref[1, group, skipped:, :])
        k_rot_t = k_rot.T.astype(BF16)

        def products(tile):
            both = dot_nt(left, qg_ref[group * TILES + tile])
            return both[:used], both[used:]

        def middle(tile, scores, dprob):
            at = tile_columns(tile)
            prob, _, total, scale = softmax_step(scores + bias, stat_ref, group, at, in_reach[tile // 2])
            inverse = 1.0 / total
            near_scale = scale * inverse
            scale_ref[group, 0:1, at] = near_scale * stat_ref[group, 3:4, at]
            prob = (prob * inverse).astype(BF16)
            dscore = prob * (dprob - stat_ref[group, 2:3, at]).astype(BF16)
            factor = near_scale.astype(BF16)
            prob_buf[:used, at] = prob
            prob_buf[used : used + rows, at] = prob1_ref[group, :, at] * factor
            ds_buf[:used, at] = dscore
            ds_buf[used : used + rows, at] = ds1_ref[group, :, at] * factor
            return near_scale, dscore

        def finish(tile, done):
            near_scale, dscore = done
            dq = sum_ref[group, :, tile_columns(tile)] * near_scale + dot_nn(k_rot_t, dscore)
            store_query_grad(dq_refs, group, tile, dq, half_ref)

        staged(tiles, products, middle, finish)
        columns = slice(0, tile_columns(tiles - 1).stop)
        grads = key_products(qg_ref, group, tiles, ds_buf[: used + rows, columns], prob_buf[: used + rows, columns])
        for which, grad in enumerate(grads):
            ret1_ref[which, group] = grad[used:]
            ret2_ref[which, group, skipped:, :] = grad[:used]
            if skipped:
                ret2_ref[which, group, :skipped, :] = jnp.zeros((skipped, HD), BF16)

    @pl.when(goes_on(notes_ref))
    def _():
        wide = high_reached(notes_ref)
        pl.when(wide)(lambda: attend(rows // 2, TILES))
        pl.when(jnp.logical_not(wide))(lambda: attend(0, TILES // 2))


def own_kv_kernel(qg_ref, prob_ref, ds_ref, scale_ref, dk_ref, dv_ref):
    @pl.loop(0, HK)
    def _(group):
        scale = scale_ref[group, 0:1, :]
        prob = (prob_ref[group].astype(F32) * scale).astype(BF16)
        dscore = (ds_ref[group].astype(F32) * scale).astype(BF16)
        dk_ref[group] = dot_nn(dscore, group_rows(qg_ref, group, slice(HD))) * SCORE_SCALE
        dv_ref[group] = dot_nn(prob, group_rows(qg_ref, group, slice(HD, 2 * HD)))


def hand_kernel(dq_ref, handed_hbm, copied):
    rows, width = dq_ref.shape[1:]
    copies = []
    for i in range(2):
        at = pl.ds(i * rows // 2, rows // 2)
        copies.append(pltpu.make_async_copy(dq_ref.at[:, at], handed_hbm.at[:, at, pl.ds(0, width)], copied.at[i]))
    for copy in copies:
        copy.start()
    for copy in copies:
        copy.wait()


def sum_kernel(
    dk_ref, dv_ref, ret2_ref, ret1_ref, late_ref, cos_ref, sin_ref, handed_in,
    key_hbm, value_hbm, handed_hbm, key_buf, value_buf, copied,
):
    del handed_in
    width = late_ref.shape[2]
    rest = pl.ds(handed_hbm.shape[2] - width, width)
    copies = [pltpu.make_async_copy(late_ref, handed_hbm.at[:, :, rest], copied.at[0])]
    copies[0].start()
    for group in range(HK):
        at = head_columns(group)
        dv = dv_ref[group] + ret1_ref[1, group].astype(F32) + ret2_ref[1, group].astype(F32)
        value_buf[0, :, at] = dv.astype(BF16)
    copies.append(pltpu.make_async_copy(value_buf, value_hbm, copied.at[1]))
    copies[-1].start()
    for group in range(HK):
        at = head_columns(group)
        dk = dk_ref[group] + ret1_ref[0, group].astype(F32) + ret2_ref[0, group].astype(F32)
        key_buf[0, :, at] = unrotate(dk, cos_ref[...], sin_ref[...]).astype(BF16)
    copies.append(pltpu.make_async_copy(key_buf, key_hbm, copied.at[2]))
    copies[-1].start()
    for copy in copies:
        copy.wait()


def cost(flops, moved, exps=0):
    return pl.CostEstimate(flops=int(flops), bytes_accessed=int(moved), transcendentals=int(exps))


def shards(query_heads, key_heads, value_heads, attn_output, output_grad, doc_start, fetch_list):
    rows = query_heads.shape[1]
    wide = RATIO * HD
    kv_width = HK * HD
    first_row = (lax.axis_index("ctx") * rows).astype(jnp.int32).reshape(1)
    doc_row = doc_start.reshape(1, rows)
    smem = pl.BlockSpec(memory_space=pltpu.SMEM)
    vmem = pl.BlockSpec(memory_space=pltpu.VMEM)
    hbm = pl.BlockSpec(memory_space=pltpu.HBM)
    anywhere = pl.BlockSpec(memory_space=pl.ANY)
    params = pltpu.CompilerParams(vmem_limit_bytes=40 * 1024 * 1024)
    shape = jax.ShapeDtypeStruct
    block_flops = 2 * HQ * rows * rows * HD
    arguments = [
        pltpu.with_memory_space_constraint(x[0], pltpu.HBM)
        for x in (query_heads, key_heads, value_heads, attn_output, output_grad)
    ]

    kv = pl.pallas_call(
        pack_kernel,
        in_specs=[hbm, hbm],
        out_specs=vmem,
        out_shape=shape((2, HK, rows, HD), BF16),
        scratch_shapes=[pltpu.SemaphoreType.DMA((2, HK))],
        compiler_params=params,
        cost_estimate=cost(0, 2**19),
        name="pack_keys",
    )(arguments[1], arguments[2])
    kv2 = from_behind(kv, "ctx", 2)
    kv1 = from_behind(kv, "ctx", 1)

    notes, qg, prob0, ds0, k_own_t, stat, half, cos, sin, cos1, sin1, cos2, sin2 = pl.pallas_call(
        own_kernel,
        in_specs=[smem, vmem, vmem] + [hbm] * 5,
        out_specs=[vmem] * 13,
        out_shape=[
            shape((8, QUAD * rows // 2), F32),
            shape((HK * TILES, QUAD * rows // 2, 2 * HD), BF16),
            shape((HK, rows, RATIO * rows), BF16),
            shape((HK, rows, RATIO * rows), BF16),
            shape((HK, HD, rows), BF16),
            shape((HK, 8, RATIO * rows), F32),
            shape((2, 2, HALF, QUAD * rows // 2), F32),
            shape((rows, HD), F32),
            shape((rows, HD), F32),
            shape((rows, HD), F32),
            shape((rows, HD), F32),
            shape((rows, HD), F32),
            shape((rows, HD), F32),
        ],
        scratch_shapes=[
            pltpu.VMEM((HK, rows, wide), BF16),
            pltpu.VMEM((HK, rows, HD), BF16),
            pltpu.VMEM((HK, rows, HD), BF16),
            pltpu.VMEM((HK, rows, wide), BF16),
            pltpu.VMEM((HK, rows, wide), BF16),
            pltpu.SemaphoreType.DMA((5, HK)),
        ],
        compiler_params=params,
        cost_estimate=cost(3 * block_flops, 9 * 2**20, HQ * rows * rows),
        name="own_block",
    )(first_row, *(pltpu.with_memory_space_constraint(x, pltpu.HBM) for x in (fetch_list, doc_row)), *arguments)

    results = [
        shape((1, rows, EARLY * RATIO * HD), BF16),
        shape((1, rows, (HK - EARLY) * RATIO * HD), BF16),
        shape((2, HK, rows, HD), BF16),
        shape((2, HK, rows, HD), BF16),
        shape((HK, 8, RATIO * rows), F32),
    ]
    *settled, prob1, ds1, dq1, stat1 = pl.pallas_call(
        near_kernel,
        in_specs=[vmem] * 9,
        out_specs=[vmem] * 9,
        out_shape=results
        + [
            shape((HK, rows, RATIO * rows), BF16),
            shape((HK, rows, RATIO * rows), BF16),
            shape((HK, HD, RATIO * rows), F32),
            shape((HK, 8, RATIO * rows), F32),
        ],
        compiler_params=params,
        cost_estimate=cost(5 * block_flops, 9 * 2**20, HQ * rows * rows),
        name="near_block",
    )(notes, qg, kv1, ds0, k_own_t, stat, half, cos1, sin1)

    dq_early, dq_late, ret2, ret1, scale = pl.pallas_call(
        far_kernel,
        in_specs=[vmem] * 15,
        out_specs=[vmem] * 5,
        out_shape=results,
        scratch_shapes=[
            pltpu.VMEM((FETCH * rows, RATIO * rows), BF16),
            pltpu.VMEM((FETCH * rows, RATIO * rows), BF16),
        ],
        input_output_aliases={10 + i: i for i in range(5)},
        compiler_params=params,
        cost_estimate=cost(5 * block_flops, 9 * 2**20, HQ * rows * rows),
        name="far_block",
    )(notes, qg, kv2, half, cos2, sin2, prob1, ds1, dq1, stat1, *settled)
    arrived1 = from_behind(ret1, "ctx", -1)
    arrived2 = from_behind(ret2, "ctx", -2)
    early = from_behind(dq_early, "section", -1)
    late = from_behind(dq_late, "section", -1)

    dk0, dv0 = pl.pallas_call(
        own_kv_kernel,
        in_specs=[vmem] * 4,
        out_specs=[vmem] * 2,
        out_shape=[shape((HK, rows, HD), F32), shape((HK, rows, HD), F32)],
        compiler_params=params,
        cost_estimate=cost(2 * block_flops, 5 * 2**20),
        name="own_keys",
    )(qg, prob0, ds0, scale)

    handed = pl.pallas_call(
        hand_kernel,
        in_specs=[anywhere],
        out_specs=hbm,
        out_shape=shape((1, rows, HQ * HD), BF16),
        scratch_shapes=[pltpu.SemaphoreType.DMA((2,))],
        compiler_params=params,
        cost_estimate=cost(0, 2 * 2**20),
        name="hand_on",
    )(early)

    key_grad, value_grad, handed_grad = pl.pallas_call(
        sum_kernel,
        in_specs=[vmem] * 4 + [anywhere] + [vmem] * 2 + [hbm],
        out_specs=[hbm] * 3,
        input_output_aliases={7: 2},
        out_shape=[
            shape((1, rows, kv_width), BF16),
            shape((1, rows, kv_width), BF16),
            shape((1, rows, HQ * HD), BF16),
        ],
        scratch_shapes=[
            pltpu.VMEM((1, rows, kv_width), BF16),
            pltpu.VMEM((1, rows, kv_width), BF16),
            pltpu.SemaphoreType.DMA((3,)),
        ],
        compiler_params=params,
        cost_estimate=cost(0, 3 * 2**20),
        name="sum_keys",
    )(dk0, dv0, arrived2, arrived1, late, cos, sin, handed)
    return (handed_grad, key_grad, value_grad)


def solution(mesh):
    return jax.shard_map(
        shards,
        mesh=mesh,
        in_specs=(
            P("section", "ctx", None),
            P("section", "ctx", None),
            P("section", "ctx", None),
            P("section", "ctx", None),
            P("section", "ctx", None),
            P("ctx"),
            P("ctx", None),
        ),
        out_specs=(P("section", "ctx", None), P("section", "ctx", None), P("section", "ctx", None)),
        check_vma=False,
    )
```

```python
import math

import jax
import jax.numpy as jnp
from jax import lax
from jax.experimental import pallas as pl
from jax.experimental.pallas import tpu as pltpu
from jax.sharding import PartitionSpec as P

HQ = 32
HK = 4
HD = 128
RATIO = HQ // HK
HALF = HD // 2
FETCH = 2
QUAD = 4
EARLY = 3
TILES = 4

ROPE_BASE = 1000000.0
TRAINED_CONTEXT = 32768.0
YARN_FACTOR = 4.0
NEG_LARGE = -1e30
SCORE_SCALE = HD ** (-0.5)
EXP2_SCALE = SCORE_SCALE / math.log(2.0)

F32 = jnp.float32
BF16 = jnp.bfloat16


def from_behind(value, axis, steps):
    count = lax.axis_size(axis)
    initial, last = (max(0, -steps), min(count, count - steps))
    return lax.ppermute(value, axis, [(source, source + steps) for source in range(initial, last)])


def dot_nn(left, right):
    return lax.dot_general(left, right, (((1,), (0,)), ((), ())), preferred_element_type=F32)


def dot_nt(left, right):
    return lax.dot_general(left, right, (((1,), (1,)), ((), ())), preferred_element_type=F32)


def frequencies(rows, columns):
    def correction(rotations):
        return HD * math.log(TRAINED_CONTEXT / (rotations * 2.0 * math.pi)) / (2.0 * math.log(ROPE_BASE))

    lower_dim = max(math.floor(correction(32.0)), 0)
    upper_dim = min(math.ceil(correction(1.0)), HD - 1)
    spread_dims = max(upper_dim - lower_dim, 0.001)
    indices = lax.broadcasted_iota(jnp.int32, (rows, columns), 0).astype(F32)
    extrapolated = jnp.exp(indices * F32(-2.0 / HD * math.log(ROPE_BASE)))
    ramp_weight = jnp.clip((indices - lower_dim) / spread_dims, 0.0, 1.0)
    return extrapolated / YARN_FACTOR * ramp_weight + extrapolated * (1.0 - ramp_weight)


def cos_sin(angles):
    turns = jnp.floor(angles * F32(2.0 / math.pi) + 0.5)
    rest = angles - turns * F32(1.5703125)
    rest = rest - turns * F32(4.837512969970703125e-4)
    rest = rest - turns * F32(7.54978995489188216e-8)
    square = rest * rest
    sine = rest + rest * square * (
        F32(-1.6666654611e-1) + square * (F32(8.3321608736e-3) + square * F32(-1.9515295891e-4))
    )
    cosine = (1.0 - 0.5 * square) + square * square * (
        F32(4.166664568298827e-2) + square * (F32(-1.388731625493765e-3) + square * F32(2.443315711809948e-5))
    )
    quarter = turns.astype(jnp.int32)
    swapped = (quarter & 1) == 1
    cos_value = jnp.where(swapped, sine, cosine)
    sin_value = jnp.where(swapped, cosine, sine)
    cos_value = jnp.where(((quarter + 1) & 2) == 2, -cos_value, cos_value)
    sin_value = jnp.where((quarter & 2) == 2, -sin_value, sin_value)
    return cos_value, sin_value


def half_tables(positions):
    factor = 0.1 * math.log(YARN_FACTOR) + 1.0
    cos_t, sin_t = cos_sin(frequencies(HALF, positions.shape[1]) * positions.astype(F32))
    return cos_t * factor, sin_t * factor


def shifted_tables(tables, shift):
    cos_t, sin_t = tables
    cos_s, sin_s = cos_sin(frequencies(HALF, cos_t.shape[1]) * F32(shift))
    return cos_t * cos_s + sin_t * sin_s, sin_t * cos_s - cos_t * sin_s


def upright(cos_t, sin_t):
    cosine = jnp.concatenate([cos_t, cos_t], axis=0).T
    signed_sine = jnp.concatenate([sin_t, -sin_t], axis=0).T
    return cosine, signed_sine


def rotate(values, cosine, signed_sine):
    return values * cosine - pltpu.roll(values, HALF, 1) * signed_sine


def unrotate(values, cosine, signed_sine):
    return values * cosine + pltpu.roll(values, HALF, 1) * signed_sine


def head_columns(head):
    return slice(head * HD, (head + 1) * HD)


def stack_heads(ref, group, first, half):
    rows = ref.shape[1] // 2
    at = slice(half * rows, (half + 1) * rows)
    return jnp.concatenate([ref[group, at, head_columns(first + i)] for i in range(QUAD)], axis=0)


def four_times(value, half):
    columns = value.shape[1] // 2
    return jnp.concatenate([value[:, half * columns : (half + 1) * columns]] * QUAD, axis=1)


def block_diagonal(upper, lower):
    zero = jnp.zeros_like(upper)
    return jnp.concatenate(
        [jnp.concatenate([upper, zero], axis=1), jnp.concatenate([zero, lower], axis=1)], axis=0
    )


def group_rows(ref, group, columns, tiles=TILES):
    return jnp.concatenate([ref[group * TILES + i, :, columns] for i in range(tiles)], axis=0)


def tile_columns(tile):
    width = RATIO * HD // TILES
    return slice(tile * width, (tile + 1) * width)


def pack_kernel(k_hbm, v_hbm, kv_ref, arrived):
    copies = [
        pltpu.make_async_copy(source.at[:, head_columns(group)], kv_ref.at[which, group], arrived.at[which, group])
        for which, source in enumerate((k_hbm, v_hbm))
        for group in range(HK)
    ]
    for copy in copies:
        copy.start()
    for copy in copies:
        copy.wait()


def own_kernel(
    first_ref, list_ref, doc_ref, q_hbm, k_hbm, v_hbm, o_hbm, g_hbm,
    notes_ref, qg_ref, prob_ref, ds_ref, kt_ref, stat_ref, half_ref, cos_ref, sin_ref, cos1_ref, sin1_ref, cos2_ref, sin2_ref,
    q_ref, k_ref, v_ref, o_ref, g_ref, arrived,
):
    rows = q_hbm.shape[0]
    arguments = ((k_hbm, k_ref), (q_hbm, q_ref), (v_hbm, v_ref), (g_hbm, g_ref), (o_hbm, o_ref))

    def fetch(which, group):
        source, buffer = arguments[which]
        width = buffer.shape[2]
        columns = pl.ds(pl.multiple_of(group * width, width), width)
        return pltpu.make_async_copy(source.at[:, columns], buffer.at[group], arrived.at[which, group])

    for group in range(HK):
        for which in range(len(arguments)):
            fetch(which, group).start()

    doc_row = doc_ref[...] - first_ref[0]
    columns = lax.broadcasted_iota(jnp.int32, (1, rows), 1)
    cos_t, sin_t = half_tables(columns - doc_row)
    cos_ref[...], sin_ref[...] = upright(cos_t, sin_t)
    reach = doc_row[:, 0:1]
    lanes = notes_ref.shape[1]
    for half in range(2):
        notes_ref[half : half + 1, :] = four_times(doc_row.astype(F32), half)
        half_ref[half, 0] = four_times(cos_t * SCORE_SCALE, half)
        half_ref[half, 1] = four_times(sin_t * SCORE_SCALE, half)
    for distance in range(1, FETCH + 1):
        listed = jnp.where(list_ref[:, distance - 1 : distance] == 1, 1.0, 0.0)
        notes_ref[distance + 1 : distance + 2, :] = jnp.broadcast_to(listed, (1, lanes))
    near_tables = half_tables(columns - rows - reach)
    cos1_ref[...], sin1_ref[...] = upright(*near_tables)
    cos2_ref[...], sin2_ref[...] = upright(*shifted_tables(near_tables, rows))
    key_idx = lax.broadcasted_iota(jnp.int32, (rows, rows), 0)
    query_idx = lax.broadcasted_iota(jnp.int32, (rows, rows), 1)
    mask = (key_idx <= query_idx) & (key_idx >= doc_row)
    bias = jnp.where(mask, 0.0, NEG_LARGE)
    bias = [four_times(bias, half) for half in range(2)]

    @pl.loop(0, HK)
    def _(group):
        for which in range(len(arguments)):
            fetch(which, group).wait()
        k_rot = rotate(k_ref[group].astype(F32), cos_ref[...], sin_ref[...])
        kt_ref[group] = k_rot.T.astype(BF16)
        left = block_diagonal(k_rot.astype(BF16), v_ref[group])

        def products(tile):
            half, quad = divmod(tile, 2)
            at = slice(half * rows // 2, (half + 1) * rows // 2)
            cosine = jnp.concatenate([cos_ref[at, :]] * QUAD, axis=0)
            signed_sine = jnp.concatenate([sin_ref[at, :]] * QUAD, axis=0)
            queries = stack_heads(q_ref, group, quad * QUAD, half).astype(F32)
            qg_ref[group * TILES + tile, :, :HD] = rotate(queries, cosine, signed_sine).astype(BF16)
            grads = stack_heads(g_ref, group, quad * QUAD, half)
            qg_ref[group * TILES + tile, :, HD:] = grads
            outputs = stack_heads(o_ref, group, quad * QUAD, half)
            delta = jnp.sum(grads.T.astype(F32) * outputs.T.astype(F32), axis=0, keepdims=True)
            both = dot_nt(left, qg_ref[group * TILES + tile])
            return both[:rows], both[rows:], delta

        def finish(tile, scores, dprob, delta):
            at = tile_columns(tile)
            scores = scores + bias[tile // 2]
            largest = jnp.max(scores, axis=0, keepdims=True)
            prob = jnp.exp2((scores - largest) * EXP2_SCALE)
            prob_ref[group, :, at] = prob.astype(BF16)
            ds_ref[group, :, at] = (prob * (dprob - delta)).astype(BF16)
            stat_ref[group, 0:1, at] = largest
            stat_ref[group, 1:2, at] = jnp.sum(prob, axis=0, keepdims=True)
            stat_ref[group, 2:3, at] = delta

        ahead = products(0)
        for tile in range(TILES):
            now = ahead
            if tile + 1 < TILES:
                ahead = products(tile + 1)
            finish(tile, *now)


def reach_bias(notes_ref, distance, rows):
    key_idx = lax.broadcasted_iota(jnp.int32, (rows, notes_ref.shape[1]), 0).astype(F32) - distance * rows
    listed = notes_ref[distance + 1 : distance + 2, 0:1]
    return jnp.where((key_idx >= notes_ref[0:1, 0:1]) & (listed > 0.0), 0.0, NEG_LARGE)


def reached(notes_ref):
    return [notes_ref[half : half + 1, :] == notes_ref[0:1, 0:1] for half in range(2)]


def high_reached(notes_ref):
    return jnp.max(jnp.where(notes_ref[1:2, :] == notes_ref[0:1, 0:1], 1.0, 0.0)) > 0.0


def goes_on(notes_ref):
    return jnp.max(notes_ref[3:4, :]) > 0.0


def softmax_step(scores, stat_ref, group, at, in_reach):
    before = stat_ref[group, 0:1, at]
    largest = jnp.maximum(before, jnp.max(scores, axis=0, keepdims=True))
    prob = jnp.exp2((scores - jnp.where(in_reach, largest, -NEG_LARGE)) * EXP2_SCALE)
    largest = jnp.where(in_reach, largest, before)
    scale = jnp.exp2((before - largest) * EXP2_SCALE)
    total = stat_ref[group, 1:2, at] * scale + jnp.sum(prob, axis=0, keepdims=True)
    return prob, largest, total, scale


def staged(tiles, products, middle, finish):
    ahead = products(0)
    behind = None
    for tile in range(tiles):
        now = ahead
        if tile + 1 < tiles:
            ahead = products(tile + 1)
        done = middle(tile, *now)
        if behind is not None:
            finish(tile - 1, behind)
        behind = done
    finish(tiles - 1, behind)


def store_query_grad(dq_refs, group, tile, dq, half_ref):
    part, group = divmod(group, EARLY)
    dq_ref = dq_refs[part]
    half, quad = divmod(tile, 2)
    rows = dq_ref.shape[1] // 2
    cos_t, sin_t = half_ref[half, 0], half_ref[half, 1]
    upper, lower = dq[:HALF], dq[HALF:]
    dq = jnp.concatenate([upper * cos_t + lower * sin_t, lower * cos_t - upper * sin_t], axis=0).astype(BF16)
    dq = dq.T
    for i in range(QUAD):
        head = group * RATIO + quad * QUAD + i
        dq_ref[0, half * rows : (half + 1) * rows, head_columns(head)] = dq[i * rows : (i + 1) * rows]


def own_alone(dq_refs, scale_ref, ds0_ref, kt0_ref, stat_ref, half_ref, group, tiles):
    for tile in tiles:
        at = tile_columns(tile)
        scale = 1.0 / stat_ref[group, 1:2, at]
        scale_ref[group, 0:1, at] = scale
        dscore = ds0_ref[group, :, at] * scale.astype(BF16)
        store_query_grad(dq_refs, group, tile, dot_nn(kt0_ref[group], dscore), half_ref)


def key_products(qg_ref, group, tiles, dscore, prob):
    rows = dscore.shape[0]
    both = dot_nn(jnp.concatenate([dscore, prob], axis=0), group_rows(qg_ref, group, slice(2 * HD), tiles))
    return (both[:rows, :HD] * SCORE_SCALE).astype(BF16), both[rows:, HD:].astype(BF16)


def near_kernel(
    notes_ref, qg_ref, kv_ref, ds0_ref, kt0_ref, stat_ref, half_ref, cos_ref, sin_ref,
    dqa_ref, dqb_ref, ret2_ref, ret1_ref, scale_ref, prob_ref, ds_ref, kt_ref, next_ref,
):
    dq_refs = (dqa_ref, dqb_ref)
    rows = kv_ref.shape[2]

    def attend(last, tiles):
        in_reach = reached(notes_ref)
        bias = reach_bias(notes_ref, 1, rows)
        for group in range(HK):
            one_group(last, tiles, in_reach, bias, group)

    def one_group(last, tiles, in_reach, bias, group):
        k_rot = rotate(kv_ref[0, group].astype(F32), cos_ref[...], sin_ref[...])
        k_rot_t = k_rot.T.astype(BF16)
        left = block_diagonal(k_rot.astype(BF16), kv_ref[1, group])
        both_t = jnp.concatenate([k_rot_t, kt0_ref[group]], axis=1)

        def products(tile):
            both = dot_nt(left, qg_ref[group * TILES + tile])
            return both[:rows], both[rows:]

        def middle(tile, scores, dprob):
            at = tile_columns(tile)
            prob, largest, total, scale = softmax_step(scores + bias, stat_ref, group, at, in_reach[tile // 2])
            delta = stat_ref[group, 2:3, at]
            if last:
                inverse = 1.0 / total
                scale = scale * inverse
                prob = prob * inverse
                scale_ref[group, 0:1, at] = scale
            prob = prob.astype(BF16)
            dscore = prob * (dprob - delta).astype(BF16)
            prob_ref[group, :, at] = prob
            ds_ref[group, :, at] = dscore
            if last:
                own_dscore = ds0_ref[group, :, at] * scale.astype(BF16)
                return jnp.concatenate([dscore, own_dscore], axis=0)
            next_ref[group, 0:1, at] = largest
            next_ref[group, 1:2, at] = total
            next_ref[group, 2:3, at] = delta
            next_ref[group, 3:4, at] = scale
            return None

        def finish(tile, dscore):
            if last:
                store_query_grad(dq_refs, group, tile, dot_nn(both_t, dscore), half_ref)

        staged(tiles, products, middle, finish)
        if last:
            own_alone(
                dq_refs, scale_ref, ds0_ref, kt0_ref, stat_ref, half_ref, group, range(tiles, TILES)
            )
            used = slice(0, tile_columns(tiles - 1).stop)
            grads = key_products(qg_ref, group, tiles, ds_ref[group, :, used], prob_ref[group, :, used])
            for which, grad in enumerate(grads):
                ret1_ref[which, group] = grad
                ret2_ref[which, group] = jnp.zeros((rows, HD), BF16)
        else:
            kt_ref[group] = k_rot_t
            for tile in range(tiles, TILES):
                next_ref[group, 1:2, tile_columns(tile)] = stat_ref[group, 1:2, tile_columns(tile)]

    further, wide = goes_on(notes_ref), high_reached(notes_ref)
    for last in (True, False):
        for tiles in (TILES // 2, TILES):
            chosen = (further != last) & (wide == (tiles == TILES))
            pl.when(chosen)(lambda last=last, tiles=tiles: attend(last, tiles))


def far_kernel(
    notes_ref, qg_ref, kv_ref, ds0_ref, kt0_ref, half_ref, cos_ref, sin_ref,
    prob1_ref, ds1_ref, kt1_ref, stat_ref, *refs,
):
    *dq_refs, ret2_ref, ret1_ref, scale_ref, prob_buf, ds_buf = refs[5:]
    rows = kv_ref.shape[2]

    def attend(skipped, tiles):
        in_reach = reached(notes_ref)
        bias = reach_bias(notes_ref, 2, rows)[skipped:]
        for group in range(HK):
            one_group(skipped, tiles, in_reach, bias, group)

    def one_group(skipped, tiles, in_reach, bias, group):
        used = rows - skipped
        k_rot = rotate(kv_ref[0, group, skipped:, :].astype(F32), cos_ref[skipped:, :], sin_ref[skipped:, :])
        left = block_diagonal(k_rot.astype(BF16), kv_ref[1, group, skipped:, :])
        k_rot_t = k_rot.T.astype(BF16)
        near_t = jnp.concatenate([kt1_ref[group], kt0_ref[group]], axis=1)

        def products(tile):
            both = dot_nt(left, qg_ref[group * TILES + tile])
            return both[:used], both[used:]

        def middle(tile, scores, dprob):
            at = tile_columns(tile)
            prob, _, total, scale = softmax_step(scores + bias, stat_ref, group, at, in_reach[tile // 2])
            inverse = 1.0 / total
            near_scale = scale * inverse
            own_scale = near_scale * stat_ref[group, 3:4, at]
            scale_ref[group, 0:1, at] = own_scale
            prob = (prob * inverse).astype(BF16)
            dscore = prob * (dprob - stat_ref[group, 2:3, at]).astype(BF16)
            near_scale = near_scale.astype(BF16)
            near_dscore = ds1_ref[group, :, at] * near_scale
            own_dscore = ds0_ref[group, :, at] * own_scale.astype(BF16)
            prob_buf[:used, at] = prob
            prob_buf[used : used + rows, at] = prob1_ref[group, :, at] * near_scale
            ds_buf[:used, at] = dscore
            ds_buf[used : used + rows, at] = near_dscore
            return dscore, jnp.concatenate([near_dscore, own_dscore], axis=0)

        def finish(tile, dscores):
            dq = dot_nn(near_t, dscores[1]) + dot_nn(k_rot_t, dscores[0])
            store_query_grad(dq_refs, group, tile, dq, half_ref)

        staged(tiles, products, middle, finish)
        own_alone(
            dq_refs, scale_ref, ds0_ref, kt0_ref, stat_ref, half_ref, group, range(tiles, TILES)
        )
        columns = slice(0, tile_columns(tiles - 1).stop)
        grads = key_products(qg_ref, group, tiles, ds_buf[: used + rows, columns], prob_buf[: used + rows, columns])
        for which, grad in enumerate(grads):
            ret1_ref[which, group] = grad[used:]
            ret2_ref[which, group, skipped:, :] = grad[:used]
            if skipped:
                ret2_ref[which, group, :skipped, :] = jnp.zeros((skipped, HD), BF16)

    @pl.when(goes_on(notes_ref))
    def _():
        wide = high_reached(notes_ref)
        pl.when(wide)(lambda: attend(rows // 2, TILES))
        pl.when(jnp.logical_not(wide))(lambda: attend(0, TILES // 2))


def own_kv_kernel(qg_ref, prob_ref, ds_ref, scale_ref, dk_ref, dv_ref):
    @pl.loop(0, HK)
    def _(group):
        scale = scale_ref[group, 0:1, :]
        prob = (prob_ref[group].astype(F32) * scale).astype(BF16)
        dscore = (ds_ref[group].astype(F32) * scale).astype(BF16)
        dk_ref[group] = dot_nn(dscore, group_rows(qg_ref, group, slice(HD))) * SCORE_SCALE
        dv_ref[group] = dot_nn(prob, group_rows(qg_ref, group, slice(HD, 2 * HD)))


def hand_kernel(dq_ref, handed_hbm, copied):
    rows, width = dq_ref.shape[1:]
    copies = []
    for i in range(2):
        at = pl.ds(i * rows // 2, rows // 2)
        copies.append(pltpu.make_async_copy(dq_ref.at[:, at], handed_hbm.at[:, at, pl.ds(0, width)], copied.at[i]))
    for copy in copies:
        copy.start()
    for copy in copies:
        copy.wait()


def sum_kernel(
    dk_ref, dv_ref, ret2_ref, ret1_ref, late_ref, cos_ref, sin_ref, handed_in,
    key_hbm, value_hbm, handed_hbm, key_buf, value_buf, copied,
):
    del handed_in
    width = late_ref.shape[2]
    rest = pl.ds(handed_hbm.shape[2] - width, width)
    copies = [pltpu.make_async_copy(late_ref, handed_hbm.at[:, :, rest], copied.at[0])]
    copies[0].start()
    for group in range(HK):
        at = head_columns(group)
        dv = dv_ref[group] + ret1_ref[1, group].astype(F32) + ret2_ref[1, group].astype(F32)
        value_buf[0, :, at] = dv.astype(BF16)
    copies.append(pltpu.make_async_copy(value_buf, value_hbm, copied.at[1]))
    copies[-1].start()
    for group in range(HK):
        at = head_columns(group)
        dk = dk_ref[group] + ret1_ref[0, group].astype(F32) + ret2_ref[0, group].astype(F32)
        key_buf[0, :, at] = unrotate(dk, cos_ref[...], sin_ref[...]).astype(BF16)
    copies.append(pltpu.make_async_copy(key_buf, key_hbm, copied.at[2]))
    copies[-1].start()
    for copy in copies:
        copy.wait()


def cost(flops, moved, exps=0):
    return pl.CostEstimate(flops=int(flops), bytes_accessed=int(moved), transcendentals=int(exps))


def shards(query_heads, key_heads, value_heads, attn_output, output_grad, doc_start, fetch_list):
    rows = query_heads.shape[1]
    wide = RATIO * HD
    kv_width = HK * HD
    first_row = (lax.axis_index("ctx") * rows).astype(jnp.int32).reshape(1)
    doc_row = doc_start.reshape(1, rows)
    smem = pl.BlockSpec(memory_space=pltpu.SMEM)
    vmem = pl.BlockSpec(memory_space=pltpu.VMEM)
    hbm = pl.BlockSpec(memory_space=pltpu.HBM)
    anywhere = pl.BlockSpec(memory_space=pl.ANY)
    params = pltpu.CompilerParams(vmem_limit_bytes=40 * 1024 * 1024)
    shape = jax.ShapeDtypeStruct
    block_flops = 2 * HQ * rows * rows * HD
    arguments = [
        pltpu.with_memory_space_constraint(x[0], pltpu.HBM)
        for x in (query_heads, key_heads, value_heads, attn_output, output_grad)
    ]

    kv = pl.pallas_call(
        pack_kernel,
        in_specs=[hbm, hbm],
        out_specs=vmem,
        out_shape=shape((2, HK, rows, HD), BF16),
        scratch_shapes=[pltpu.SemaphoreType.DMA((2, HK))],
        compiler_params=params,
        cost_estimate=cost(0, 2**19),
        name="pack_keys",
    )(arguments[1], arguments[2])
    kv2 = from_behind(kv, "ctx", 2)
    kv1 = from_behind(kv, "ctx", 1)

    notes, qg, prob0, ds0, k_own_t, stat, half, cos, sin, cos1, sin1, cos2, sin2 = pl.pallas_call(
        own_kernel,
        in_specs=[smem, vmem, vmem] + [hbm] * 5,
        out_specs=[vmem] * 13,
        out_shape=[
            shape((8, QUAD * rows // 2), F32),
            shape((HK * TILES, QUAD * rows // 2, 2 * HD), BF16),
            shape((HK, rows, RATIO * rows), BF16),
            shape((HK, rows, RATIO * rows), BF16),
            shape((HK, HD, rows), BF16),
            shape((HK, 8, RATIO * rows), F32),
            shape((2, 2, HALF, QUAD * rows // 2), F32),
            shape((rows, HD), F32),
            shape((rows, HD), F32),
            shape((rows, HD), F32),
            shape((rows, HD), F32),
            shape((rows, HD), F32),
            shape((rows, HD), F32),
        ],
        scratch_shapes=[
            pltpu.VMEM((HK, rows, wide), BF16),
            pltpu.VMEM((HK, rows, HD), BF16),
            pltpu.VMEM((HK, rows, HD), BF16),
            pltpu.VMEM((HK, rows, wide), BF16),
            pltpu.VMEM((HK, rows, wide), BF16),
            pltpu.SemaphoreType.DMA((5, HK)),
        ],
        compiler_params=params,
        cost_estimate=cost(3 * block_flops, 9 * 2**20, HQ * rows * rows),
        name="own_block",
    )(first_row, *(pltpu.with_memory_space_constraint(x, pltpu.HBM) for x in (fetch_list, doc_row)), *arguments)

    results = [
        shape((1, rows, EARLY * RATIO * HD), BF16),
        shape((1, rows, (HK - EARLY) * RATIO * HD), BF16),
        shape((2, HK, rows, HD), BF16),
        shape((2, HK, rows, HD), BF16),
        shape((HK, 8, RATIO * rows), F32),
    ]
    *settled, prob1, ds1, k_near_t, stat1 = pl.pallas_call(
        near_kernel,
        in_specs=[vmem] * 9,
        out_specs=[vmem] * 9,
        out_shape=results
        + [
            shape((HK, rows, RATIO * rows), BF16),
            shape((HK, rows, RATIO * rows), BF16),
            shape((HK, HD, rows), BF16),
            shape((HK, 8, RATIO * rows), F32),
        ],
        compiler_params=params,
        cost_estimate=cost(5 * block_flops, 9 * 2**20, HQ * rows * rows),
        name="near_block",
    )(notes, qg, kv1, ds0, k_own_t, stat, half, cos1, sin1)

    dq_early, dq_late, ret2, ret1, scale = pl.pallas_call(
        far_kernel,
        in_specs=[vmem] * 17,
        out_specs=[vmem] * 5,
        out_shape=results,
        scratch_shapes=[
            pltpu.VMEM((FETCH * rows, RATIO * rows), BF16),
            pltpu.VMEM((FETCH * rows, RATIO * rows), BF16),
        ],
        input_output_aliases={12 + i: i for i in range(5)},
        compiler_params=params,
        cost_estimate=cost(5 * block_flops, 9 * 2**20, HQ * rows * rows),
        name="far_block",
    )(notes, qg, kv2, ds0, k_own_t, half, cos2, sin2, prob1, ds1, k_near_t, stat1, *settled)
    arrived1 = from_behind(ret1, "ctx", -1)
    arrived2 = from_behind(ret2, "ctx", -2)
    early = from_behind(dq_early, "section", -1)
    late = from_behind(dq_late, "section", -1)

    dk0, dv0 = pl.pallas_call(
        own_kv_kernel,
        in_specs=[vmem] * 4,
        out_specs=[vmem] * 2,
        out_shape=[shape((HK, rows, HD), F32), shape((HK, rows, HD), F32)],
        compiler_params=params,
        cost_estimate=cost(2 * block_flops, 5 * 2**20),
        name="own_keys",
    )(qg, prob0, ds0, scale)

    handed = pl.pallas_call(
        hand_kernel,
        in_specs=[anywhere],
        out_specs=hbm,
        out_shape=shape((1, rows, HQ * HD), BF16),
        scratch_shapes=[pltpu.SemaphoreType.DMA((2,))],
        compiler_params=params,
        cost_estimate=cost(0, 2 * 2**20),
        name="hand_on",
    )(early)

    key_grad, value_grad, handed_grad = pl.pallas_call(
        sum_kernel,
        in_specs=[vmem] * 4 + [anywhere] + [vmem] * 2 + [hbm],
        out_specs=[hbm] * 3,
        input_output_aliases={7: 2},
        out_shape=[
            shape((1, rows, kv_width), BF16),
            shape((1, rows, kv_width), BF16),
            shape((1, rows, HQ * HD), BF16),
        ],
        scratch_shapes=[
            pltpu.VMEM((1, rows, kv_width), BF16),
            pltpu.VMEM((1, rows, kv_width), BF16),
            pltpu.SemaphoreType.DMA((3,)),
        ],
        compiler_params=params,
        cost_estimate=cost(0, 3 * 2**20),
        name="sum_keys",
    )(dk0, dv0, arrived2, arrived1, late, cos, sin, handed)
    return (handed_grad, key_grad, value_grad)


def solution(mesh):
    return jax.shard_map(
        shards,
        mesh=mesh,
        in_specs=(
            P("section", "ctx", None),
            P("section", "ctx", None),
            P("section", "ctx", None),
            P("section", "ctx", None),
            P("section", "ctx", None),
            P("ctx"),
            P("ctx", None),
        ),
        out_specs=(P("section", "ctx", None), P("section", "ctx", None), P("section", "ctx", None)),
        check_vma=False,
    )
```

```python
import math

import jax
import jax.numpy as jnp
from jax import lax
from jax.experimental import pallas as pl
from jax.experimental.pallas import tpu as pltpu
from jax.sharding import PartitionSpec as P

HQ = 32
HK = 4
HD = 128
RATIO = HQ // HK
HALF = HD // 2
FETCH = 2
QUAD = 4
EARLY = 3
TILES = 4

ROPE_BASE = 1000000.0
TRAINED_CONTEXT = 32768.0
YARN_FACTOR = 4.0
NEG_LARGE = -1e30
SCORE_SCALE = HD ** (-0.5)
EXP2_SCALE = SCORE_SCALE / math.log(2.0)

F32 = jnp.float32
BF16 = jnp.bfloat16


def from_behind(value, axis, steps):
    count = lax.axis_size(axis)
    initial, last = (max(0, -steps), min(count, count - steps))
    return lax.ppermute(value, axis, [(source, source + steps) for source in range(initial, last)])


def dot_nn(left, right):
    return lax.dot_general(left, right, (((1,), (0,)), ((), ())), preferred_element_type=F32)


def dot_nt(left, right):
    return lax.dot_general(left, right, (((1,), (1,)), ((), ())), preferred_element_type=F32)


def frequencies(rows, columns):
    def correction(rotations):
        return HD * math.log(TRAINED_CONTEXT / (rotations * 2.0 * math.pi)) / (2.0 * math.log(ROPE_BASE))

    lower_dim = max(math.floor(correction(32.0)), 0)
    upper_dim = min(math.ceil(correction(1.0)), HD - 1)
    spread_dims = max(upper_dim - lower_dim, 0.001)
    indices = lax.broadcasted_iota(jnp.int32, (rows, columns), 0).astype(F32)
    extrapolated = jnp.exp(indices * F32(-2.0 / HD * math.log(ROPE_BASE)))
    ramp_weight = jnp.clip((indices - lower_dim) / spread_dims, 0.0, 1.0)
    return extrapolated / YARN_FACTOR * ramp_weight + extrapolated * (1.0 - ramp_weight)


def cos_sin(angles):
    turns = jnp.floor(angles * F32(2.0 / math.pi) + 0.5)
    rest = angles - turns * F32(1.5703125)
    rest = rest - turns * F32(4.837512969970703125e-4)
    rest = rest - turns * F32(7.54978995489188216e-8)
    square = rest * rest
    sine = rest + rest * square * (
        F32(-1.6666654611e-1) + square * (F32(8.3321608736e-3) + square * F32(-1.9515295891e-4))
    )
    cosine = (1.0 - 0.5 * square) + square * square * (
        F32(4.166664568298827e-2) + square * (F32(-1.388731625493765e-3) + square * F32(2.443315711809948e-5))
    )
    quarter = turns.astype(jnp.int32)
    swapped = (quarter & 1) == 1
    cos_value = jnp.where(swapped, sine, cosine)
    sin_value = jnp.where(swapped, cosine, sine)
    cos_value = jnp.where(((quarter + 1) & 2) == 2, -cos_value, cos_value)
    sin_value = jnp.where((quarter & 2) == 2, -sin_value, sin_value)
    return cos_value, sin_value


def half_tables(positions):
    factor = 0.1 * math.log(YARN_FACTOR) + 1.0
    cos_t, sin_t = cos_sin(frequencies(HALF, positions.shape[1]) * positions.astype(F32))
    return cos_t * factor, sin_t * factor


def shifted_tables(tables, shift):
    cos_t, sin_t = tables
    cos_s, sin_s = cos_sin(frequencies(HALF, cos_t.shape[1]) * F32(shift))
    return cos_t * cos_s + sin_t * sin_s, sin_t * cos_s - cos_t * sin_s


def upright(cos_t, sin_t):
    cosine = jnp.concatenate([cos_t, cos_t], axis=0).T
    signed_sine = jnp.concatenate([sin_t, -sin_t], axis=0).T
    return cosine, signed_sine


def rotate(values, cosine, signed_sine):
    return values * cosine - pltpu.roll(values, HALF, 1) * signed_sine


def unrotate(values, cosine, signed_sine):
    return values * cosine + pltpu.roll(values, HALF, 1) * signed_sine


def head_columns(head):
    return slice(head * HD, (head + 1) * HD)


def stack_heads(ref, group, first, half):
    rows = ref.shape[1] // 2
    at = slice(half * rows, (half + 1) * rows)
    return jnp.concatenate([ref[group, at, head_columns(first + i)] for i in range(QUAD)], axis=0)


def four_times(value, half):
    columns = value.shape[1] // 2
    return jnp.concatenate([value[:, half * columns : (half + 1) * columns]] * QUAD, axis=1)


def block_diagonal(upper, lower):
    zero = jnp.zeros_like(upper)
    return jnp.concatenate(
        [jnp.concatenate([upper, zero], axis=1), jnp.concatenate([zero, lower], axis=1)], axis=0
    )


def group_rows(ref, group, columns, tiles=TILES):
    return jnp.concatenate([ref[group * TILES + i, :, columns] for i in range(tiles)], axis=0)


def tile_columns(tile):
    width = RATIO * HD // TILES
    return slice(tile * width, (tile + 1) * width)


def pack_kernel(k_hbm, v_hbm, kv_ref, arrived):
    copies = [
        pltpu.make_async_copy(source.at[:, head_columns(group)], kv_ref.at[which, group], arrived.at[which, group])
        for which, source in enumerate((k_hbm, v_hbm))
        for group in range(HK)
    ]
    for copy in copies:
        copy.start()
    for copy in copies:
        copy.wait()


def own_kernel(
    first_ref, list_ref, doc_ref, q_hbm, k_hbm, v_hbm, o_hbm, g_hbm,
    notes_ref, qg_ref, prob_ref, ds_ref, kt_ref, stat_ref, half_ref, cos_ref, sin_ref, cos1_ref, sin1_ref, cos2_ref, sin2_ref,
    q_ref, k_ref, v_ref, o_ref, g_ref, arrived,
):
    rows = q_hbm.shape[0]
    arguments = ((k_hbm, k_ref), (q_hbm, q_ref), (v_hbm, v_ref), (g_hbm, g_ref), (o_hbm, o_ref))

    def fetch(which, group):
        source, buffer = arguments[which]
        width = buffer.shape[2]
        columns = pl.ds(pl.multiple_of(group * width, width), width)
        return pltpu.make_async_copy(source.at[:, columns], buffer.at[group], arrived.at[which, group])

    for group in range(HK):
        for which in range(len(arguments)):
            fetch(which, group).start()

    doc_row = doc_ref[...] - first_ref[0]
    columns = lax.broadcasted_iota(jnp.int32, (1, rows), 1)
    cos_t, sin_t = half_tables(columns - doc_row)
    cos_ref[...], sin_ref[...] = upright(cos_t, sin_t)
    reach = doc_row[:, 0:1]
    lanes = notes_ref.shape[1]
    for half in range(2):
        notes_ref[half : half + 1, :] = four_times(doc_row.astype(F32), half)
        half_ref[half, 0] = four_times(cos_t * SCORE_SCALE, half)
        half_ref[half, 1] = four_times(sin_t * SCORE_SCALE, half)
    for distance in range(1, FETCH + 1):
        listed = jnp.where(list_ref[:, distance - 1 : distance] == 1, 1.0, 0.0)
        notes_ref[distance + 1 : distance + 2, :] = jnp.broadcast_to(listed, (1, lanes))
    near_tables = half_tables(columns - rows - reach)
    cos1_ref[...], sin1_ref[...] = upright(*near_tables)
    cos2_ref[...], sin2_ref[...] = upright(*shifted_tables(near_tables, rows))
    key_idx = lax.broadcasted_iota(jnp.int32, (rows, rows), 0)
    query_idx = lax.broadcasted_iota(jnp.int32, (rows, rows), 1)
    mask = (key_idx <= query_idx) & (key_idx >= doc_row)
    bias = jnp.where(mask, 0.0, NEG_LARGE)
    bias = [four_times(bias, half) for half in range(2)]

    @pl.loop(0, HK)
    def _(group):
        for which in range(len(arguments)):
            fetch(which, group).wait()
        k_rot = rotate(k_ref[group].astype(F32), cos_ref[...], sin_ref[...])
        kt_ref[group] = k_rot.T.astype(BF16)
        left = block_diagonal(k_rot.astype(BF16), v_ref[group])

        def products(tile):
            half, quad = divmod(tile, 2)
            at = slice(half * rows // 2, (half + 1) * rows // 2)
            cosine = jnp.concatenate([cos_ref[at, :]] * QUAD, axis=0)
            signed_sine = jnp.concatenate([sin_ref[at, :]] * QUAD, axis=0)
            queries = stack_heads(q_ref, group, quad * QUAD, half).astype(F32)
            qg_ref[group * TILES + tile, :, :HD] = rotate(queries, cosine, signed_sine).astype(BF16)
            grads = stack_heads(g_ref, group, quad * QUAD, half)
            qg_ref[group * TILES + tile, :, HD:] = grads
            outputs = stack_heads(o_ref, group, quad * QUAD, half)
            delta = jnp.sum(grads.T.astype(F32) * outputs.T.astype(F32), axis=0, keepdims=True)
            both = dot_nt(left, qg_ref[group * TILES + tile])
            return both[:rows], both[rows:], delta

        def finish(tile, scores, dprob, delta):
            at = tile_columns(tile)
            scores = scores + bias[tile // 2]
            largest = jnp.max(scores, axis=0, keepdims=True)
            prob = jnp.exp2((scores - largest) * EXP2_SCALE)
            prob_ref[group, :, at] = prob.astype(BF16)
            ds_ref[group, :, at] = (prob * (dprob - delta)).astype(BF16)
            stat_ref[group, 0:1, at] = largest
            stat_ref[group, 1:2, at] = jnp.sum(prob, axis=0, keepdims=True)
            stat_ref[group, 2:3, at] = delta

        ahead = products(0)
        for tile in range(TILES):
            now = ahead
            if tile + 1 < TILES:
                ahead = products(tile + 1)
            finish(tile, *now)


def reach_bias(notes_ref, distance, rows):
    key_idx = lax.broadcasted_iota(jnp.int32, (rows, notes_ref.shape[1]), 0).astype(F32) - distance * rows
    listed = notes_ref[distance + 1 : distance + 2, 0:1]
    return jnp.where((key_idx >= notes_ref[0:1, 0:1]) & (listed > 0.0), 0.0, NEG_LARGE)


def reached(notes_ref):
    return [notes_ref[half : half + 1, :] == notes_ref[0:1, 0:1] for half in range(2)]


def high_reached(notes_ref):
    return jnp.max(jnp.where(notes_ref[1:2, :] == notes_ref[0:1, 0:1], 1.0, 0.0)) > 0.0


def goes_on(notes_ref):
    return jnp.max(notes_ref[3:4, :]) > 0.0


def softmax_step(scores, stat_ref, group, at, in_reach):
    before = stat_ref[group, 0:1, at]
    largest = jnp.maximum(before, jnp.max(scores, axis=0, keepdims=True))
    prob = jnp.exp2((scores - jnp.where(in_reach, largest, -NEG_LARGE)) * EXP2_SCALE)
    largest = jnp.where(in_reach, largest, before)
    scale = jnp.exp2((before - largest) * EXP2_SCALE)
    total = stat_ref[group, 1:2, at] * scale + jnp.sum(prob, axis=0, keepdims=True)
    return prob, largest, total, scale


def staged(tiles, products, middle, finish):
    ahead = products(0)
    behind = None
    for tile in range(tiles):
        now = ahead
        if tile + 1 < tiles:
            ahead = products(tile + 1)
        done = middle(tile, *now)
        if behind is not None:
            finish(tile - 1, behind)
        behind = done
    finish(tiles - 1, behind)


def store_query_grad(dq_refs, group, tile, dq, half_ref):
    part, group = divmod(group, EARLY)
    dq_ref = dq_refs[part]
    half, quad = divmod(tile, 2)
    rows = dq_ref.shape[1] // 2
    cos_t, sin_t = half_ref[half, 0], half_ref[half, 1]
    upper, lower = dq[:HALF], dq[HALF:]
    dq = jnp.concatenate([upper * cos_t + lower * sin_t, lower * cos_t - upper * sin_t], axis=0).astype(BF16)
    dq = dq.T
    for i in range(QUAD):
        head = group * RATIO + quad * QUAD + i
        dq_ref[0, half * rows : (half + 1) * rows, head_columns(head)] = dq[i * rows : (i + 1) * rows]


def own_alone(dq_refs, scale_ref, ds0_ref, kt0_ref, stat_ref, half_ref, group, tiles):
    for tile in tiles:
        at = tile_columns(tile)
        scale = 1.0 / stat_ref[group, 1:2, at]
        scale_ref[group, 0:1, at] = scale
        dscore = ds0_ref[group, :, at] * scale.astype(BF16)
        store_query_grad(dq_refs, group, tile, dot_nn(kt0_ref[group], dscore), half_ref)


def key_products(qg_ref, group, tiles, dscore, prob):
    rows = dscore.shape[0]
    both = dot_nn(jnp.concatenate([dscore, prob], axis=0), group_rows(qg_ref, group, slice(2 * HD), tiles))
    return (both[:rows, :HD] * SCORE_SCALE).astype(BF16), both[rows:, HD:].astype(BF16)


def near_kernel(
    notes_ref, qg_ref, kv_ref, ds0_ref, kt0_ref, stat_ref, half_ref, cos_ref, sin_ref,
    dqa_ref, dqb_ref, ret2_ref, ret1_ref, scale_ref, prob_ref, ds_ref, kt_ref, next_ref,
):
    dq_refs = (dqa_ref, dqb_ref)
    rows = kv_ref.shape[2]

    def attend(last, tiles):
        in_reach = reached(notes_ref)
        bias = reach_bias(notes_ref, 1, rows)
        for group in range(HK):
            one_group(last, tiles, in_reach, bias, group)

    def one_group(last, tiles, in_reach, bias, group):
        k_rot = rotate(kv_ref[0, group].astype(F32), cos_ref[...], sin_ref[...])
        k_rot_t = k_rot.T.astype(BF16)
        left = block_diagonal(k_rot.astype(BF16), kv_ref[1, group])
        both_t = jnp.concatenate([k_rot_t, kt0_ref[group]], axis=1)

        def products(tile):
            both = dot_nt(left, qg_ref[group * TILES + tile])
            return both[:rows], both[rows:]

        def middle(tile, scores, dprob):
            at = tile_columns(tile)
            prob, largest, total, scale = softmax_step(scores + bias, stat_ref, group, at, in_reach[tile // 2])
            delta = stat_ref[group, 2:3, at]
            if last:
                inverse = 1.0 / total
                scale = scale * inverse
                scale_ref[group, 0:1, at] = scale
            prob = prob.astype(BF16)
            if last:
                prob = prob * inverse.astype(BF16)
            dscore = prob * (dprob - delta).astype(BF16)
            prob_ref[group, :, at] = prob
            ds_ref[group, :, at] = dscore
            if last:
                own_dscore = ds0_ref[group, :, at] * scale.astype(BF16)
                return jnp.concatenate([dscore, own_dscore], axis=0)
            next_ref[group, 0:1, at] = largest
            next_ref[group, 1:2, at] = total
            next_ref[group, 2:3, at] = delta
            next_ref[group, 3:4, at] = scale
            return None

        def finish(tile, dscore):
            if last:
                store_query_grad(dq_refs, group, tile, dot_nn(both_t, dscore), half_ref)

        staged(tiles, products, middle, finish)
        if last:
            own_alone(
                dq_refs, scale_ref, ds0_ref, kt0_ref, stat_ref, half_ref, group, range(tiles, TILES)
            )
            used = slice(0, tile_columns(tiles - 1).stop)
            grads = key_products(qg_ref, group, tiles, ds_ref[group, :, used], prob_ref[group, :, used])
            for which, grad in enumerate(grads):
                ret1_ref[which, group] = grad
                ret2_ref[which, group] = jnp.zeros((rows, HD), BF16)
        else:
            kt_ref[group] = k_rot_t
            for tile in range(tiles, TILES):
                next_ref[group, 1:2, tile_columns(tile)] = stat_ref[group, 1:2, tile_columns(tile)]

    further, wide = goes_on(notes_ref), high_reached(notes_ref)
    for last in (True, False):
        for tiles in (TILES // 2, TILES):
            chosen = (further != last) & (wide == (tiles == TILES))
            pl.when(chosen)(lambda last=last, tiles=tiles: attend(last, tiles))


def far_kernel(
    notes_ref, qg_ref, kv_ref, ds0_ref, kt0_ref, half_ref, cos_ref, sin_ref,
    prob1_ref, ds1_ref, kt1_ref, stat_ref, *refs,
):
    *dq_refs, ret2_ref, ret1_ref, scale_ref, prob_buf, ds_buf = refs[5:]
    rows = kv_ref.shape[2]

    def attend(skipped, tiles):
        in_reach = reached(notes_ref)
        bias = reach_bias(notes_ref, 2, rows)[skipped:]
        for group in range(HK):
            one_group(skipped, tiles, in_reach, bias, group)

    def one_group(skipped, tiles, in_reach, bias, group):
        used = rows - skipped
        k_rot = rotate(kv_ref[0, group, skipped:, :].astype(F32), cos_ref[skipped:, :], sin_ref[skipped:, :])
        left = block_diagonal(k_rot.astype(BF16), kv_ref[1, group, skipped:, :])
        k_rot_t = k_rot.T.astype(BF16)
        near_t = jnp.concatenate([kt1_ref[group], kt0_ref[group]], axis=1)

        def products(tile):
            both = dot_nt(left, qg_ref[group * TILES + tile])
            return both[:used], both[used:]

        def middle(tile, scores, dprob):
            at = tile_columns(tile)
            prob, _, total, scale = softmax_step(scores + bias, stat_ref, group, at, in_reach[tile // 2])
            inverse = 1.0 / total
            near_scale = scale * inverse
            own_scale = near_scale * stat_ref[group, 3:4, at]
            scale_ref[group, 0:1, at] = own_scale
            prob = prob.astype(BF16) * inverse.astype(BF16)
            dscore = prob * (dprob - stat_ref[group, 2:3, at]).astype(BF16)
            near_scale = near_scale.astype(BF16)
            near_dscore = ds1_ref[group, :, at] * near_scale
            own_dscore = ds0_ref[group, :, at] * own_scale.astype(BF16)
            prob_buf[:used, at] = prob
            prob_buf[used : used + rows, at] = prob1_ref[group, :, at] * near_scale
            ds_buf[:used, at] = dscore
            ds_buf[used : used + rows, at] = near_dscore
            return dscore, jnp.concatenate([near_dscore, own_dscore], axis=0)

        def finish(tile, dscores):
            dq = dot_nn(near_t, dscores[1]) + dot_nn(k_rot_t, dscores[0])
            store_query_grad(dq_refs, group, tile, dq, half_ref)

        staged(tiles, products, middle, finish)
        own_alone(
            dq_refs, scale_ref, ds0_ref, kt0_ref, stat_ref, half_ref, group, range(tiles, TILES)
        )
        columns = slice(0, tile_columns(tiles - 1).stop)
        grads = key_products(qg_ref, group, tiles, ds_buf[: used + rows, columns], prob_buf[: used + rows, columns])
        for which, grad in enumerate(grads):
            ret1_ref[which, group] = grad[used:]
            ret2_ref[which, group, skipped:, :] = grad[:used]
            if skipped:
                ret2_ref[which, group, :skipped, :] = jnp.zeros((skipped, HD), BF16)

    @pl.when(goes_on(notes_ref))
    def _():
        wide = high_reached(notes_ref)
        pl.when(wide)(lambda: attend(rows // 2, TILES))
        pl.when(jnp.logical_not(wide))(lambda: attend(0, TILES // 2))


def own_kv_kernel(qg_ref, prob_ref, ds_ref, scale_ref, dk_ref, dv_ref):
    @pl.loop(0, HK)
    def _(group):
        scale = scale_ref[group, 0:1, :]
        prob = (prob_ref[group].astype(F32) * scale).astype(BF16)
        dscore = (ds_ref[group].astype(F32) * scale).astype(BF16)
        dk_ref[group] = dot_nn(dscore, group_rows(qg_ref, group, slice(HD))) * SCORE_SCALE
        dv_ref[group] = dot_nn(prob, group_rows(qg_ref, group, slice(HD, 2 * HD)))


def hand_kernel(dq_ref, handed_hbm, copied):
    rows, width = dq_ref.shape[1:]
    copies = []
    for i in range(2):
        at = pl.ds(i * rows // 2, rows // 2)
        copies.append(pltpu.make_async_copy(dq_ref.at[:, at], handed_hbm.at[:, at, pl.ds(0, width)], copied.at[i]))
    for copy in copies:
        copy.start()
    for copy in copies:
        copy.wait()


def sum_kernel(
    dk_ref, dv_ref, ret2_ref, ret1_ref, late_ref, cos_ref, sin_ref, handed_in,
    key_hbm, value_hbm, handed_hbm, key_buf, value_buf, copied,
):
    del handed_in
    width = late_ref.shape[2]
    rest = pl.ds(handed_hbm.shape[2] - width, width)
    copies = [pltpu.make_async_copy(late_ref, handed_hbm.at[:, :, rest], copied.at[0])]
    copies[0].start()
    for group in range(HK):
        at = head_columns(group)
        dv = dv_ref[group] + ret1_ref[1, group].astype(F32) + ret2_ref[1, group].astype(F32)
        value_buf[0, :, at] = dv.astype(BF16)
    copies.append(pltpu.make_async_copy(value_buf, value_hbm, copied.at[1]))
    copies[-1].start()
    for group in range(HK):
        at = head_columns(group)
        dk = dk_ref[group] + ret1_ref[0, group].astype(F32) + ret2_ref[0, group].astype(F32)
        key_buf[0, :, at] = unrotate(dk, cos_ref[...], sin_ref[...]).astype(BF16)
    copies.append(pltpu.make_async_copy(key_buf, key_hbm, copied.at[2]))
    copies[-1].start()
    for copy in copies:
        copy.wait()


def cost(flops, moved, exps=0):
    return pl.CostEstimate(flops=int(flops), bytes_accessed=int(moved), transcendentals=int(exps))


def shards(query_heads, key_heads, value_heads, attn_output, output_grad, doc_start, fetch_list):
    rows = query_heads.shape[1]
    wide = RATIO * HD
    kv_width = HK * HD
    first_row = (lax.axis_index("ctx") * rows).astype(jnp.int32).reshape(1)
    doc_row = doc_start.reshape(1, rows)
    smem = pl.BlockSpec(memory_space=pltpu.SMEM)
    vmem = pl.BlockSpec(memory_space=pltpu.VMEM)
    hbm = pl.BlockSpec(memory_space=pltpu.HBM)
    anywhere = pl.BlockSpec(memory_space=pl.ANY)
    params = pltpu.CompilerParams(vmem_limit_bytes=40 * 1024 * 1024)
    shape = jax.ShapeDtypeStruct
    block_flops = 2 * HQ * rows * rows * HD
    arguments = [
        pltpu.with_memory_space_constraint(x[0], pltpu.HBM)
        for x in (query_heads, key_heads, value_heads, attn_output, output_grad)
    ]

    kv = pl.pallas_call(
        pack_kernel,
        in_specs=[hbm, hbm],
        out_specs=vmem,
        out_shape=shape((2, HK, rows, HD), BF16),
        scratch_shapes=[pltpu.SemaphoreType.DMA((2, HK))],
        compiler_params=params,
        cost_estimate=cost(0, 2**19),
        name="pack_keys",
    )(arguments[1], arguments[2])
    kv2 = from_behind(kv, "ctx", 2)
    kv1 = from_behind(kv, "ctx", 1)

    notes, qg, prob0, ds0, k_own_t, stat, half, cos, sin, cos1, sin1, cos2, sin2 = pl.pallas_call(
        own_kernel,
        in_specs=[smem, vmem, vmem] + [hbm] * 5,
        out_specs=[vmem] * 13,
        out_shape=[
            shape((8, QUAD * rows // 2), F32),
            shape((HK * TILES, QUAD * rows // 2, 2 * HD), BF16),
            shape((HK, rows, RATIO * rows), BF16),
            shape((HK, rows, RATIO * rows), BF16),
            shape((HK, HD, rows), BF16),
            shape((HK, 8, RATIO * rows), F32),
            shape((2, 2, HALF, QUAD * rows // 2), F32),
            shape((rows, HD), F32),
            shape((rows, HD), F32),
            shape((rows, HD), F32),
            shape((rows, HD), F32),
            shape((rows, HD), F32),
            shape((rows, HD), F32),
        ],
        scratch_shapes=[
            pltpu.VMEM((HK, rows, wide), BF16),
            pltpu.VMEM((HK, rows, HD), BF16),
            pltpu.VMEM((HK, rows, HD), BF16),
            pltpu.VMEM((HK, rows, wide), BF16),
            pltpu.VMEM((HK, rows, wide), BF16),
            pltpu.SemaphoreType.DMA((5, HK)),
        ],
        compiler_params=params,
        cost_estimate=cost(3 * block_flops, 9 * 2**20, HQ * rows * rows),
        name="own_block",
    )(first_row, *(pltpu.with_memory_space_constraint(x, pltpu.HBM) for x in (fetch_list, doc_row)), *arguments)

    results = [
        shape((1, rows, EARLY * RATIO * HD), BF16),
        shape((1, rows, (HK - EARLY) * RATIO * HD), BF16),
        shape((2, HK, rows, HD), BF16),
        shape((2, HK, rows, HD), BF16),
        shape((HK, 8, RATIO * rows), F32),
    ]
    *settled, prob1, ds1, k_near_t, stat1 = pl.pallas_call(
        near_kernel,
        in_specs=[vmem] * 9,
        out_specs=[vmem] * 9,
        out_shape=results
        + [
            shape((HK, rows, RATIO * rows), BF16),
            shape((HK, rows, RATIO * rows), BF16),
            shape((HK, HD, rows), BF16),
            shape((HK, 8, RATIO * rows), F32),
        ],
        compiler_params=params,
        cost_estimate=cost(5 * block_flops, 9 * 2**20, HQ * rows * rows),
        name="near_block",
    )(notes, qg, kv1, ds0, k_own_t, stat, half, cos1, sin1)

    dq_early, dq_late, ret2, ret1, scale = pl.pallas_call(
        far_kernel,
        in_specs=[vmem] * 17,
        out_specs=[vmem] * 5,
        out_shape=results,
        scratch_shapes=[
            pltpu.VMEM((FETCH * rows, RATIO * rows), BF16),
            pltpu.VMEM((FETCH * rows, RATIO * rows), BF16),
        ],
        input_output_aliases={12 + i: i for i in range(5)},
        compiler_params=params,
        cost_estimate=cost(5 * block_flops, 9 * 2**20, HQ * rows * rows),
        name="far_block",
    )(notes, qg, kv2, ds0, k_own_t, half, cos2, sin2, prob1, ds1, k_near_t, stat1, *settled)
    arrived1 = from_behind(ret1, "ctx", -1)
    arrived2 = from_behind(ret2, "ctx", -2)
    early = from_behind(dq_early, "section", -1)
    late = from_behind(dq_late, "section", -1)

    dk0, dv0 = pl.pallas_call(
        own_kv_kernel,
        in_specs=[vmem] * 4,
        out_specs=[vmem] * 2,
        out_shape=[shape((HK, rows, HD), F32), shape((HK, rows, HD), F32)],
        compiler_params=params,
        cost_estimate=cost(2 * block_flops, 5 * 2**20),
        name="own_keys",
    )(qg, prob0, ds0, scale)

    handed = pl.pallas_call(
        hand_kernel,
        in_specs=[anywhere],
        out_specs=hbm,
        out_shape=shape((1, rows, HQ * HD), BF16),
        scratch_shapes=[pltpu.SemaphoreType.DMA((2,))],
        compiler_params=params,
        cost_estimate=cost(0, 2 * 2**20),
        name="hand_on",
    )(early)

    key_grad, value_grad, handed_grad = pl.pallas_call(
        sum_kernel,
        in_specs=[vmem] * 4 + [anywhere] + [vmem] * 2 + [hbm],
        out_specs=[hbm] * 3,
        input_output_aliases={7: 2},
        out_shape=[
            shape((1, rows, kv_width), BF16),
            shape((1, rows, kv_width), BF16),
            shape((1, rows, HQ * HD), BF16),
        ],
        scratch_shapes=[
            pltpu.VMEM((1, rows, kv_width), BF16),
            pltpu.VMEM((1, rows, kv_width), BF16),
            pltpu.SemaphoreType.DMA((3,)),
        ],
        compiler_params=params,
        cost_estimate=cost(0, 3 * 2**20),
        name="sum_keys",
    )(dk0, dv0, arrived2, arrived1, late, cos, sin, handed)
    return (handed_grad, key_grad, value_grad)


def solution(mesh):
    return jax.shard_map(
        shards,
        mesh=mesh,
        in_specs=(
            P("section", "ctx", None),
            P("section", "ctx", None),
            P("section", "ctx", None),
            P("section", "ctx", None),
            P("section", "ctx", None),
            P("ctx"),
            P("ctx", None),
        ),
        out_specs=(P("section", "ctx", None), P("section", "ctx", None), P("section", "ctx", None)),
        check_vma=False,
    )
```
